32 devices in a mesh: dp: 8 (over y, x, core), mp: 4 (over z).
Axes of the slice: x: 2, y: 2, z: 4, core: 2. Of those that a mesh axis runs over, the one named last changes fastest.
Arguments:
- tokens: bfloat16 [3, 8192, 1024], P(None, ('dp', 'mp')), may hold values from -6 to 6
- segment_ids: int32 [3, 8192], P(None, 'dp'), may hold values from 0 to 63, never falling along the last dimension, each value on 1 to 1024 neighbouring positions
- row_lengths: int32 [3, 8], P(None, 'dp'), may hold values from 512 to 1024, as said below
- ln1_gain: float32 [1024], replicated, may hold values from 0.5 to 1.5
- ln1_bias: float32 [1024], replicated, may hold values from -4 to 4
- qkv_weight: bfloat16 [1024, 3072], P(None, 'mp'), may hold values from -0.1875 to 0.1875
- qkv_bias: float32 [3072], P('mp'), may hold values from -4 to 4
- out_weight: bfloat16 [1024, 1024], P('mp'), may hold values from -0.75 to 0.75
- out_bias: float32 [1024], replicated, may hold values from -4 to 4
- ln2_gain: float32 [1024], replicated, may hold values from 0.5 to 1.5
- ln2_bias: float32 [1024], replicated, may hold values from -4 to 4
- up_weight: bfloat16 [1024, 4096], P(None, 'mp'), may hold values from -0.1875 to 0.1875
- up_bias: float32 [4096], P('mp'), may hold values from -4 to 4
- down_weight: bfloat16 [4096, 1024], P('mp'), may hold values from -0.09375 to 0.09375
- down_bias: float32 [1024], replicated, may hold values from -4 to 4
- prefix_embed: bfloat16 [10, 1024], replicated, may hold values from -6 to 6
- reparam_in: bfloat16 [1024, 512], replicated, may hold values from -0.1875 to 0.1875
- reparam_in_bias: float32 [512], replicated, may hold values from -4 to 4
- reparam_out: bfloat16 [512, 2048], P(None, ('mp', 'dp')), may hold values from -0.25 to 0.25
- reparam_out_bias: float32 [2048], P(('mp', 'dp')), may hold values from -4 to 4
- cotangent: bfloat16 [3, 8192, 1024], P(None, ('dp', 'mp')), may hold values from -6 to 6
Outputs:
- block_out: bfloat16 [3, 8192, 1024], P(None, ('dp', 'mp'))
- input_grad: float32 [3, 8192, 1024], P(None, ('dp', 'mp'))
- ln1_gain_grad: float32 [1024], replicated
- ln1_bias_grad: float32 [1024], replicated
- qkv_weight_grad: float32 [1024, 3072], P(None, 'mp')
- qkv_bias_grad: float32 [3072], P('mp')
- out_weight_grad: float32 [1024, 1024], P('mp')
- out_bias_grad: float32 [1024], replicated
- ln2_gain_grad: float32 [1024], replicated
- ln2_bias_grad: float32 [1024], replicated
- up_weight_grad: float32 [1024, 4096], P(None, 'mp')
- up_bias_grad: float32 [4096], P('mp')
- down_weight_grad: float32 [4096, 1024], P('mp')
- down_bias_grad: float32 [1024], replicated
- prefix_embed_grad: float32 [10, 1024], replicated
- reparam_in_grad: float32 [1024, 512], replicated
- reparam_in_bias_grad: float32 [512], replicated
- reparam_out_grad: float32 [512, 2048], P(None, ('mp', 'dp'))
- reparam_out_bias_grad: float32 [2048], P(('mp', 'dp'))
The draws below stay inside these ranges and needn't reach their ends.
Inputs may be any that keep to these rules, and one draw needn't show every extreme that they name: `segment_ids`: within each micro-batch the numbers never fall along the tokens; each number covers 1 to 1024 consecutive tokens, and every number of the range occurs. `row_lengths`: the first packed row of every micro-batch is full and the last one is half full.
All inputs are finite; a program needn't handle non-finite values.
Results may differ from the reference program's by a relative error of at most 0.02.
Values may be sent and summed in bfloat16 or wider, within the bound.
A program may use at most 192 MiB of HBM per device.

```python
import math
import jax
import jax.numpy as jnp
import numpy as np
from jax import lax

D = 1024
HEADS = 16
FF = 4096
REPARAM = 512
PREFIX = 10
SEQ = 1024
MB = 3
HEAD_DIM = 64
TOKENS = 8192
N_DP = 8
N_MP = 4


def draw_row_lengths(key, part):
    key = jax.random.fold_in(key, 7)
    lengths = jax.random.randint(key, (MB, N_DP), SEQ // 2, SEQ + 1)
    column = jnp.arange(N_DP)[None, :]
    lengths = jnp.where(column == 0, SEQ, lengths)
    lengths = jnp.where(column == N_DP - 1, SEQ // 2, lengths)
    return lengths.astype(jnp.int32)


def level_of(stream_key, extent, cuts, least, top_value):
    level, own = 1.0, jax.random.fold_in(stream_key, 6)
    for dim, shards_of in cuts:
        draws = jnp.exp(jax.random.uniform(jax.random.fold_in(own, dim), (shards_of,), jnp.float32, least / len(cuts), top_value / len(cuts)))
        level = level * jnp.repeat(draws, extent[dim] // shards_of).reshape([-1 if axis == dim else 1 for axis in range(len(extent))])
    return level


def split_up(number_of, total, limit, lean):
    portions = [(1 << 20) // math.isqrt(standing ** lean) + 1 for standing in range(2, number_of + 1)]
    spare, holding = total - limit - (number_of - 1), [1] * (number_of - 1)
    while spare > 0:
        candidates = [i for i in range(number_of - 1) if holding[i] < limit]
        mass, left = sum([portions[i] for i in candidates]), spare
        for i in candidates:
            addition = min(limit - holding[i], max(1, left * portions[i] // mass), spare)
            holding[i] = holding[i] + addition
            spare = spare - addition
    return np.array([limit] + holding)


def uneven(stream_key, number_of, total, limit, skew):
    if number_of == 2:
        one = jax.random.randint(stream_key, (), max(1, total - limit), min(limit, total - 1) + 1)
        return jnp.stack([one, total - one])
    sizes = jnp.asarray(split_up(number_of, total, limit, skew), jnp.int32)
    couples = (number_of - 1) // 2
    source_of, receiver = sizes[1:1 + 2 * couples:2], sizes[2:2 + 2 * couples:2]
    slack = jnp.minimum(source_of - 1, limit - receiver)
    passed = jax.random.randint(jax.random.fold_in(stream_key, 1), (couples,), 0, 1 << 20) % (slack + 1)
    sizes = sizes.at[1:1 + 2 * couples:2].set(source_of - passed).at[2:2 + 2 * couples:2].set(receiver + passed)
    return sizes[jax.random.permutation(jax.random.fold_in(stream_key, 2), number_of)]


def noise(own_key, extent, spread, limit, cuts=(), held_as=jnp.bfloat16):
    entries = jax.random.normal(own_key, extent, jnp.float32) * spread
    if len(cuts) > 0:
        entries = level_of(own_key, extent, cuts, -0.22, 0.18) * entries
    return jnp.clip(entries, min=-limit, max=limit).astype(held_as)


def setup_inputs(seed: int = 0) -> dict:
    splits = jax.random.split(jax.random.key(seed), 22)
    tokens = noise(splits[0], (MB, TOKENS, D), 1.0, 6.0, ((1, 32),))
    segment_ids = jax.vmap(lambda own: jnp.searchsorted(jnp.cumsum(uneven(own, 8 * N_DP, TOKENS, SEQ, 2)), jnp.arange(TOKENS), side="right"))(jax.random.split(splits[1], MB)).reshape((MB, TOKENS)).astype(jnp.int32)
    row_lengths = draw_row_lengths(jax.random.fold_in(splits[21], 71), 0)
    ln1_gain = jnp.clip(1.0 + 0.1 * jax.random.normal(splits[3], (D,), jnp.float32), 0.5, 1.5)
    ln1_bias = noise(splits[4], (D,), 0.3, 4.0, (), jnp.float32)
    qkv_weight = noise(splits[5], (D, 3 * D), D ** -0.5, 0.1875, ((1, 4),))
    qkv_bias = noise(splits[6], (3 * D,), 0.3, 4.0, ((0, 4),), jnp.float32)
    out_weight = noise(splits[7], (D, D), (D // 16) ** -0.5, 0.75, ((0, 4),))
    out_bias = noise(splits[8], (D,), 0.3, 4.0, (), jnp.float32)
    ln2_gain = jnp.clip(1.0 + 0.1 * jax.random.normal(splits[9], (D,), jnp.float32), 0.5, 1.5)
    ln2_bias = noise(splits[10], (D,), 0.3, 4.0, (), jnp.float32)
    up_weight = noise(splits[11], (D, FF), D ** -0.5, 0.1875, ((1, 4),))
    up_bias = noise(splits[12], (FF,), 0.3, 4.0, ((0, 4),), jnp.float32)
    down_weight = noise(splits[13], (FF, D), FF ** -0.5, 0.09375, ((0, 4),))
    down_bias = noise(splits[14], (D,), 0.3, 4.0, (), jnp.float32)
    prefix_embed = noise(splits[15], (PREFIX, D), 1.0, 6.0)
    reparam_in = noise(splits[16], (D, REPARAM), D ** -0.5, 0.1875)
    reparam_in_bias = noise(splits[17], (REPARAM,), 0.3, 4.0, (), jnp.float32)
    reparam_out = noise(splits[18], (REPARAM, 2 * D), REPARAM ** -0.5, 0.25, ((1, 32),))
    reparam_out_bias = noise(splits[19], (2 * D,), 0.3, 4.0, ((0, 32),), jnp.float32)
    cotangent = noise(splits[20], (MB, TOKENS, D), 1.0, 6.0, ((1, 32),))
    return {"tokens": tokens, "segment_ids": segment_ids, "row_lengths": row_lengths, "ln1_gain": ln1_gain, "ln1_bias": ln1_bias, "qkv_weight": qkv_weight, "qkv_bias": qkv_bias, "out_weight": out_weight, "out_bias": out_bias, "ln2_gain": ln2_gain, "ln2_bias": ln2_bias, "up_weight": up_weight, "up_bias": up_bias, "down_weight": down_weight, "down_bias": down_bias, "prefix_embed": prefix_embed, "reparam_in": reparam_in, "reparam_in_bias": reparam_in_bias, "reparam_out": reparam_out, "reparam_out_bias": reparam_out_bias, "cotangent": cotangent}


@jax.custom_vjp
def low(v):
    return lax.optimization_barrier(v.astype(jnp.bfloat16)).astype(jnp.float32)

@jax.custom_vjp
def low_back(v):
    return v

def low_keep(v):
    return (low(v), None)

def low_pass(kept, grad):
    return (grad,)

def back_keep(v):
    return (v, None)

def back_low(kept, grad):
    return (low(grad),)
low.defvjp(low_keep, low_pass)
low_back.defvjp(back_keep, back_low)
EPSILON = 1e-05
MASKED = -1e+30
HIGHEST = lax.Precision.HIGHEST

def product(left, right):
    return jnp.dot(left, right, precision=HIGHEST)

def layer_norm(inputs, norm_gain, norm_offset):
    average = lax.optimization_barrier(jnp.mean(inputs, -1, keepdims=True))
    centered = inputs - average
    variance = lax.optimization_barrier(jnp.mean(centered * centered, -1, keepdims=True))
    return centered * lax.rsqrt(variance + EPSILON) * norm_gain + norm_offset

def attend(queries, keys_tok, values_tok, keys_pre, values_pre, visible):
    score_scale = 1.0 / math.sqrt(HEAD_DIM)
    raw_tok = jnp.einsum('hqd,hkd->hqk', queries, keys_tok, precision=HIGHEST) * score_scale
    raw_pre = jnp.einsum('hqd,hkd->hqk', queries, keys_pre, precision=HIGHEST) * score_scale
    scores = jnp.concatenate([low_back(raw_pre), jnp.where(visible[None], low_back(raw_tok), MASKED)], -1)
    attn_weights = low(jax.nn.softmax(scores, -1))
    values_all = jnp.concatenate([values_pre, values_tok], 1)
    return low(low_back(jnp.einsum('hqk,hkd->hqd', attn_weights, values_all, precision=HIGHEST)))

def row_forward(layer_weights, table, row_inputs):
    ln1_gain, ln1_bias, qkv_weight, qkv_bias, out_weight, out_bias, ln2_gain, ln2_bias, up_weight, up_bias, down_weight, down_bias = layer_weights
    row_tokens, row_segments, row_length = row_inputs
    positions = jnp.arange(SEQ)
    visible = (row_segments[:, None] == row_segments[None, :]) & (positions[None, :] <= positions[:, None]) & (positions[None, :] < row_length)
    heads_local = HEADS // N_MP
    width_head = heads_local * HEAD_DIM
    width_hidden = FF // N_MP
    normed_first = low(layer_norm(row_tokens, ln1_gain, ln1_bias))
    attention = jnp.zeros((SEQ, D), jnp.float32)
    for shard_number in range(N_MP):
        head_begin = shard_number * width_head
        raw = product(low_back(normed_first), qkv_weight[:, 3 * head_begin:3 * (head_begin + width_head)]) + qkv_bias[3 * head_begin:3 * (head_begin + width_head)]
        packed = low(low_back(raw)).reshape(SEQ, heads_local, 3, HEAD_DIM).transpose(2, 1, 0, 3)
        table_heads = table[:, 2 * head_begin:2 * (head_begin + width_head)].reshape(PREFIX, heads_local, 2, HEAD_DIM).transpose(2, 1, 0, 3)
        heads_out = attend(packed[0], packed[1], packed[2], table_heads[0], table_heads[1], visible)
        head_rows = heads_out.transpose(1, 0, 2).reshape(SEQ, width_head)
        attention = attention + low(product(head_rows, out_weight[head_begin:head_begin + width_head]))
    resid = row_tokens + low_back(attention) + out_bias
    normed_second = low(layer_norm(resid, ln2_gain, ln2_bias))
    feed = jnp.zeros((SEQ, D), jnp.float32)
    for shard_number in range(N_MP):
        unit_begin = shard_number * width_hidden
        up_act = low_back(product(low_back(normed_second), up_weight[:, unit_begin:unit_begin + width_hidden]) + up_bias[unit_begin:unit_begin + width_hidden])
        hidden = low(jax.nn.gelu(up_act, approximate=True))
        feed = feed + low(product(hidden, down_weight[unit_begin:unit_begin + width_hidden]))
    return resid + feed + down_bias

def reference(tokens, segment_ids, row_lengths, ln1_gain, ln1_bias, qkv_weight, qkv_bias, out_weight, out_bias, ln2_gain, ln2_bias, up_weight, up_bias, down_weight, down_bias, prefix_embed, reparam_in, reparam_in_bias, reparam_out, reparam_out_bias, cotangent):
    weights = (ln1_gain, ln1_bias, qkv_weight, qkv_bias, out_weight, out_bias, ln2_gain, ln2_bias, up_weight, up_bias, down_weight, down_bias, prefix_embed, reparam_in, reparam_in_bias, reparam_out, reparam_out_bias)
    weights = tuple((member.astype(jnp.float32) for member in weights))
    row_segments = segment_ids.reshape(MB * N_DP, SEQ)
    lengths_flat = row_lengths.reshape(MB * N_DP)

    def forward(weights, inputs):
        prefix_hidden = low(jnp.tanh(product(weights[12], weights[13]) + weights[14]))
        table = low(product(prefix_hidden, weights[15]) + weights[16])
        layer_weights = weights[:12]

        def one_row(row_inputs):
            return row_forward(layer_weights, table, row_inputs)
        outputs = lax.map(jax.checkpoint(one_row), (inputs.reshape(MB * N_DP, SEQ, D), row_segments, lengths_flat))
        return outputs.reshape(MB, TOKENS, D)
    primal, backward = jax.vjp(forward, weights, tokens.astype(jnp.float32))
    weight_grads, input_grad = backward(cotangent.astype(jnp.float32))
    return (primal.astype(jnp.bfloat16), input_grad, weight_grads[0], weight_grads[1], weight_grads[2], weight_grads[3], weight_grads[4], weight_grads[5], weight_grads[6], weight_grads[7], weight_grads[8], weight_grads[9], weight_grads[10], weight_grads[11], weight_grads[12], weight_grads[13], weight_grads[14], weight_grads[15], weight_grads[16])
```

```python
import functools
import math

import jax
import jax.numpy as jnp
from jax import lax
from jax.experimental import pallas as pl
from jax.experimental.pallas import tpu as pltpu
from jax.sharding import PartitionSpec as P

HEAD_DIM = 64


EPSILON = 1e-05
MASKED = -1e30
HIGHEST = lax.Precision.HIGHEST


def normalize(inputs):
    average = jnp.mean(inputs, -1, keepdims=True)
    centered = inputs - average
    variance = jnp.mean(centered * centered, -1, keepdims=True)
    inverse = lax.rsqrt(variance + EPSILON)
    return (centered * inverse, inverse)


def norm_back(grad_norm, normed_hat, inverse, norm_gain):
    scaled = grad_norm * norm_gain
    return inverse * (
        scaled
        - jnp.mean(scaled, -1, keepdims=True)
        - normed_hat * jnp.mean(scaled * normed_hat, -1, keepdims=True)
    )


def product_transposed(rows_in, matrix):
    return lax.dot_general(
        rows_in, matrix, (((1,), (1,)), ((), ())), preferred_element_type=jnp.float32
    )


def outer_sum(left, right):
    return lax.dot_general(
        left, right, (((0,), (0,)), ((), ())), preferred_element_type=jnp.float32
    )


def gelu_tanh(values_in):
    return jax.nn.gelu(values_in, approximate=True)


def attention_scores(queries, keys_tok, keys_pre, visible, log_total):
    score_scale = 1.0 / math.sqrt(queries.shape[-1])
    scores_tok = (
        jnp.einsum("hqd,hkd->hqk", queries, keys_tok, preferred_element_type=jnp.float32)
        * score_scale
    )
    scores_tok = jnp.where(visible[None], scores_tok, MASKED)
    scores_pre = (
        jnp.einsum("hqd,hkd->hqk", queries, keys_pre, preferred_element_type=jnp.float32)
        * score_scale
    )
    if log_total is None:
        highest = jnp.maximum(
            jnp.max(scores_tok, -1, keepdims=True), jnp.max(scores_pre, -1, keepdims=True)
        )
        totals = jnp.sum(jnp.exp(scores_tok - highest), -1, keepdims=True) + jnp.sum(
            jnp.exp(scores_pre - highest), -1, keepdims=True
        )
        log_total = highest + jnp.log(totals)
    return (jnp.exp(scores_tok - log_total), jnp.exp(scores_pre - log_total), log_total)


def per_device(
    tokens,
    segment_ids,
    row_lengths,
    ln1_gain,
    ln1_bias,
    qkv_weight,
    qkv_bias,
    out_weight,
    out_bias,
    ln2_gain,
    ln2_bias,
    up_weight,
    up_bias,
    down_weight,
    down_bias,
    prefix_embed,
    reparam_in,
    reparam_in_bias,
    reparam_out,
    reparam_out_bias,
    cotangent,
):
    width_head = out_weight.shape[0]
    heads_local = width_head // HEAD_DIM
    prefix_slots = prefix_embed.shape[0]
    pre_act = (
        jnp.dot(prefix_embed, reparam_in, preferred_element_type=jnp.float32) + reparam_in_bias
    )
    tanh_hidden = jnp.tanh(pre_act)
    tanh_low = tanh_hidden.astype(jnp.bfloat16)
    table_part = (
        jnp.dot(tanh_low, reparam_out, preferred_element_type=jnp.float32) + reparam_out_bias
    ).astype(jnp.bfloat16)

    def micro_step(carried, inputs):
        big_sums, small_sums, table_grad = carried
        tokens_mb, segments_mb, length_mb, cotangent_mb = inputs
        table_full = lax.all_gather(table_part, "dp", axis=1, tiled=True)
        seq_len = segments_mb.shape[0]
        table_heads = table_full.reshape(prefix_slots, heads_local, 2, HEAD_DIM).transpose(
            2, 1, 0, 3
        )
        positions = jnp.arange(seq_len)
        visible = (
            (segments_mb[:, None] == segments_mb[None, :])
            & (positions[None, :] <= positions[:, None])
            & (positions[None, :] < length_mb)
        )
        x_share = tokens_mb.astype(jnp.float32)
        hat_first, inverse_first = normalize(x_share)
        normed_first = lax.all_gather(
            (hat_first * ln1_gain + ln1_bias).astype(jnp.bfloat16), "mp", axis=0, tiled=True
        )
        qkv_low = (
            jnp.dot(normed_first, qkv_weight, preferred_element_type=jnp.float32) + qkv_bias
        ).astype(jnp.bfloat16)
        packed = qkv_low.reshape(seq_len, heads_local, 3, HEAD_DIM).transpose(2, 1, 0, 3)
        weights_tok, weights_pre, log_total = attention_scores(
            packed[0], packed[1], table_heads[0], visible, None
        )
        heads_out = (
            jnp.einsum(
                "hqk,hkd->hqd",
                weights_tok.astype(jnp.bfloat16),
                packed[2],
                preferred_element_type=jnp.float32,
            )
            + jnp.einsum(
                "hqk,hkd->hqd",
                weights_pre.astype(jnp.bfloat16),
                table_heads[1],
                preferred_element_type=jnp.float32,
            )
        ).astype(jnp.bfloat16)
        head_rows = heads_out.transpose(1, 0, 2).reshape(seq_len, width_head)
        resid = (
            x_share
            + lax.psum_scatter(
                jnp.dot(head_rows, out_weight, preferred_element_type=jnp.float32).astype(
                    jnp.bfloat16
                ),
                "mp",
                scatter_dimension=0,
                tiled=True,
            ).astype(jnp.float32)
            + out_bias
        )
        hat_second, inverse_second = normalize(resid)
        normed_second = lax.all_gather(
            (hat_second * ln2_gain + ln2_bias).astype(jnp.bfloat16), "mp", axis=0, tiled=True
        )
        up_act = jnp.dot(normed_second, up_weight, preferred_element_type=jnp.float32) + up_bias
        gelu_out, gelu_back = jax.vjp(gelu_tanh, up_act)
        hidden_low = gelu_out.astype(jnp.bfloat16)
        block_share = (
            resid
            + lax.psum_scatter(
                jnp.dot(hidden_low, down_weight, preferred_element_type=jnp.float32).astype(
                    jnp.bfloat16
                ),
                "mp",
                scatter_dimension=0,
                tiled=True,
            ).astype(jnp.float32)
            + down_bias
        ).astype(jnp.bfloat16)
        cot_full = lax.all_gather(cotangent_mb, "mp", axis=0, tiled=True)
        d_up = gelu_back(product_transposed(cot_full, down_weight))[0].astype(jnp.bfloat16)
        grad_down = outer_sum(hidden_low, cot_full)
        grad_up = outer_sum(normed_second, d_up)
        grad_up_bias = jnp.sum(d_up.astype(jnp.float32), 0)
        d_second = lax.psum_scatter(
            product_transposed(d_up, up_weight).astype(jnp.bfloat16),
            "mp",
            scatter_dimension=0,
            tiled=True,
        ).astype(jnp.float32)
        cot_share = cotangent_mb.astype(jnp.float32)
        d_resid = cot_share + norm_back(d_second, hat_second, inverse_second, ln2_gain)
        d_attn = lax.all_gather(d_resid.astype(jnp.bfloat16), "mp", axis=0, tiled=True)
        grad_out = outer_sum(head_rows, d_attn)
        d_heads = (
            product_transposed(d_attn, out_weight)
            .astype(jnp.bfloat16)
            .reshape(seq_len, heads_local, HEAD_DIM)
            .transpose(1, 0, 2)
        )
        weights_tok, weights_pre, unused_total = attention_scores(
            packed[0], packed[1], table_heads[0], visible, log_total
        )
        score_scale = 1.0 / math.sqrt(HEAD_DIM)
        d_vtok = jnp.einsum(
            "hqk,hqd->hkd",
            weights_tok.astype(jnp.bfloat16),
            d_heads,
            preferred_element_type=jnp.float32,
        )
        d_vpre = jnp.einsum(
            "hqk,hqd->hkd",
            weights_pre.astype(jnp.bfloat16),
            d_heads,
            preferred_element_type=jnp.float32,
        )
        dprob_tok = jnp.einsum(
            "hqd,hkd->hqk", d_heads, packed[2], preferred_element_type=jnp.float32
        )
        dprob_pre = jnp.einsum(
            "hqd,hkd->hqk", d_heads, table_heads[1], preferred_element_type=jnp.float32
        )
        delta = jnp.sum(weights_tok * dprob_tok, -1, keepdims=True) + jnp.sum(
            weights_pre * dprob_pre, -1, keepdims=True
        )
        dscore_tok = (weights_tok * (dprob_tok - delta)).astype(jnp.bfloat16)
        dscore_pre = (weights_pre * (dprob_pre - delta)).astype(jnp.bfloat16)
        d_queries = (
            jnp.einsum("hqk,hkd->hqd", dscore_tok, packed[1], preferred_element_type=jnp.float32)
            + jnp.einsum(
                "hqk,hkd->hqd", dscore_pre, table_heads[0], preferred_element_type=jnp.float32
            )
        ) * score_scale
        d_ktok = (
            jnp.einsum("hqk,hqd->hkd", dscore_tok, packed[0], preferred_element_type=jnp.float32)
            * score_scale
        )
        d_kpre = (
            jnp.einsum("hqk,hqd->hkd", dscore_pre, packed[0], preferred_element_type=jnp.float32)
            * score_scale
        )
        prefix_add = (
            jnp.stack([d_kpre, d_vpre], 0)
            .transpose(2, 1, 0, 3)
            .reshape(prefix_slots, 2 * width_head)
        )
        d_qkv = (
            jnp.stack([d_queries, d_ktok, d_vtok], 0)
            .transpose(2, 1, 0, 3)
            .reshape(seq_len, 3 * width_head)
            .astype(jnp.bfloat16)
        )
        grad_qkv = outer_sum(normed_first, d_qkv)
        grad_qkv_bias = jnp.sum(d_qkv.astype(jnp.float32), 0)
        d_first = lax.psum_scatter(
            product_transposed(d_qkv, qkv_weight).astype(jnp.bfloat16),
            "mp",
            scatter_dimension=0,
            tiled=True,
        ).astype(jnp.float32)
        input_grad = d_resid + norm_back(d_first, hat_first, inverse_first, ln1_gain)
        small_add = (
            jnp.sum(d_first * hat_first, 0),
            jnp.sum(d_first, 0),
            jnp.sum(d_second * hat_second, 0),
            jnp.sum(d_second, 0),
            jnp.sum(d_resid, 0),
            jnp.sum(cot_share, 0),
        )
        big_add = (
            lax.psum(grad_qkv.astype(jnp.bfloat16), "dp").astype(jnp.float32),
            lax.psum(grad_qkv_bias.astype(jnp.bfloat16), "dp").astype(jnp.float32),
            lax.psum(grad_out.astype(jnp.bfloat16), "dp").astype(jnp.float32),
            lax.psum(grad_up.astype(jnp.bfloat16), "dp").astype(jnp.float32),
            lax.psum(grad_up_bias.astype(jnp.bfloat16), "dp").astype(jnp.float32),
            lax.psum(grad_down.astype(jnp.bfloat16), "dp").astype(jnp.float32),
        )
        big_sums = jax.tree.map(jnp.add, big_sums, tuple(big_add))
        small_sums = jax.tree.map(jnp.add, small_sums, small_add)
        return ((big_sums, small_sums, table_grad + prefix_add), (block_share, input_grad))

    big_zero = tuple(
        (
            jnp.zeros(member.shape, jnp.float32)
            for member in (qkv_weight, qkv_bias, out_weight, up_weight, up_bias, down_weight)
        )
    )
    small_zero = tuple((jnp.zeros(ln1_gain.shape, jnp.float32) for member in range(6)))
    table_zero = jnp.zeros((prefix_slots, 2 * width_head), jnp.float32)
    carried, stacked = lax.scan(
        micro_step,
        (big_zero, small_zero, table_zero),
        (tokens, segment_ids, row_lengths[:, 0], cotangent),
    )
    big_sums, small_sums, table_grad = carried
    block_out, input_grad = stacked
    table_own = lax.psum_scatter(table_grad, "dp", scatter_dimension=1, tiled=True)
    grad_rout = jnp.dot(tanh_low.astype(jnp.float32).T, table_own, precision=HIGHEST)
    grad_rout_bias = jnp.sum(table_own, 0)
    tanh_part = jnp.dot(table_own, reparam_out.astype(jnp.float32).T, precision=HIGHEST)
    shared = lax.psum(
        (
            tanh_part,
            small_sums[0],
            small_sums[1],
            small_sums[2],
            small_sums[3],
            small_sums[4],
            small_sums[5],
        ),
        ("dp", "mp"),
    )
    d_pre = shared[0] * (1.0 - tanh_hidden * tanh_hidden)
    grad_rin = jnp.dot(prefix_embed.astype(jnp.float32).T, d_pre, precision=HIGHEST)
    grad_rin_bias = jnp.sum(d_pre, 0)
    grad_embed = jnp.dot(d_pre, reparam_in.astype(jnp.float32).T, precision=HIGHEST)
    return (
        block_out,
        input_grad,
        shared[1],
        shared[2],
        big_sums[0],
        big_sums[1],
        big_sums[2],
        shared[5],
        shared[3],
        shared[4],
        big_sums[3],
        big_sums[4],
        big_sums[5],
        shared[6],
        grad_embed,
        grad_rin,
        grad_rin_bias,
        grad_rout,
        grad_rout_bias,
    )


ALL = ("pl", "core", "mp")
QB = 256
MICRO = 3


def nt(left, right):
    return lax.dot_general(
        left, right, (((1,), (1,)), ((), ())), preferred_element_type=jnp.float32
    )


def nn(left, right):
    return jnp.dot(left, right, preferred_element_type=jnp.float32)


def half_mask(value, head):
    lane = lax.broadcasted_iota(jnp.int32, value.shape, 1)
    keep = (lane < HEAD_DIM) if head == 0 else (lane >= HEAD_DIM)
    return jnp.where(keep, value, jnp.zeros_like(value))


GELU_A = math.sqrt(2.0 / math.pi)
GELU_B = 0.044715


def feed_kernel(
    heads_ref, tokens_ref, cot_ref, out_own_ref, out_ref, vectors_ref,
    own_up_ref, own_down_ref, weight_ref, bias_ref,
    block_ref, resid_ref, dheads_ref, gout_ref, sums_ref, grad_ref, gbias_ref,
    heads_s, normed_s, resid_s, mlp_s, dn_s,
):
    step = pl.program_id(0)
    blocks, near, cores, share, lanes = heads_ref.shape
    own_rows = out_own_ref.shape[0]
    out_bias, gain, offset, down_bias = [vectors_ref[j : j + 1] for j in range(4)]

    @pl.when(step == 0)
    def _before():
        for m in range(blocks):
            rows = slice(m * share, (m + 1) * share)
            heads = jnp.concatenate(
                [heads_ref[m, r, c] for r in range(near) for c in range(cores)], 1
            )
            heads_s[rows] = heads
            resid = (
                tokens_ref[rows].astype(jnp.float32)
                + nn(heads[:, :own_rows], out_own_ref[...])
                + nn(heads[:, own_rows:], out_ref[...])
                + out_bias
            )
            resid_s[rows] = resid
            hat, _ = normalize(resid)
            normed_s[rows] = (hat * gain + offset).astype(jnp.bfloat16)

    normed, cot = normed_s[...], cot_ref[...]
    groups, depth, width = grad_ref.shape[1:]
    half_rows = depth // 2
    units = (groups - 1) * half_rows
    up = jnp.concatenate(
        [jnp.transpose(own_up_ref[...]), weight_ref[0, :, :half_rows].reshape(units, width)], 0
    )
    down = jnp.concatenate(
        [own_down_ref[0], weight_ref[0, :, half_rows:].reshape(units, width)], 0
    )
    act = nt(normed, up) + bias_ref[0]
    square = act * act
    curve = jnp.tanh(GELU_A * act * (1.0 + GELU_B * square))
    half = 0.5 * (1.0 + curve)
    hidden = (act * half).astype(jnp.bfloat16)
    slope = half + 0.5 * act * (1.0 - curve * curve) * (
        GELU_A * (1.0 + (3.0 * GELU_B) * square)
    )
    d_act = nt(cot, down) * slope
    gbias_ref[0] = jnp.sum(d_act, 0, keepdims=True)
    d_low = d_act.astype(jnp.bfloat16)
    gup = outer_sum(d_low, normed).astype(jnp.bfloat16)
    gdown = outer_sum(hidden, cot).astype(jnp.bfloat16)
    grad_ref[0, :, :half_rows] = gup.reshape(groups, half_rows, width)
    grad_ref[0, :, half_rows:] = gdown.reshape(groups, half_rows, width)
    mlp, dn = nn(hidden, down), nn(d_low, up)

    @pl.when(step == 0)
    def _first():
        mlp_s[...] = mlp
        dn_s[...] = dn

    @pl.when(step > 0)
    def _later():
        mlp_s[...] += mlp
        dn_s[...] += dn

    @pl.when(step == pl.num_programs(0) - 1)
    def _after():
        sums = [jnp.zeros((1, width), jnp.float32) for _ in range(4)]
        for m in range(blocks):
            rows = slice(m * share, (m + 1) * share)
            resid, d_second = resid_s[rows], dn_s[rows]
            block_ref[rows] = (resid + mlp_s[rows] + down_bias).astype(jnp.bfloat16)
            hat, inverse = normalize(resid)
            cot_wide = cot_ref[rows].astype(jnp.float32)
            d_resid = cot_wide + norm_back(d_second, hat, inverse, gain)
            resid_ref[rows] = d_resid
            for j, value in enumerate((d_second * hat, d_second, d_resid, cot_wide)):
                sums[j] = sums[j] + jnp.sum(value, 0, keepdims=True)
            d_attn = d_resid.astype(jnp.bfloat16)
            normed_s[rows] = d_attn
            d_own = nt(d_attn, out_own_ref[...]).astype(jnp.bfloat16)
            d_rest = nt(d_attn, out_ref[...]).astype(jnp.bfloat16)
            for r in range(near):
                for c in range(cores):
                    source = d_rest if r else d_own
                    at = (2 * r + c) * lanes - (own_rows if r else 0)
                    dheads_ref[m, r, c] = source[:, at : at + lanes]
        for j in range(4):
            sums_ref[j : j + 1] = sums[j]
        for j in range(near):
            columns = slice(j * own_rows, (j + 1) * own_rows)
            gout_ref[columns] = outer_sum(heads_s[:, columns], normed_s[...]).astype(jnp.bfloat16)


def feed_forward(heads, tokens, cot, out_own, out, vectors, own_up, own_down, weights, bias):
    rows, width = tokens.shape
    tiles, others, depth, _ = weights.shape
    groups = others + 1
    units = groups * depth // 2
    once = pl.Buffered(1)

    def whole(shape):
        return pl.BlockSpec(shape, lambda i: (0,) * len(shape), pipeline_mode=once)

    shaped, bf16, f32 = jax.ShapeDtypeStruct, jnp.bfloat16, jnp.float32
    line = pl.BlockSpec((1, 1, units), lambda i: (i, 0, 0))
    square = (rows, width)
    return pl.pallas_call(
        feed_kernel,
        grid=(tiles,),
        in_specs=[
            whole(heads.shape),
            whole(square),
            whole(square),
            whole(out_own.shape),
            whole(out.shape),
            whole(vectors.shape),
            pl.BlockSpec((width, depth // 2), lambda i: (0, i)),
            pl.BlockSpec((1, depth // 2, width), lambda i: (i, 0, 0)),
            pl.BlockSpec((1, others, depth, width), lambda i: (i, 0, 0, 0)),
            line,
        ],
        out_specs=[
            whole(square),
            whole(square),
            whole(heads.shape),
            whole((width, width)),
            whole((4, width)),
            pl.BlockSpec((1, groups, depth, width), lambda i: (i, 0, 0, 0)),
            line,
        ],
        out_shape=[
            shaped(square, bf16),
            shaped(square, f32),
            shaped(heads.shape, bf16),
            shaped((width, width), bf16),
            shaped((4, width), f32),
            shaped((tiles, groups, depth, width), bf16),
            shaped((tiles, 1, units), f32),
        ],
        scratch_shapes=[
            pltpu.VMEM(square, bf16),
            pltpu.VMEM(square, bf16),
            pltpu.VMEM(square, f32),
            pltpu.VMEM(square, f32),
            pltpu.VMEM(square, f32),
        ],
        compiler_params=pltpu.CompilerParams(vmem_limit_bytes=62 << 20),
        cost_estimate=pl.CostEstimate(
            flops=12 * rows * width * tiles * units, bytes_accessed=60_000_000,
            transcendentals=rows * tiles * units,
        ),
        name="feed_forward",
    )(heads, tokens, cot, out_own, out, vectors, own_up, own_down, weights, bias)


MESH_IDS = pl.DeviceIdType.MESH


def position():
    return lax.axis_index("pl"), lax.axis_index("core"), lax.axis_index("mp")


def plane_at(plane, offset):
    across, down = lax.rem(plane, 2), lax.div(plane, 2)
    if offset & 1:
        across = 1 - across
    if offset & 2:
        down = 1 - down
    return 2 * down + across


def greet(partners):
    barrier = pltpu.get_barrier_semaphore()
    for partner in partners:
        pl.semaphore_signal(barrier, inc=1, device_id=partner, device_id_type=MESH_IDS)
    pl.semaphore_wait(barrier, len(partners))


def column_partners():
    plane, core, zed = position()
    found = [(plane, core, lax.rem(zed + step, 4)) for step in range(1, 4)]
    return found + [(plane, 1 - core, lax.rem(zed + step, 4)) for step in range(4)]


def plane_partners():
    plane, core, zed = position()
    return [(plane_at(plane, offset), core, zed) for offset in range(1, 4)]


class Wires:
    def __init__(self, sends, recvs):
        self.sends, self.recvs, self.out = sends, recvs, []

    def copy(self, source, target, slot, device):
        return pltpu.make_async_remote_copy(
            src_ref=source,
            dst_ref=target,
            send_sem=self.sends.at[slot],
            recv_sem=self.recvs.at[slot],
            device_id=device,
            device_id_type=MESH_IDS,
        )

    def put(self, source, target, slot, device):
        copy = self.copy(source, target, slot, device)
        copy.start()
        self.out.append((copy, None))

    def put_unless(self, own, source, target, slot, device):
        copy = self.copy(source, target, slot, device)

        @pl.when(own)
        def _here():
            pltpu.make_async_copy(source, target, self.recvs.at[slot]).start()

        @pl.when(jnp.logical_not(own))
        def _there():
            copy.start()

        self.out.append((copy, own))

    def put_if(self, valid, source, target, slot, device):
        copy = self.copy(source, target, slot, device)
        pl.when(valid)(copy.start)
        self.out.append((copy, jnp.logical_not(valid)))

    def got(self, target, slot, device):
        self.copy(target, target, slot, device).wait_recv()

    def got_if(self, valid, target, slot, device):
        pl.when(valid)(self.copy(target, target, slot, device).wait_recv)

    def wait_sent(self, puts):
        gone = [id(put) for put in puts]
        self.out = [put for put in self.out if id(put) not in gone]
        for copy, own in puts:
            if own is None:
                copy.wait_send()
            else:
                pl.when(jnp.logical_not(own))(copy.wait_send)

    def finish(self):
        self.wait_sent(list(self.out))


ANYWHERE = pl.BlockSpec(memory_space=pl.ANY)


def visible_to(seg_col, seg_row, block):
    keys = (block + 1) * QB
    lanes = seg_row[:, block * QB : keys]
    cols = seg_col[:keys, :]
    same = jnp.concatenate([cols, cols], 1) == lanes
    rows = lax.broadcasted_iota(jnp.int32, (keys, QB), 0)
    places = lax.broadcasted_iota(jnp.int32, (keys, QB), 1) + block * QB
    return same & (rows <= places)


def forward_pair(slots, qkv, keys_pre, values_pre, seg_row, seg_col, heads, logs):
    seq = qkv.shape[0]
    keys = qkv[:, 128:256]
    values_t = jnp.transpose(qkv[:, 256:384])
    values_pre_t = jnp.transpose(values_pre)
    pre_row = lax.broadcasted_iota(jnp.int32, (keys_pre.shape[0], QB), 0)
    for block in range(seq // QB):
        extent = (block + 1) * QB
        here = slice(block * QB, extent)
        visible = visible_to(seg_col, seg_row, block)
        queries = qkv[here, :128] * 0.125
        parts = []
        for head in range(2):
            rows = slice(head * HEAD_DIM, (head + 1) * HEAD_DIM)
            query = half_mask(queries, head)
            s_tok = jnp.where(visible, nt(keys[:extent], query), MASKED)
            s_pre = jnp.where(pre_row < slots, nt(keys_pre, query), MASKED)
            top = jnp.maximum(
                jnp.max(s_tok, 0, keepdims=True), jnp.max(s_pre, 0, keepdims=True)
            )
            p_tok, p_pre = jnp.exp(s_tok - top), jnp.exp(s_pre - top)
            total = jnp.sum(p_tok, 0, keepdims=True) + jnp.sum(p_pre, 0, keepdims=True)
            mixed = nn(values_t[rows, :extent], p_tok.astype(jnp.bfloat16)) + nn(
                values_pre_t[rows], p_pre.astype(jnp.bfloat16)
            )
            parts.append(mixed * (1.0 / total))
            logs[head : head + 1, here] = top + jnp.log(total)
        heads[here, :] = jnp.transpose(jnp.concatenate(parts, 0)).astype(jnp.bfloat16)


PAIRS = 6


def front_kernel(
    slots,
    normed_ref, qkv_ref, bias_ref, table_ref, ids_ref, own_ref,
    rows_out, weight_out, qkv_out, heads_out, feed_out, proj_out,
    log_out, tab_out, seg_out, live_out, bias_out,
    sends, recvs, local,
    rows_v, weight_v, qkv_v, heads_v, log_v, biases_v, tables_v, ids_v, other_v, col_v, feed_v,
):
    plane, core, zed = position()
    parity = lax.rem(zed, 2)
    mine = 2 * parity + core
    origin = lax.div(zed, 2)
    sibling = (plane, 1 - core, zed)
    share = normed_ref.shape[1]
    seq = 4 * share
    around = [(plane_at(plane, offset), core, zed) for offset in range(4)]
    ahead = [lax.rem(zed + step, 4) for step in range(4)]
    greet(column_partners() + plane_partners())
    wires = Wires(sends, recvs)
    slot_at = {}

    def slot(*name):
        return slot_at.setdefault(name, len(slot_at))

    width = qkv_ref.shape[0] // 4

    def strip(at):
        return pl.ds(pl.multiple_of(at * width, 32), width)

    def rolled(z_from, z_at):
        return lax.rem(z_from + 2 * lax.rem(z_at, 2), 4)

    def apart(z_of, z_at):
        return lax.rem(z_of - z_at + 4, 4)

    own_copies = [
        pltpu.make_async_copy(qkv_ref, weight_v.at[rolled(zed, zed)], local.at[0]),
        pltpu.make_async_copy(bias_ref, biases_v.at[zed], local.at[1]),
        pltpu.make_async_copy(table_ref, tables_v.at[plane, core, zed], local.at[2]),
        pltpu.make_async_copy(ids_ref, ids_v, local.at[3]),
    ]
    for copy in own_copies:
        copy.start()
    wires.put(ids_ref, other_v, slot("ids"), sibling)

    sides = (1, -1)
    hops = [(sign, hop) for hop in range(1, 4) for sign in sides]

    def owner(sign, hop):
        at = zed - sign * hop
        return lax.rem(at + 4, 4), jnp.logical_and(at >= 0, at <= 3)

    def next_along(sign):
        at = zed + sign
        return lax.rem(at + 4, 4), jnp.logical_and(at >= 0, at <= 3)

    def early_parts(z_of, z_at):
        return (
            weight_v.at[rolled(z_of, z_at), strip(plane)],
            biases_v.at[z_of],
            tables_v.at[plane, core, z_of],
        )

    def late_part(at, core_at, z_of, z_at):
        return feed_v.at[at, core_at, apart(z_of, z_at) - 1]

    total = own_ref.shape[0]
    part_rows = feed_out.shape[3] // 2
    halves = (pl.ds(0, total // 2), pl.ds(total // 2, total // 2))
    routes = ((1, 2), (2, 1))

    def half_strip(at, half):
        return pl.ds(pl.multiple_of(at * width + half * (width // 2), 16), width // 2)

    def send_early(sign, hop):
        z_of, there_is = owner(sign, hop - 1)
        z_to, can = next_along(sign)
        valid = jnp.logical_and(there_is, can)
        sources, targets = early_parts(z_of, zed), early_parts(z_of, z_to)
        for kind in range(3):
            wires.put_if(
                valid, sources[kind], targets[kind], slot("e", sign, hop, kind), (plane, core, z_to)
            )

    def send_late(sign, hop):
        z_of, there_is = owner(sign, hop - 1)
        z_to, can = next_along(sign)
        valid = jnp.logical_and(there_is, can)
        source = own_ref if hop == 1 else late_part(plane, core, z_of, zed)
        wires.put_if(
            valid, source, late_part(plane, core, z_of, z_to), slot("l", sign, hop), (plane, core, z_to)
        )

    def take_early(sign, hop):
        z_of, valid = owner(sign, hop)
        back = (plane, core, lax.rem(zed + 4 - sign, 4))
        for kind, part in enumerate(early_parts(z_of, zed)):
            wires.got_if(valid, part, slot("e", sign, hop, kind), back)
        if hop < 3:
            send_early(sign, hop + 1)
        for half in range(2):
            part = weight_v.at[rolled(z_of, zed), half_strip(plane, half)]
            for offset in routes[half]:
                wires.put_if(valid, part, part, slot("ep", sign, hop, half, offset), around[offset])

    def early_across(sign, hop):
        z_of, valid = owner(sign, hop)
        for half, (came, goes) in enumerate(routes):
            part = weight_v.at[rolled(z_of, zed), half_strip(plane_at(plane, came), half)]
            wires.got_if(valid, part, slot("ep", sign, hop, half, came), around[came])
            wires.put_if(valid, part, part, slot("ep", sign, hop, half, 3), around[goes])

    def early_end(sign, hop):
        z_of, valid = owner(sign, hop)
        for half, (came, goes) in enumerate(routes):
            for offset, over in ((goes, goes), (3, goes)):
                part = weight_v.at[rolled(z_of, zed), half_strip(plane_at(plane, offset), half)]
                wires.got_if(valid, part, slot("ep", sign, hop, half, offset), around[over])

    def take_late(sign, hop):
        z_of, valid = owner(sign, hop)
        part = late_part(plane, core, z_of, zed)
        wires.got_if(valid, part, slot("l", sign, hop), (plane, core, lax.rem(zed + 4 - sign, 4)))
        if hop < 3:
            send_late(sign, hop + 1)
        for half in range(2):
            piece = part.at[halves[half]]
            for offset in routes[half]:
                wires.put_if(
                    valid, piece, piece, slot("lp", sign, hop, half, offset), around[offset]
                )
        wires.put_if(valid, part, part, slot("ls", sign, hop, 0), sibling)

    def take_across(sign, hop):
        z_of, valid = owner(sign, hop)
        for half, (came, goes) in enumerate(routes):
            piece = late_part(plane_at(plane, came), core, z_of, zed).at[halves[half]]
            wires.got_if(valid, piece, slot("lp", sign, hop, half, came), around[came])
            wires.put_if(valid, piece, piece, slot("lp", sign, hop, half, 3), around[goes])
        for half, (_, other) in enumerate(routes):
            piece = late_part(plane_at(plane, other), core, z_of, zed).at[halves[half]]
            wires.got_if(valid, piece, slot("lp", sign, hop, half, other), around[other])
        for offset in (1, 2):
            part = late_part(plane_at(plane, offset), core, z_of, zed)
            wires.put_if(valid, part, part, slot("ls", sign, hop, offset), sibling)

    def take_far(sign, hop):
        z_of, valid = owner(sign, hop)
        part = late_part(plane_at(plane, 3), core, z_of, zed)
        for half, (_, goes) in enumerate(routes):
            wires.got_if(
                valid, part.at[halves[half]], slot("lp", sign, hop, half, 3), around[goes]
            )
        wires.put_if(valid, part, part, slot("ls", sign, hop, 3), sibling)

    def end_across(sign, hop):
        z_of, valid = owner(sign, hop)
        for offset in range(4):
            part = late_part(plane_at(plane, offset), 1 - core, z_of, zed)
            wires.got_if(valid, part, slot("ls", sign, hop, offset), sibling)

    for copy in own_copies:
        copy.wait()
    for sign in sides:
        send_early(sign, 1)
    first_far = slot("nb", 0)
    slot("nb", 1)
    first_row = slot("n", 0)
    for step in range(1, 4):
        slot("n", step)
    outside = lax.div(zed, 2) != core
    near_home = jnp.logical_or(zed == 1, zed == 2)
    far_z = zed + 1 - 2 * parity
    first_over = slot("f", 0)
    for step in range(1, 4):
        slot("f", step)

    def send_rows(kind):
        for half in range(2):
            k = 2 * half + kind
            z_to = 2 * core + half
            own = jnp.logical_and(core == kind, z_to == zed)
            source, target = normed_ref.at[1 if kind else k], rows_v.at[kind, zed]
            number = first_row + lax.rem(k + 4 - zed, 4)

            @pl.when(own)
            def _here():
                pltpu.make_async_copy(source, target, recvs.at[number]).start()

            goes = jnp.logical_not(own)
            if kind:
                far_to = jnp.logical_or(z_to == 0, z_to == 3)
                goes = jnp.logical_and(goes, jnp.logical_not(jnp.logical_and(outside, far_to)))
            wires.put_if(goes, source, target, number, (plane, kind, z_to))

    def pass_rows(kind):
        here = core == kind
        for step in range(4):
            z_from = lax.rem(2 * parity + kind + 4 - step, 4)
            block = rows_v.at[kind, z_from]
            if kind:
                from_outside = jnp.logical_and(here, lax.div(z_from, 2) != origin)
                via = jnp.logical_and(from_outside, jnp.logical_not(near_home))
                far_number = first_far + lax.rem(z_from, 2)
                wires.got_if(via, block, far_number, sibling)
                wires.got_if(
                    jnp.logical_and(here, jnp.logical_not(via)), block, first_row + step, sibling
                )
                wires.put_if(
                    jnp.logical_and(from_outside, near_home),
                    block,
                    block,
                    far_number,
                    (plane, core, far_z),
                )
            else:
                wires.got_if(here, block, first_row + step, sibling)
            wires.put_if(here, block, block, first_over + step, sibling)

    def rows_passed(kind):
        for step in range(4):
            z_from = lax.rem(2 * parity + kind + 4 - step, 4)
            wires.got_if(core != kind, rows_v.at[kind, z_from], first_over + step, sibling)

    send_rows(0)
    for sign in sides:
        send_late(sign, 1)
    for hop in range(1, 4):
        for sign in sides:
            take_early(sign, hop)
    for sign in sides:
        take_late(sign, 1)
    for sign, hop in hops:
        early_across(sign, hop)
    pass_rows(0)
    send_rows(1)
    for offset in range(1, 4):
        wires.put(
            tables_v.at[plane, core], tables_v.at[plane, core], slot("tp", offset), around[offset]
        )
    for offset in range(1, 4):
        wires.got(tables_v.at[plane_at(plane, offset), core], slot("tp", offset), around[offset])
    wires.put(tables_v.at[:, core], tables_v.at[:, core], slot("ts"), sibling)

    wires.got(other_v, slot("ids"), sibling)
    wires.got(tables_v.at[:, 1 - core], slot("ts"), sibling)
    for row in range(2):
        at = 1 if row else 2 * parity
        here = jnp.where(origin == core, ids_v[at], other_v[at])
        seg = here[:, :seq]
        length = jnp.concatenate([here[:, seq:]] * (seq // 128), 1)
        live = (lax.broadcasted_iota(jnp.int32, (1, seq), 1) < length).astype(jnp.int32)
        seg_out[row] = seg
        live_out[row] = live
        line = jnp.where(live > 0, seg, -1).astype(jnp.float32)
        col_v[row] = jnp.transpose(jnp.broadcast_to(line, (128, seq)))
    for at in range(8):
        for step in range(4):
            bias_out[at, step : step + 1] = biases_v[ahead[step], 2, at : at + 1]
    for at in range(4):
        z_at = rolled(at, zed)
        for s in range(2):
            tab_out[at, :, 128 * s : 128 * s + 128] = jnp.concatenate(
                [tables_v[2 * core + t, s, z_at][:, :HEAD_DIM] for t in range(2)], 1
            )

    for sign, hop in hops:
        early_end(sign, hop)
    rows_passed(0)
    keep = [
        pltpu.make_async_copy(weight_v, weight_out, local.at[5]),
        pltpu.make_async_copy(rows_v, rows_out, local.at[4]),
    ]
    keep[0].start()

    def heads_copy(pair, step):
        z_to = lax.rem(mine + 4 - step, 4)
        own = jnp.logical_and(origin == core, z_to == zed)
        tokens = pl.ds(pl.multiple_of(z_to * share, share), share)
        on_b = lax.div(pair, 4)
        row = on_b + (1 - on_b) * 2 * parity
        target = heads_out.at[row, apart(rolled(lax.rem(pair, 4), zed), z_to), core]
        return own, heads_v.at[pair, tokens], target, (plane, origin, z_to)

    first_heads = slot("h", 0)
    for number in range(1, 4 * PAIRS):
        slot("h", number)

    def attend(pair):
        row, at = lax.div(pair, 4), lax.rem(pair, 4)
        z_at = rolled(at, zed)
        bias = jnp.concatenate([biases_v[z_at, core, j : j + 1] for j in range(3)], 1)
        for quarter in range(4):
            part = nt(rows_v[row, quarter], weight_v[at]) + bias
            qkv_v[pair, quarter * share : (quarter + 1) * share] = part.astype(jnp.bfloat16)
        forward_pair(
            slots,
            qkv_v.at[pair],
            tab_out[at, :, :128],
            tab_out[at, :, 128:],
            seg_out[row].astype(jnp.float32),
            col_v.at[row],
            heads_v.at[pair],
            log_v.at[pair],
        )
        for step in range(4):
            own, source, target, there = heads_copy(pair, step)
            number = first_heads + 4 * pair + step
            copy = wires.copy(source, target, number, there)

            @pl.when(own)
            def _here():
                pltpu.make_async_copy(source, target, recvs.at[number]).start()

            @pl.when(jnp.logical_not(own))
            def _there():
                copy.start()

    pl.loop(0, 2)(attend)
    for sign in sides:
        take_late(sign, 2)
    for sign in sides:
        take_across(sign, 1)
    pass_rows(1)
    pl.loop(2, 4)(attend)
    for sign in sides:
        take_late(sign, 3)
    for sign in sides:
        take_across(sign, 2)
    for sign in sides:
        take_far(sign, 1)
    rows_passed(1)
    keep[1].start()
    pl.loop(4, PAIRS)(attend)
    for sign in sides:
        take_across(sign, 3)
    for sign in sides:
        take_far(sign, 2)
    keep.append(pltpu.make_async_copy(qkv_v, qkv_out, local.at[6]))
    keep[-1].start()
    log_out[...] = log_v[...]
    for sign in sides:
        take_far(sign, 3)
    for at in range(2):
        if at:
            for sign, hop in hops:
                end_across(sign, hop)
        side = core if at == 0 else 1 - core
        keep.append(
            pltpu.make_async_copy(
                feed_v.at[:, side, :, : 2 * part_rows], feed_out.at[:, side], local.at[7 + at]
            )
        )
        keep[-1].start()
        for quarter in range(4):
            keep.append(
                pltpu.make_async_copy(
                    feed_v.at[quarter, side, :, 2 * part_rows :],
                    proj_out.at[:, side, quarter],
                    local.at[9 + 4 * at + quarter],
                )
            )
            keep[-1].start()
    for pair in range(PAIRS):
        for k in range(4):
            half, c = k // 2, k % 2
            step = lax.rem(k + 4 - zed, 4)
            row = 1 if pair >= 4 else 2 * half
            target = heads_out.at[row, apart((pair % 4 + 2 * half) % 4, zed), c]
            wires.got(target, first_heads + 4 * pair + step, (plane, c, 2 * core + half))
        for step in range(4):
            own, source, target, there = heads_copy(pair, step)
            copy = wires.copy(source, target, first_heads + 4 * pair + step, there)
            pl.when(jnp.logical_not(own))(copy.wait_send)
    for copy in keep:
        copy.wait()
    wires.finish()
    assert len(slot_at) == FRONT_COPIES, len(slot_at)


FRONT_COPIES = 159


def front(slots, normed, qkv, bias, table, ids, own):
    bf16, f32 = jnp.bfloat16, jnp.float32
    _, share, width = normed.shape
    seq = 4 * share
    vmem = pl.BlockSpec(memory_space=pltpu.VMEM)
    shaped = jax.ShapeDtypeStruct
    return pl.pallas_call(
        functools.partial(front_kernel, slots),
        in_specs=[ANYWHERE] * 6,
        out_specs=[ANYWHERE] * 6 + [vmem] * 5,
        out_shape=[
            shaped((2, 4, share, width), bf16),
            shaped((4, 384, width), bf16),
            shaped((PAIRS, seq, 384), bf16),
            shaped((3, 4, 2, share, 128), bf16),
            shaped((4, 2, 3, 256, width), bf16),
            shaped((3, 2, 4, 32, width), bf16),
            shaped((PAIRS, 2, seq), f32),
            shaped((4, 16, 256), bf16),
            shaped((2, 1, seq), jnp.int32),
            shaped((2, 1, seq), jnp.int32),
            shaped((8, 4, 128), f32),
        ],
        scratch_shapes=[
            pltpu.SemaphoreType.DMA((FRONT_COPIES,)),
            pltpu.SemaphoreType.DMA((FRONT_COPIES,)),
            pltpu.SemaphoreType.DMA((17,)),
            pltpu.VMEM((2, 4, share, width), bf16),
            pltpu.VMEM((4, 384, width), bf16),
            pltpu.VMEM((PAIRS, seq, 384), bf16),
            pltpu.VMEM((PAIRS, seq, 128), bf16),
            pltpu.VMEM((PAIRS, 2, seq), f32),
            pltpu.VMEM((4, 3, 8, 128), f32),
            pltpu.VMEM((4, 2, 4, 16, 128), bf16),
            pltpu.VMEM(ids.shape, jnp.int32),
            pltpu.VMEM(ids.shape, jnp.int32),
            pltpu.VMEM((2, seq, 128), f32),
            pltpu.VMEM((4, 2, 3, own.shape[0], width), bf16),
        ],
        compiler_params=pltpu.CompilerParams(
            collective_id=0, has_side_effects=True, vmem_limit_bytes=48 << 20
        ),
        cost_estimate=pl.CostEstimate(
            flops=40_000_000_000, bytes_accessed=60 << 20, transcendentals=8_000_000
        ),
        name="front",
    )(normed, qkv, bias, table, ids, own)


def backward_pair(
    slots, qkv, keys_pre, values_pre, seg_row, seg_col, grads_in, logs, dtab, dbias, dk_acc, dv_acc
):
    seq = qkv.shape[0]
    keys, values = qkv[:, 128:256], qkv[:, 256:384]
    keys_t = jnp.transpose(keys)
    keys_pre_t = jnp.transpose(keys_pre)
    pre_row = lax.broadcasted_iota(jnp.int32, (keys_pre.shape[0], QB), 0)
    zero = jnp.zeros((keys_pre.shape[0], 128), jnp.float32)
    dtab_k, dtab_v, dq_sum = zero, zero, jnp.zeros((1, 128), jnp.float32)
    for block in reversed(range(seq // QB)):
        extent = (block + 1) * QB
        here = slice(block * QB, extent)
        visible = visible_to(seg_col, seg_row, block)
        queries = qkv[here, :128] * 0.125
        grads = grads_in[here, :]
        weights, dscores, weights_pre, dscores_pre, query_halves, grad_halves, dq_parts = (
            [], [], [], [], [], [], [],
        )
        for head in range(2):
            rows = slice(head * HEAD_DIM, (head + 1) * HEAD_DIM)
            query, grad = half_mask(queries, head), half_mask(grads, head)
            log_total = logs[head : head + 1, here]
            s_tok = jnp.where(visible, nt(keys[:extent], query), MASKED)
            s_pre = jnp.where(pre_row < slots, nt(keys_pre, query), MASKED)
            w_tok, w_pre = jnp.exp(s_tok - log_total), jnp.exp(s_pre - log_total)
            dp_tok, dp_pre = nt(values[:extent], grad), nt(values_pre, grad)
            delta = jnp.sum(w_tok * dp_tok, 0, keepdims=True) + jnp.sum(
                w_pre * dp_pre, 0, keepdims=True
            )
            ds_tok = (w_tok * (dp_tok - delta)).astype(jnp.bfloat16)
            ds_pre = (w_pre * (dp_pre - delta)).astype(jnp.bfloat16)
            dq_parts.append(nn(keys_t[rows, :extent], ds_tok) + nn(keys_pre_t[rows], ds_pre))
            weights.append(w_tok.astype(jnp.bfloat16))
            weights_pre.append(w_pre.astype(jnp.bfloat16))
            dscores.append(ds_tok)
            dscores_pre.append(ds_pre)
            query_halves.append(query)
            grad_halves.append(grad)
        query_both = jnp.concatenate(query_halves, 0)
        grad_both = jnp.concatenate(grad_halves, 0)
        dv = nn(jnp.concatenate(weights, 1), grad_both)
        dk = nn(jnp.concatenate(dscores, 1), query_both)
        if block == seq // QB - 1:
            dv_acc[...] = dv
            dk_acc[...] = dk
        else:
            dv_acc[:extent] += dv
            dk_acc[:extent] += dk
        dtab_v = dtab_v + nn(jnp.concatenate(weights_pre, 1), grad_both)
        dtab_k = dtab_k + nn(jnp.concatenate(dscores_pre, 1), query_both)
        dq = jnp.transpose(jnp.concatenate(dq_parts, 0)) * 0.125
        dq_sum = dq_sum + jnp.sum(dq, 0, keepdims=True)
        qkv[here, :128] = dq.astype(jnp.bfloat16)
    dk, dv = dk_acc[...], dv_acc[...]
    qkv[:, 128:256] = dk.astype(jnp.bfloat16)
    qkv[:, 256:384] = dv.astype(jnp.bfloat16)
    dbias[...] = jnp.concatenate(
        [dq_sum, jnp.sum(dk, 0, keepdims=True), jnp.sum(dv, 0, keepdims=True)], 1
    )
    dtab[:, :128] = dtab_k
    dtab[:, 128:] = dtab_v


def add_up(rows, target, *sources):
    chunk = 96 if rows % 96 == 0 else 64

    @pl.loop(0, rows // chunk)
    def _add(at):
        span = pl.ds(pl.multiple_of(at * chunk, 32), chunk)
        if len(sources) == 2:
            target[span] = sources[0][span] + sources[1][span]
            return
        value = sources[0][span].astype(jnp.float32)
        for source in sources[1:]:
            value = value + source[span].astype(jnp.float32)
        target[span] = value.astype(jnp.bfloat16)


def back_kernel(
    slots,
    heads_ref, feed_ref, proj_ref, qkv_ref, rows_ref, weight_ref,
    log_ref, tab_ref, seg_ref, live_ref, small_ref, tokens_ref, rout_ref,
    full_out, back_out, first_out, second_out,
    sends, recvs, local,
    dh_v, sib_v, own_v, plane_v, sum_v, z_v, gq_v, plane_q, sum_q, z_q, done_v,
    qkv_v, weight_v, df_v, dfs_v, col_v, dk_acc, dv_acc,
    dtab_v, dbias_v, back_v, first_v, first_in, second_v, second_in,
):
    plane, core, zed = position()
    parity = lax.rem(zed, 2)
    mine = 2 * parity + core
    origin = lax.div(zed, 2)
    sibling = (plane, 1 - core, zed)
    share = heads_ref.shape[3]
    seq = 4 * share
    feed_rows, proj_rows = feed_ref.shape[3], proj_ref.shape[3]
    both = feed_rows + proj_rows
    q_rows = gq_v.shape[2]
    around = [(plane_at(plane, offset), core, zed) for offset in range(4)]
    ahead = [lax.rem(zed + step, 4) for step in range(4)]
    greet(column_partners() + plane_partners())
    wires = Wires(sends, recvs)
    slot_at = {}

    def slot(*name):
        return slot_at.setdefault(name, len(slot_at))

    tokens = pl.ds(pl.multiple_of(zed * share, share), share)
    first_heads = slot("h", 0)
    for number in range(1, 4 * PAIRS):
        slot("h", number)
    for pair in range(PAIRS):
        for step in range(4):
            k = ahead[step]
            half, c = lax.div(k, 2), lax.rem(k, 2)
            z_to = 2 * core + half
            own = jnp.logical_and(c == core, z_to == zed)
            row = 1 if pair >= 4 else 2 * half
            wires.put_unless(
                own,
                heads_ref.at[row, lax.rem(pair % 4 + 2 * half + 4 - zed, 4), c],
                dh_v.at[pair, tokens],
                first_heads + 4 * pair + step,
                (plane, c, z_to),
            )
    turns = [lax.rem(zed + 1 + turn, 4) for turn in range(4)]
    own_copies = []
    for turn in range(4):
        z_at = (turn + 1) % 4
        wires.put(
            feed_ref.at[:, 1 - core, z_at], sib_v.at[turn, :, :feed_rows], slot("s", turn), sibling
        )
        wires.put(
            proj_ref.at[z_at, 1 - core], sib_v.at[turn, :, feed_rows:], slot("sp", turn), sibling
        )
        own_copies.append(
            [
                pltpu.make_async_copy(
                    feed_ref.at[:, core, z_at],
                    own_v.at[turn % 2, :, :feed_rows],
                    local.at[2 * (turn % 2)],
                ),
                pltpu.make_async_copy(
                    proj_ref.at[z_at, core],
                    own_v.at[turn % 2, :, feed_rows:],
                    local.at[2 * (turn % 2) + 1],
                ),
            ]
        )
    later = [
        pltpu.make_async_copy(qkv_ref, qkv_v, local.at[4]),
        pltpu.make_async_copy(weight_ref, weight_v, local.at[5]),
    ]
    for copy in own_copies[0] + own_copies[1] + later:
        copy.start()
    for row in range(2):
        line = jnp.where(live_ref[row] > 0, seg_ref[row], -1).astype(jnp.float32)
        col_v[row] = jnp.transpose(jnp.broadcast_to(line, (128, seq)))

    def chip_sum(turn):
        for copy in own_copies[turn]:
            copy.wait()
        wires.got(sib_v.at[turn, :, :feed_rows], slot("s", turn), sibling)
        wires.got(sib_v.at[turn, :, feed_rows:], slot("sp", turn), sibling)
        for at in range(4):
            add_up(both, sib_v.at[turn, at], sib_v.at[turn, at], own_v.at[turn % 2, at])
        if turn < 2:
            for copy in own_copies[turn + 2]:
                copy.start()
        first, _ = axes(turn)
        for kind, offset in enumerate((3, first)):
            wires.put(
                sib_v.at[turn, plane_at(plane, offset)],
                plane_v.at[kind, turn],
                slot("p", turn, kind),
                around[first],
            )

    def axes(turn):
        return (1, 2) if turn % 2 else (2, 1)

    def merge(turn):
        first, other = axes(turn)
        wires.got(plane_v.at[0, turn], slot("p", turn, 0), around[first])
        target = sib_v.at[turn, plane_at(plane, other)]
        add_up(both, target, target, plane_v.at[0, turn])
        wires.put(target, plane_v.at[2, turn], slot("p", turn, 2), around[other])

    chip_sum(0)
    chip_sum(1)
    for copy in later:
        copy.wait()

    def heads_here(pairs):
        for pair in pairs:
            for step in range(4):
                z_from = lax.rem(mine + 4 - step, 4)
                there = pl.ds(pl.multiple_of(z_from * share, share), share)
                wires.got(dh_v.at[pair, there], first_heads + 4 * pair + step, sibling)

    def attend(pair):
        row, at = lax.div(pair, 4), lax.rem(pair, 4)
        backward_pair(
            slots,
            qkv_v.at[pair],
            tab_ref[at, :, :128],
            tab_ref[at, :, 128:],
            seg_ref[row].astype(jnp.float32),
            col_v.at[row],
            dh_v.at[pair],
            log_ref.at[pair],
            dtab_v.at[pair],
            dbias_v.at[pair],
            dk_acc,
            dv_acc,
        )

    def plane_sum(turn):
        for kind, offset in zip((1, 2), axes(turn)):
            wires.got(plane_v.at[kind, turn], slot("p", turn, kind), around[offset])
        add_up(
            both, sum_v.at[turn], sib_v.at[turn, plane], *[plane_v.at[j, turn] for j in (1, 2)]
        )
        if turn < 3:
            wires.put(
                sum_v.at[turn], z_v.at[turn], slot("z", turn), (plane, core, turns[turn])
            )

    low = lax.rem(zed, 2)
    partners = [
        sibling, around[1], around[2],
        (plane, core, zed + 1 - 2 * low), (plane, core, ahead[2]),
    ]

    def small_send(name, values, arrived, step):
        wires.put(values.at[step], arrived.at[step], slot(name, step), partners[step])

    def small_take(name, values, arrived, step):
        wires.got(arrived.at[step], slot(name, step), partners[step])
        values[step + 1] = values[step] + arrived[step]
        if step < 4:
            small_send(name, values, arrived, step + 1)

    def first_sums():
        first_v[0] = jnp.zeros(first_v.shape[1:], jnp.float32)
        first_v[0, :64] = small_ref[...]
        for at in range(4):
            entry = core * 4 + lax.rem(at + 2 * parity, 4)
            table, bias = dtab_v[at], dbias_v[at]
            if at < 2:
                table, bias = table + dtab_v[4 + at], bias + dbias_v[4 + at]
            base = pl.multiple_of(64 + 32 * entry, 8)
            first_v[0, pl.ds(base, 16)] = table[:, :128]
            first_v[0, pl.ds(base + 16, 16)] = table[:, 128:]
            base = pl.multiple_of(320 + 8 * entry, 8)
            first_v[0, pl.ds(base, 8)] = jnp.concatenate(
                [bias[:, :128], bias[:, 128:256], bias[:, 256:], jnp.zeros((5, 128), jnp.float32)], 0
            )
        small_send("a", first_v, first_in, 0)

    def tanh_part():
        entry = lax.div(plane, 2) * 4 + zed
        base = pl.multiple_of(64 + 32 * entry + 16 * core, 8)
        table = first_v[5, pl.ds(base, 16)]
        table = jnp.where(lax.rem(plane, 2) == 0, table[:, :HEAD_DIM], table[:, HEAD_DIM:])
        part = lax.dot_general(
            table,
            rout_ref[...].astype(jnp.float32),
            (((1,), (1,)), ((), ())),
            preferred_element_type=jnp.float32,
            precision=HIGHEST,
        )
        for j in range(4):
            second_v[0, 16 * j : 16 * j + 16] = part[:, 128 * j : 128 * j + 128]

    def norm_sums():
        span_rows = 64

        def body(at, sums):
            row, part = lax.div(at, share // span_rows), lax.rem(at, share // span_rows)
            span = pl.ds(pl.multiple_of(part * span_rows, span_rows), span_rows)
            grad = back_v[row, span].astype(jnp.float32)
            extra = back_v[3, span].astype(jnp.float32)
            grad = grad + jnp.where(row == 1, extra, 0.0)
            hat, _ = normalize(tokens_ref[row, span].astype(jnp.float32))
            return (
                sums[0] + jnp.sum(grad * hat, 0, keepdims=True),
                sums[1] + jnp.sum(grad, 0, keepdims=True),
            )

        zero = jnp.zeros((1, back_v.shape[2]), jnp.float32)
        sums = lax.fori_loop(0, 3 * (share // span_rows), body, (zero, zero))
        for kind in range(2):
            for j in range(8):
                at = 64 + 8 * kind + j
                second_v[0, at : at + 1] = sums[kind][:, 128 * j : 128 * j + 128]
        small_send("b", second_v, second_in, 0)

    first_row = slot("r", 0)
    for number in range(1, 4):
        slot("r", number)

    def row_grads(kind):
        for quarter in range(4):
            span = slice(quarter * share, (quarter + 1) * share)
            parts = [
                nn(qkv_v[4 * kind + at, span], weight_v[at]) for at in range(2 if kind else 4)
            ]
            total = parts[0] + parts[1]
            for part in parts[2:]:
                total = total + part
            df_v[kind, quarter] = total.astype(jnp.bfloat16)
            wires.put_if(
                core != kind, df_v.at[kind, quarter], dfs_v.at[quarter], slot("df", quarter, kind),
                sibling,
            )

    def send_rows(kind):
        here = core == kind
        for quarter in range(4):
            wires.got_if(here, dfs_v.at[quarter], slot("df", quarter, kind), sibling)

            @pl.when(here)
            def _sum():
                add_up(share, dfs_v.at[quarter], dfs_v.at[quarter], df_v.at[kind, quarter])

        for step in range(4):
            z_to = lax.rem(2 * parity + kind + 4 - step, 4)
            own = jnp.logical_and(origin == core, z_to == zed)
            source, target = dfs_v.at[z_to], back_v.at[2 * parity + kind]

            @pl.when(jnp.logical_and(here, own))
            def _here():
                pltpu.make_async_copy(source, target, recvs.at[first_row + step]).start()

            wires.put_if(
                jnp.logical_and(here, jnp.logical_not(own)),
                source,
                target,
                first_row + step,
                (plane, origin, z_to),
            )

    heads_here((0, 1))
    pl.loop(0, 2)(attend)
    chip_sum(2)
    merge(0)
    heads_here((2, 3))
    pl.loop(2, 4)(attend)
    chip_sum(3)
    merge(1)
    rows_v = own_v
    row_copy = pltpu.make_async_copy(rows_ref, rows_v.at[:, :, :share], local.at[0])
    row_copy.start()
    plane_sum(0)
    row_grads(0)
    merge(2)
    heads_here((4, 5))
    pl.loop(4, PAIRS)(attend)
    merge(3)
    plane_sum(1)
    first_sums()
    send_rows(0)
    row_grads(1)
    plane_sum(2)
    small_take("a", first_v, first_in, 0)
    row_copy.wait()
    rows_a = jnp.concatenate([rows_v[0, j, :share] for j in range(4)], 0)
    for at in range(4):
        grad = outer_sum(qkv_v[at], rows_a)
        if at < 2:
            grad = grad + outer_sum(
                qkv_v[4 + at], jnp.concatenate([rows_v[1, j, :share] for j in range(4)], 0)
            )
        grad = grad.astype(jnp.bfloat16)
        for j in range(4):
            gq_v[at, j] = grad[j * q_rows : (j + 1) * q_rows]
        if at % 2:
            sub = at // 2
            slots_here = slice(at - 1, at + 1)
            first, _ = axes(sub)
            for kind, offset in enumerate((3, first)):
                wires.put(
                    gq_v.at[slots_here, plane_at(plane, offset)],
                    plane_q.at[kind, slots_here],
                    slot("pq", sub, kind),
                    around[first],
                )
    small_take("a", first_v, first_in, 1)
    send_rows(1)
    plane_sum(3)
    small_take("a", first_v, first_in, 2)
    for sub in range(2):
        first, other = axes(sub)
        slots_here = slice(2 * sub, 2 * sub + 2)
        wires.got(plane_q.at[0, slots_here], slot("pq", sub, 0), around[first])
        at_other = plane_at(plane, other)
        for at in (2 * sub, 2 * sub + 1):
            target = gq_v.at[at, at_other]
            add_up(q_rows, target, target, plane_q.at[0, at])
        wires.put(
            gq_v.at[slots_here, at_other], plane_q.at[2, slots_here], slot("pq", sub, 2), around[other]
        )
    small_take("a", first_v, first_in, 3)

    def spread(name, span_of):
        copy = pltpu.make_async_copy(
            done_v.at[span_of(2)],
            full_out.at[plane, core, span_of(2)],
            local.at[6 if name == "f" else 7],
        )
        copy.start()
        for half in range(2):
            for offset in (1, 2) if half == 0 else (2, 1):
                wires.put(
                    done_v.at[span_of(half)],
                    full_out.at[plane, core, span_of(half)],
                    slot(name, half, offset),
                    around[offset],
                )
        wires.put(
            done_v.at[span_of(2)], full_out.at[plane, core, span_of(2)], slot(name, 2, 0), sibling
        )
        return copy

    def spread_on(name, span_of):
        for half in range(2):
            came, goes = (1, 2) if half == 0 else (2, 1)
            piece = full_out.at[plane_at(plane, came), core, span_of(half)]
            wires.got(piece, slot(name, half, came), around[came])
            wires.put(piece, piece, slot(name, half, 3), around[goes])
        for half in range(2):
            came = 2 if half == 0 else 1
            piece = full_out.at[plane_at(plane, came), core, span_of(half)]
            wires.got(piece, slot(name, half, came), around[came])
        for offset in (1, 2):
            piece = full_out.at[plane_at(plane, offset), core, span_of(2)]
            wires.put(piece, piece, slot(name, 2, offset), sibling)

    def spread_far(name, span_of):
        for half in range(2):
            piece = full_out.at[plane_at(plane, 3), core, span_of(half)]
            wires.got(piece, slot(name, half, 3), around[2 if half == 0 else 1])
        piece = full_out.at[plane_at(plane, 3), core, span_of(2)]
        wires.put(piece, piece, slot(name, 2, 3), sibling)

    def spread_end(name, span_of):
        for offset in range(4):
            wires.got(
                full_out.at[plane_at(plane, offset), 1 - core, span_of(2)],
                slot(name, 2, offset),
                sibling,
            )

    def feed_span(half):
        return (pl.ds(0, both // 2), pl.ds(both // 2, both // 2), pl.ds(0, both))[half]

    def q_span(half):
        return (
            pl.ds(both, q_rows // 2), pl.ds(both + q_rows // 2, q_rows // 2), pl.ds(both, q_rows)
        )[half]

    for turn in range(3):
        wires.got(z_v.at[turn], slot("z", turn), (plane, core, lax.rem(zed + 3 - turn, 4)))
    add_up(both, done_v.at[feed_span(2)], sum_v.at[3], *[z_v.at[j] for j in range(3)])
    last = [spread("f", feed_span)]
    small_take("a", first_v, first_in, 4)
    tanh_part()
    for sub in range(2):
        slots_here = slice(2 * sub, 2 * sub + 2)
        for kind, offset in zip((1, 2), axes(sub)):
            wires.got(plane_q.at[kind, slots_here], slot("pq", sub, kind), around[offset])
        for at in (2 * sub, 2 * sub + 1):
            add_up(q_rows, sum_q.at[at], gq_v.at[at, plane], *[plane_q.at[j, at] for j in (1, 2)])
    for turn in range(3):
        wires.put(
            sum_q.at[lax.rem(turns[turn] + 2 * parity, 4)],
            z_q.at[turn],
            slot("zq", turn),
            (plane, core, turns[turn]),
        )
    spread_on("f", feed_span)
    for k in range(4):
        wires.got(
            back_v.at[k],
            first_row + lax.rem(k + 4 - zed, 4),
            (plane, k % 2, 2 * core + k // 2),
        )
    last.append(pltpu.make_async_copy(back_v, back_out, local.at[8]))
    last[-1].start()
    norm_sums()
    for turn in range(3):
        wires.got(z_q.at[turn], slot("zq", turn), (plane, core, lax.rem(zed + 3 - turn, 4)))
    add_up(
        q_rows,
        done_v.at[q_span(2)],
        sum_q.at[lax.rem(zed + 2 * parity, 4)],
        *[z_q.at[j] for j in range(3)],
    )
    last.append(spread("q", q_span))
    small_take("b", second_v, second_in, 0)
    spread_far("f", feed_span)
    small_take("b", second_v, second_in, 1)
    spread_on("q", q_span)
    small_take("b", second_v, second_in, 2)
    spread_far("q", q_span)
    small_take("b", second_v, second_in, 3)
    small_take("b", second_v, second_in, 4)
    first_out[...] = first_v[5]
    second_out[...] = second_v[5]
    spread_end("f", feed_span)
    spread_end("q", q_span)
    for copy in last:
        copy.wait()
    wires.finish()
    assert len(slot_at) == BACK_COPIES, len(slot_at)


BACK_COPIES = 98


def back(
    slots, d_heads, grad_feed, grad_out, qkv, rows, weights, logs, tab, seg, live, small, tokens, rout
):
    bf16, f32 = jnp.bfloat16, jnp.float32
    share, width = rows.shape[2:]
    seq = 4 * share
    vmem = pl.BlockSpec(memory_space=pltpu.VMEM)
    shaped, held = jax.ShapeDtypeStruct, pltpu.VMEM
    both, q_rows = grad_feed.shape[3] + grad_out.shape[3], 96
    return pl.pallas_call(
        functools.partial(back_kernel, slots),
        in_specs=[ANYWHERE] * 6 + [vmem] * 7,
        out_specs=[ANYWHERE] * 2 + [vmem] * 2,
        out_shape=[
            shaped((4, 2, both + q_rows, width), bf16),
            shaped((4, share, width), bf16),
            shaped((384, 128), f32),
            shaped((80, 128), f32),
        ],
        scratch_shapes=[
            pltpu.SemaphoreType.DMA((BACK_COPIES,)),
            pltpu.SemaphoreType.DMA((BACK_COPIES,)),
            pltpu.SemaphoreType.DMA((9,)),
            held((PAIRS, seq, 128), bf16),
            held((4, 4, both, width), bf16),
            held((2, 4, both, width), bf16),
            held((3, 4, both, width), bf16),
            held((4, both, width), bf16),
            held((3, both, width), bf16),
            held((4, 4, q_rows, width), bf16),
            held((3, 4, q_rows, width), bf16),
            held((4, q_rows, width), bf16),
            held((3, q_rows, width), bf16),
            held((both + q_rows, width), bf16),
            held((PAIRS, seq, 384), bf16),
            held((4, 384, width), bf16),
            held((2, 4, share, width), bf16),
            held((4, share, width), bf16),
            held((2, seq, 128), f32),
            held((seq, 128), f32),
            held((seq, 128), f32),
            held((PAIRS, 16, 256), f32),
            held((PAIRS, 1, 384), f32),
            held((4, share, width), bf16),
            held((6, 384, 128), f32),
            held((5, 384, 128), f32),
            held((6, 80, 128), f32),
            held((5, 80, 128), f32),
        ],
        compiler_params=pltpu.CompilerParams(
            collective_id=2, has_side_effects=True, vmem_limit_bytes=62 << 20
        ),
        cost_estimate=pl.CostEstimate(
            flops=80_000_000_000, bytes_accessed=60 << 20, transcendentals=8_000_000
        ),
        name="back",
    )(
        d_heads, grad_feed, grad_out, qkv, rows, weights, logs, tab, seg, live, small, tokens, rout
    )


def write_feed_kernel(piece_ref, up_ref, down_ref):
    for c in range(2):
        span = slice(128 * c, 128 * c + 128)
        up_ref[:, span] = jnp.transpose(piece_ref[0, c, :128].astype(jnp.float32))
        down_ref[span] = piece_ref[0, c, 128:].astype(jnp.float32)


def write_rest_kernel(piece_ref, grad_ref, out_ref):
    for at in range(4):
        out_ref[32 * at : 32 * at + 32] = piece_ref[at, 0, :32].astype(jnp.float32)
    turned = [jnp.transpose(piece_ref[at, 0, 32:].astype(jnp.float32)) for at in range(4)]
    turned = jnp.concatenate(turned, 1)
    order = [(kind, head) for head in range(2) for kind in range(3)]
    grad_ref[...] = jnp.concatenate(
        [turned[:, 128 * kind + 64 * head : 128 * kind + 64 * head + 64] for kind, head in order], 1
    )


def write_grads(full):
    f32 = jnp.float32
    width = full.shape[3]
    up, down = pl.pallas_call(
        write_feed_kernel,
        grid=(4,),
        in_specs=[pl.BlockSpec((1, 2, 256, width), lambda p: (p, 0, 0, 0))],
        out_specs=[
            pl.BlockSpec((width, 256), lambda p: (0, p)),
            pl.BlockSpec((256, width), lambda p: (p, 0)),
        ],
        out_shape=[
            jax.ShapeDtypeStruct((width, 1024), f32),
            jax.ShapeDtypeStruct((1024, width), f32),
        ],
        name="write_feed",
    )(full)
    qkv, out = pl.pallas_call(
        write_rest_kernel,
        grid=(2,),
        in_specs=[pl.BlockSpec((4, 1, 128, width), lambda c: (0, c, 2, 0))],
        out_specs=[
            pl.BlockSpec((width, 384), lambda c: (0, c)),
            pl.BlockSpec((128, width), lambda c: (c, 0)),
        ],
        out_shape=[
            jax.ShapeDtypeStruct((width, 768), f32),
            jax.ShapeDtypeStruct((256, width), f32),
        ],
        compiler_params=pltpu.CompilerParams(vmem_limit_bytes=40 << 20),
        name="write_rest",
    )(full)
    return up, down, out, qkv


def per_device_fast(
    tokens,
    segment_ids,
    row_lengths,
    ln1_gain,
    ln1_bias,
    qkv_weight,
    qkv_bias,
    out_weight,
    out_bias,
    ln2_gain,
    ln2_bias,
    up_weight,
    up_bias,
    down_weight,
    down_bias,
    prefix_embed,
    reparam_in,
    reparam_in_bias,
    reparam_out,
    reparam_out_bias,
    cotangent,
):
    bf16, f32 = jnp.bfloat16, jnp.float32
    plane, core, zed = lax.axis_index("pl"), lax.axis_index("core"), lax.axis_index("mp")
    micro, share, width = tokens.shape
    seq = segment_ids.shape[1]
    slots = prefix_embed.shape[0]

    def pick(stack, index):
        return lax.dynamic_index_in_dim(stack, index, 0, keepdims=False)

    pre_act = nn(prefix_embed, reparam_in) + reparam_in_bias
    tanh_hidden = jnp.tanh(pre_act)
    tanh_low = tanh_hidden.astype(bf16)
    table_part = (nn(tanh_low, reparam_out) + reparam_out_bias).astype(bf16)
    table_part = jnp.pad(table_part, ((0, 16 - slots), (0, 128 - HEAD_DIM)))
    packed_ids = jnp.concatenate(
        [segment_ids, jnp.broadcast_to(row_lengths[:, :1], (micro, 128))], 1
    )
    packed_ids = jnp.pad(packed_ids, ((0, 8 - micro), (0, 0)))[:, None]
    packed_bias = jnp.concatenate(
        [
            jnp.pad(
                qkv_bias.reshape(2, 2, 3, HEAD_DIM).transpose(0, 2, 1, 3).reshape(2, 3, 128),
                ((0, 0), (0, 5), (0, 0)),
            ),
            up_bias.reshape(1, 8, 128),
        ]
    )
    x_share = tokens.astype(f32)
    hat_first, inverse_first = normalize(x_share)
    normed_first = (hat_first * ln1_gain + ln1_bias).astype(bf16)
    qkv_half = lax.dynamic_index_in_dim(
        qkv_weight.reshape(width, 2, 2, 3, HEAD_DIM), core, 1, keepdims=False
    )
    qkv_half = qkv_half.transpose(2, 1, 3, 0).reshape(384, width)
    down_own = down_weight.reshape(8, 128, width)
    (
        normed_home, qkv_full, qkv, heads_rows, feed_full, out_full, logs, tab, seg, live, biases
    ) = front(
        slots,
        normed_first,
        qkv_half,
        packed_bias,
        table_part,
        packed_ids,
        jnp.concatenate(
            [
                lax.dynamic_slice_in_dim(up_weight, (2 * plane + core) * 128, 128, 1).T,
                pick(down_own, 2 * plane + core),
                lax.dynamic_slice_in_dim(out_weight, core * 128 + plane * 32, 32, 0),
            ]
        ),
    )
    up_bias_all = biases.reshape(8, 1, 512)
    block_out, d_resid, d_heads, grad_out, sums, grad_feed, grad_up_bias = feed_forward(
        heads_rows,
        tokens.reshape(3 * share, width),
        cotangent.reshape(3 * share, width),
        out_weight,
        out_full.reshape(3 * 256, width),
        jnp.stack([out_bias, ln2_gain, ln2_bias, down_bias]),
        up_weight,
        down_own,
        feed_full.reshape(8, 3, 256, width),
        up_bias_all,
    )
    block_out = block_out.reshape(tokens.shape)
    grad_feed = grad_feed.reshape(4, 2, 4, 256, width)
    grad_out = grad_out.reshape(4, 2, 4, 32, width)
    small = jnp.concatenate(
        [
            jnp.roll(grad_up_bias.reshape(8, 4, 128), zed, 1).reshape(32, 128),
            sums.reshape(32, 128),
        ]
    )
    full, came, first, second = back(
        slots,
        d_heads,
        grad_feed,
        grad_out,
        qkv,
        normed_home,
        qkv_full,
        logs,
        tab,
        seg,
        live,
        small,
        tokens,
        reparam_out,
    )
    came = came.astype(f32)
    d_first = jnp.stack([came[0], came[1] + came[3], came[2]])
    input_grad = d_resid.reshape(tokens.shape) + norm_back(
        d_first, hat_first, inverse_first, ln1_gain
    )
    grad_up, grad_down, grad_out, grad_qkv = write_grads(full)
    grad_up_bias = pick(first[:32].reshape(8, 4, 128).transpose(1, 0, 2).reshape(4, 1024), zed)
    ln2_gain_grad, ln2_bias_grad, out_bias_grad, down_bias_grad = first[32:64].reshape(4, width)
    table_own = first[64:320].reshape(2, 4, 2, 16, 2, HEAD_DIM)
    table_own = table_own[plane // 2, zed, core, :slots, plane % 2]
    grad_qkv_bias = pick(
        first[320:].reshape(2, 4, 8, 2, HEAD_DIM).transpose(1, 0, 3, 2, 4)[..., :3, :], zed
    ).reshape(768)
    grad_rout = jnp.dot(tanh_low.astype(f32).T, table_own, precision=HIGHEST)
    grad_rout_bias = jnp.sum(table_own, 0)
    tanh_sum = second[:64].reshape(4, 16, 128).transpose(1, 0, 2).reshape(16, 512)[:slots]
    ln1_gain_grad, ln1_bias_grad = second[64:].reshape(2, width)
    d_pre = tanh_sum * (1.0 - tanh_hidden * tanh_hidden)
    grad_rin = jnp.dot(prefix_embed.astype(f32).T, d_pre, precision=HIGHEST)
    grad_rin_bias = jnp.sum(d_pre, 0)
    grad_embed = jnp.dot(d_pre, reparam_in.astype(f32).T, precision=HIGHEST)
    return (
        block_out,
        input_grad,
        ln1_gain_grad,
        ln1_bias_grad,
        grad_qkv,
        grad_qkv_bias,
        grad_out,
        out_bias_grad,
        ln2_gain_grad,
        ln2_bias_grad,
        grad_up,
        grad_up_bias,
        grad_down,
        down_bias_grad,
        grad_embed,
        grad_rin,
        grad_rin_bias,
        grad_rout,
        grad_rout_bias,
    )


def specs(dp, mp):
    rows = P(None, dp + mp, None)
    ins = (
        rows, P(None, dp), P(None, dp), P(), P(), P(None, mp), P(mp), P(mp, None), P(), P(), P(),
        P(None, mp), P(mp), P(mp, None), P(), P(), P(), P(), P(None, mp + dp), P(mp + dp), rows,
    )
    outs = (
        rows, rows, P(), P(), P(None, mp), P(mp), P(mp, None), P(), P(), P(), P(None, mp), P(mp),
        P(mp, None), P(), P(), P(), P(), P(None, mp + dp), P(mp + dp),
    )
    return ins, outs


def solution(mesh):
    if mesh.shape["dp"] == 8 and mesh.shape["mp"] == 4:
        body = per_device_fast
        grid = jax.sharding.Mesh(mesh.devices.reshape(4, 2, 4), ALL)
        ins, outs = specs(("pl", "core"), ("mp",))
    else:
        body = per_device
        grid = mesh
        ins, outs = specs(("dp",), ("mp",))
    return jax.shard_map(body, mesh=grid, in_specs=ins, out_specs=outs, check_vma=False)
```

```python
import functools
import math

import jax
import jax.numpy as jnp
from jax import lax
from jax.experimental import pallas as pl
from jax.experimental.pallas import tpu as pltpu
from jax.sharding import PartitionSpec as P

HEAD_DIM = 64


EPSILON = 1e-05
MASKED = -1e30
HIGHEST = lax.Precision.HIGHEST


def normalize(inputs):
    average = jnp.mean(inputs, -1, keepdims=True)
    centered = inputs - average
    variance = jnp.mean(centered * centered, -1, keepdims=True)
    inverse = lax.rsqrt(variance + EPSILON)
    return (centered * inverse, inverse)


def norm_back(grad_norm, normed_hat, inverse, norm_gain):
    scaled = grad_norm * norm_gain
    return inverse * (
        scaled
        - jnp.mean(scaled, -1, keepdims=True)
        - normed_hat * jnp.mean(scaled * normed_hat, -1, keepdims=True)
    )


def product_transposed(rows_in, matrix):
    return lax.dot_general(
        rows_in, matrix, (((1,), (1,)), ((), ())), preferred_element_type=jnp.float32
    )


def outer_sum(left, right):
    return lax.dot_general(
        left, right, (((0,), (0,)), ((), ())), preferred_element_type=jnp.float32
    )


def gelu_tanh(values_in):
    return jax.nn.gelu(values_in, approximate=True)


def attention_scores(queries, keys_tok, keys_pre, visible, log_total):
    score_scale = 1.0 / math.sqrt(queries.shape[-1])
    scores_tok = (
        jnp.einsum("hqd,hkd->hqk", queries, keys_tok, preferred_element_type=jnp.float32)
        * score_scale
    )
    scores_tok = jnp.where(visible[None], scores_tok, MASKED)
    scores_pre = (
        jnp.einsum("hqd,hkd->hqk", queries, keys_pre, preferred_element_type=jnp.float32)
        * score_scale
    )
    if log_total is None:
        highest = jnp.maximum(
            jnp.max(scores_tok, -1, keepdims=True), jnp.max(scores_pre, -1, keepdims=True)
        )
        totals = jnp.sum(jnp.exp(scores_tok - highest), -1, keepdims=True) + jnp.sum(
            jnp.exp(scores_pre - highest), -1, keepdims=True
        )
        log_total = highest + jnp.log(totals)
    return (jnp.exp(scores_tok - log_total), jnp.exp(scores_pre - log_total), log_total)


def per_device(
    tokens,
    segment_ids,
    row_lengths,
    ln1_gain,
    ln1_bias,
    qkv_weight,
    qkv_bias,
    out_weight,
    out_bias,
    ln2_gain,
    ln2_bias,
    up_weight,
    up_bias,
    down_weight,
    down_bias,
    prefix_embed,
    reparam_in,
    reparam_in_bias,
    reparam_out,
    reparam_out_bias,
    cotangent,
):
    width_head = out_weight.shape[0]
    heads_local = width_head // HEAD_DIM
    prefix_slots = prefix_embed.shape[0]
    pre_act = (
        jnp.dot(prefix_embed, reparam_in, preferred_element_type=jnp.float32) + reparam_in_bias
    )
    tanh_hidden = jnp.tanh(pre_act)
    tanh_low = tanh_hidden.astype(jnp.bfloat16)
    table_part = (
        jnp.dot(tanh_low, reparam_out, preferred_element_type=jnp.float32) + reparam_out_bias
    ).astype(jnp.bfloat16)

    def micro_step(carried, inputs):
        big_sums, small_sums, table_grad = carried
        tokens_mb, segments_mb, length_mb, cotangent_mb = inputs
        table_full = lax.all_gather(table_part, "dp", axis=1, tiled=True)
        seq_len = segments_mb.shape[0]
        table_heads = table_full.reshape(prefix_slots, heads_local, 2, HEAD_DIM).transpose(
            2, 1, 0, 3
        )
        positions = jnp.arange(seq_len)
        visible = (
            (segments_mb[:, None] == segments_mb[None, :])
            & (positions[None, :] <= positions[:, None])
            & (positions[None, :] < length_mb)
        )
        x_share = tokens_mb.astype(jnp.float32)
        hat_first, inverse_first = normalize(x_share)
        normed_first = lax.all_gather(
            (hat_first * ln1_gain + ln1_bias).astype(jnp.bfloat16), "mp", axis=0, tiled=True
        )
        qkv_low = (
            jnp.dot(normed_first, qkv_weight, preferred_element_type=jnp.float32) + qkv_bias
        ).astype(jnp.bfloat16)
        packed = qkv_low.reshape(seq_len, heads_local, 3, HEAD_DIM).transpose(2, 1, 0, 3)
        weights_tok, weights_pre, log_total = attention_scores(
            packed[0], packed[1], table_heads[0], visible, None
        )
        heads_out = (
            jnp.einsum(
                "hqk,hkd->hqd",
                weights_tok.astype(jnp.bfloat16),
                packed[2],
                preferred_element_type=jnp.float32,
            )
            + jnp.einsum(
                "hqk,hkd->hqd",
                weights_pre.astype(jnp.bfloat16),
                table_heads[1],
                preferred_element_type=jnp.float32,
            )
        ).astype(jnp.bfloat16)
        head_rows = heads_out.transpose(1, 0, 2).reshape(seq_len, width_head)
        resid = (
            x_share
            + lax.psum_scatter(
                jnp.dot(head_rows, out_weight, preferred_element_type=jnp.float32).astype(
                    jnp.bfloat16
                ),
                "mp",
                scatter_dimension=0,
                tiled=True,
            ).astype(jnp.float32)
            + out_bias
        )
        hat_second, inverse_second = normalize(resid)
        normed_second = lax.all_gather(
            (hat_second * ln2_gain + ln2_bias).astype(jnp.bfloat16), "mp", axis=0, tiled=True
        )
        up_act = jnp.dot(normed_second, up_weight, preferred_element_type=jnp.float32) + up_bias
        gelu_out, gelu_back = jax.vjp(gelu_tanh, up_act)
        hidden_low = gelu_out.astype(jnp.bfloat16)
        block_share = (
            resid
            + lax.psum_scatter(
                jnp.dot(hidden_low, down_weight, preferred_element_type=jnp.float32).astype(
                    jnp.bfloat16
                ),
                "mp",
                scatter_dimension=0,
                tiled=True,
            ).astype(jnp.float32)
            + down_bias
        ).astype(jnp.bfloat16)
        cot_full = lax.all_gather(cotangent_mb, "mp", axis=0, tiled=True)
        d_up = gelu_back(product_transposed(cot_full, down_weight))[0].astype(jnp.bfloat16)
        grad_down = outer_sum(hidden_low, cot_full)
        grad_up = outer_sum(normed_second, d_up)
        grad_up_bias = jnp.sum(d_up.astype(jnp.float32), 0)
        d_second = lax.psum_scatter(
            product_transposed(d_up, up_weight).astype(jnp.bfloat16),
            "mp",
            scatter_dimension=0,
            tiled=True,
        ).astype(jnp.float32)
        cot_share = cotangent_mb.astype(jnp.float32)
        d_resid = cot_share + norm_back(d_second, hat_second, inverse_second, ln2_gain)
        d_attn = lax.all_gather(d_resid.astype(jnp.bfloat16), "mp", axis=0, tiled=True)
        grad_out = outer_sum(head_rows, d_attn)
        d_heads = (
            product_transposed(d_attn, out_weight)
            .astype(jnp.bfloat16)
            .reshape(seq_len, heads_local, HEAD_DIM)
            .transpose(1, 0, 2)
        )
        weights_tok, weights_pre, unused_total = attention_scores(
            packed[0], packed[1], table_heads[0], visible, log_total
        )
        score_scale = 1.0 / math.sqrt(HEAD_DIM)
        d_vtok = jnp.einsum(
            "hqk,hqd->hkd",
            weights_tok.astype(jnp.bfloat16),
            d_heads,
            preferred_element_type=jnp.float32,
        )
        d_vpre = jnp.einsum(
            "hqk,hqd->hkd",
            weights_pre.astype(jnp.bfloat16),
            d_heads,
            preferred_element_type=jnp.float32,
        )
        dprob_tok = jnp.einsum(
            "hqd,hkd->hqk", d_heads, packed[2], preferred_element_type=jnp.float32
        )
        dprob_pre = jnp.einsum(
            "hqd,hkd->hqk", d_heads, table_heads[1], preferred_element_type=jnp.float32
        )
        delta = jnp.sum(weights_tok * dprob_tok, -1, keepdims=True) + jnp.sum(
            weights_pre * dprob_pre, -1, keepdims=True
        )
        dscore_tok = (weights_tok * (dprob_tok - delta)).astype(jnp.bfloat16)
        dscore_pre = (weights_pre * (dprob_pre - delta)).astype(jnp.bfloat16)
        d_queries = (
            jnp.einsum("hqk,hkd->hqd", dscore_tok, packed[1], preferred_element_type=jnp.float32)
            + jnp.einsum(
                "hqk,hkd->hqd", dscore_pre, table_heads[0], preferred_element_type=jnp.float32
            )
        ) * score_scale
        d_ktok = (
            jnp.einsum("hqk,hqd->hkd", dscore_tok, packed[0], preferred_element_type=jnp.float32)
            * score_scale
        )
        d_kpre = (
            jnp.einsum("hqk,hqd->hkd", dscore_pre, packed[0], preferred_element_type=jnp.float32)
            * score_scale
        )
        prefix_add = (
            jnp.stack([d_kpre, d_vpre], 0)
            .transpose(2, 1, 0, 3)
            .reshape(prefix_slots, 2 * width_head)
        )
        d_qkv = (
            jnp.stack([d_queries, d_ktok, d_vtok], 0)
            .transpose(2, 1, 0, 3)
            .reshape(seq_len, 3 * width_head)
            .astype(jnp.bfloat16)
        )
        grad_qkv = outer_sum(normed_first, d_qkv)
        grad_qkv_bias = jnp.sum(d_qkv.astype(jnp.float32), 0)
        d_first = lax.psum_scatter(
            product_transposed(d_qkv, qkv_weight).astype(jnp.bfloat16),
            "mp",
            scatter_dimension=0,
            tiled=True,
        ).astype(jnp.float32)
        input_grad = d_resid + norm_back(d_first, hat_first, inverse_first, ln1_gain)
        small_add = (
            jnp.sum(d_first * hat_first, 0),
            jnp.sum(d_first, 0),
            jnp.sum(d_second * hat_second, 0),
            jnp.sum(d_second, 0),
            jnp.sum(d_resid, 0),
            jnp.sum(cot_share, 0),
        )
        big_add = (
            lax.psum(grad_qkv.astype(jnp.bfloat16), "dp").astype(jnp.float32),
            lax.psum(grad_qkv_bias.astype(jnp.bfloat16), "dp").astype(jnp.float32),
            lax.psum(grad_out.astype(jnp.bfloat16), "dp").astype(jnp.float32),
            lax.psum(grad_up.astype(jnp.bfloat16), "dp").astype(jnp.float32),
            lax.psum(grad_up_bias.astype(jnp.bfloat16), "dp").astype(jnp.float32),
            lax.psum(grad_down.astype(jnp.bfloat16), "dp").astype(jnp.float32),
        )
        big_sums = jax.tree.map(jnp.add, big_sums, tuple(big_add))
        small_sums = jax.tree.map(jnp.add, small_sums, small_add)
        return ((big_sums, small_sums, table_grad + prefix_add), (block_share, input_grad))

    big_zero = tuple(
        (
            jnp.zeros(member.shape, jnp.float32)
            for member in (qkv_weight, qkv_bias, out_weight, up_weight, up_bias, down_weight)
        )
    )
    small_zero = tuple((jnp.zeros(ln1_gain.shape, jnp.float32) for member in range(6)))
    table_zero = jnp.zeros((prefix_slots, 2 * width_head), jnp.float32)
    carried, stacked = lax.scan(
        micro_step,
        (big_zero, small_zero, table_zero),
        (tokens, segment_ids, row_lengths[:, 0], cotangent),
    )
    big_sums, small_sums, table_grad = carried
    block_out, input_grad = stacked
    table_own = lax.psum_scatter(table_grad, "dp", scatter_dimension=1, tiled=True)
    grad_rout = jnp.dot(tanh_low.astype(jnp.float32).T, table_own, precision=HIGHEST)
    grad_rout_bias = jnp.sum(table_own, 0)
    tanh_part = jnp.dot(table_own, reparam_out.astype(jnp.float32).T, precision=HIGHEST)
    shared = lax.psum(
        (
            tanh_part,
            small_sums[0],
            small_sums[1],
            small_sums[2],
            small_sums[3],
            small_sums[4],
            small_sums[5],
        ),
        ("dp", "mp"),
    )
    d_pre = shared[0] * (1.0 - tanh_hidden * tanh_hidden)
    grad_rin = jnp.dot(prefix_embed.astype(jnp.float32).T, d_pre, precision=HIGHEST)
    grad_rin_bias = jnp.sum(d_pre, 0)
    grad_embed = jnp.dot(d_pre, reparam_in.astype(jnp.float32).T, precision=HIGHEST)
    return (
        block_out,
        input_grad,
        shared[1],
        shared[2],
        big_sums[0],
        big_sums[1],
        big_sums[2],
        shared[5],
        shared[3],
        shared[4],
        big_sums[3],
        big_sums[4],
        big_sums[5],
        shared[6],
        grad_embed,
        grad_rin,
        grad_rin_bias,
        grad_rout,
        grad_rout_bias,
    )


ALL = ("pl", "core", "mp")
QB = 256
MICRO = 3


def nt(left, right):
    return lax.dot_general(
        left, right, (((1,), (1,)), ((), ())), preferred_element_type=jnp.float32
    )


def nn(left, right):
    return jnp.dot(left, right, preferred_element_type=jnp.float32)


def half_mask(value, head):
    lane = lax.broadcasted_iota(jnp.int32, value.shape, 1)
    keep = (lane < HEAD_DIM) if head == 0 else (lane >= HEAD_DIM)
    return jnp.where(keep, value, jnp.zeros_like(value))


GELU_A = math.sqrt(2.0 / math.pi)
GELU_B = 0.044715


def feed_kernel(
    heads_ref, tokens_ref, cot_ref, out_own_ref, out_ref, obias_ref, gain_ref, offset_ref, dbias_ref,
    own_up_ref, own_down_ref, weight_ref, bias_ref,
    block_ref, resid_ref, dheads_ref, gout_ref, sums_ref, grad_ref, gbias_ref,
    heads_s, normed_s, resid_s, mlp_s, dn_s,
):
    step = pl.program_id(0)
    blocks, near, cores, share, lanes = heads_ref.shape
    own_rows = out_own_ref.shape[0]
    out_bias, gain, offset, down_bias = obias_ref[...], gain_ref[...], offset_ref[...], dbias_ref[...]

    @pl.when(step == 0)
    def _before():
        for m in range(blocks):
            rows = slice(m * share, (m + 1) * share)
            heads = jnp.concatenate(
                [heads_ref[m, r, c] for r in range(near) for c in range(cores)], 1
            )
            heads_s[rows] = heads
            resid = (
                tokens_ref[rows].astype(jnp.float32)
                + nn(heads[:, :own_rows], out_own_ref[...])
                + nn(heads[:, own_rows:], out_ref[...])
                + out_bias
            )
            resid_s[rows] = resid
            hat, _ = normalize(resid)
            normed_s[rows] = (hat * gain + offset).astype(jnp.bfloat16)

    normed, cot = normed_s[...], cot_ref[...]
    groups, depth, width = grad_ref.shape[1:]
    half_rows = depth // 2
    units = (groups - 1) * half_rows
    up = jnp.concatenate(
        [jnp.transpose(own_up_ref[...]), weight_ref[0, :, :half_rows].reshape(units, width)], 0
    )
    down = jnp.concatenate(
        [own_down_ref[0], weight_ref[0, :, half_rows:].reshape(units, width)], 0
    )
    act = nt(normed, up) + bias_ref[0]
    square = act * act
    curve = jnp.tanh(GELU_A * act * (1.0 + GELU_B * square))
    half = 0.5 * (1.0 + curve)
    hidden = (act * half).astype(jnp.bfloat16)
    slope = half + 0.5 * act * (1.0 - curve * curve) * (
        GELU_A * (1.0 + (3.0 * GELU_B) * square)
    )
    d_act = nt(cot, down) * slope
    gbias_ref[0] = jnp.sum(d_act, 0, keepdims=True)
    d_low = d_act.astype(jnp.bfloat16)
    gup = outer_sum(d_low, normed).astype(jnp.bfloat16)
    gdown = outer_sum(hidden, cot).astype(jnp.bfloat16)
    grad_ref[0, :, :half_rows] = gup.reshape(groups, half_rows, width)
    grad_ref[0, :, half_rows:] = gdown.reshape(groups, half_rows, width)
    mlp, dn = nn(hidden, down), nn(d_low, up)

    @pl.when(step == 0)
    def _first():
        mlp_s[...] = mlp
        dn_s[...] = dn

    @pl.when(step > 0)
    def _later():
        mlp_s[...] += mlp
        dn_s[...] += dn

    @pl.when(step == pl.num_programs(0) - 1)
    def _after():
        sums = [jnp.zeros((1, width), jnp.float32) for _ in range(4)]
        for m in range(blocks):
            rows = slice(m * share, (m + 1) * share)
            resid, d_second = resid_s[rows], dn_s[rows]
            block_ref[rows] = (resid + mlp_s[rows] + down_bias).astype(jnp.bfloat16)
            hat, inverse = normalize(resid)
            cot_wide = cot_ref[rows].astype(jnp.float32)
            d_resid = cot_wide + norm_back(d_second, hat, inverse, gain)
            resid_ref[rows] = d_resid
            for j, value in enumerate((d_second * hat, d_second, d_resid, cot_wide)):
                sums[j] = sums[j] + jnp.sum(value, 0, keepdims=True)
            d_attn = d_resid.astype(jnp.bfloat16)
            normed_s[rows] = d_attn
            d_own = nt(d_attn, out_own_ref[...]).astype(jnp.bfloat16)
            d_rest = nt(d_attn, out_ref[...]).astype(jnp.bfloat16)
            for r in range(near):
                for c in range(cores):
                    source = d_rest if r else d_own
                    at = (2 * r + c) * lanes - (own_rows if r else 0)
                    dheads_ref[m, r, c] = source[:, at : at + lanes]
        for j in range(4):
            sums_ref[j : j + 1] = sums[j]
        for j in range(near):
            columns = slice(j * own_rows, (j + 1) * own_rows)
            gout_ref[columns] = outer_sum(heads_s[:, columns], normed_s[...]).astype(jnp.bfloat16)


def feed_forward(heads, tokens, cot, out_own, out, vectors, own_up, own_down, weights, bias):
    rows, width = tokens.shape
    tiles, others, depth, _ = weights.shape
    groups = others + 1
    units = groups * depth // 2
    once = pl.Buffered(1)

    def whole(shape):
        return pl.BlockSpec(shape, lambda i: (0,) * len(shape), pipeline_mode=once)

    shaped, bf16, f32 = jax.ShapeDtypeStruct, jnp.bfloat16, jnp.float32
    line = pl.BlockSpec((1, 1, units), lambda i: (i, 0, 0))
    square = (rows, width)
    return pl.pallas_call(
        feed_kernel,
        grid=(tiles,),
        in_specs=[
            whole(heads.shape),
            whole(square),
            whole(square),
            whole(out_own.shape),
            whole(out.shape),
            *[whole((1, width))] * 4,
            pl.BlockSpec((width, depth // 2), lambda i: (0, i)),
            pl.BlockSpec((1, depth // 2, width), lambda i: (i, 0, 0)),
            pl.BlockSpec((1, others, depth, width), lambda i: (i, 0, 0, 0)),
            line,
        ],
        out_specs=[
            whole(square),
            whole(square),
            whole(heads.shape),
            whole((width, width)),
            whole((4, width)),
            pl.BlockSpec((1, groups, depth, width), lambda i: (i, 0, 0, 0)),
            line,
        ],
        out_shape=[
            shaped(square, bf16),
            shaped(square, f32),
            shaped(heads.shape, bf16),
            shaped((width, width), bf16),
            shaped((4, width), f32),
            shaped((tiles, groups, depth, width), bf16),
            shaped((tiles, 1, units), f32),
        ],
        scratch_shapes=[
            pltpu.VMEM(square, bf16),
            pltpu.VMEM(square, bf16),
            pltpu.VMEM(square, f32),
            pltpu.VMEM(square, f32),
            pltpu.VMEM(square, f32),
        ],
        compiler_params=pltpu.CompilerParams(vmem_limit_bytes=62 << 20),
        cost_estimate=pl.CostEstimate(
            flops=12 * rows * width * tiles * units, bytes_accessed=60_000_000,
            transcendentals=rows * tiles * units,
        ),
        name="feed_forward",
    )(heads, tokens, cot, out_own, out, *vectors, own_up, own_down, weights, bias)


MESH_IDS = pl.DeviceIdType.MESH


def position():
    return lax.axis_index("pl"), lax.axis_index("core"), lax.axis_index("mp")


def plane_at(plane, offset):
    across, down = lax.rem(plane, 2), lax.div(plane, 2)
    if offset & 1:
        across = 1 - across
    if offset & 2:
        down = 1 - down
    return 2 * down + across


def greet(partners):
    barrier = pltpu.get_barrier_semaphore()
    for partner in partners:
        pl.semaphore_signal(barrier, inc=1, device_id=partner, device_id_type=MESH_IDS)
    pl.semaphore_wait(barrier, len(partners))


def column_partners():
    plane, core, zed = position()
    found = [(plane, core, lax.rem(zed + step, 4)) for step in range(1, 4)]
    return found + [(plane, 1 - core, lax.rem(zed + step, 4)) for step in range(4)]


def plane_partners():
    plane, core, zed = position()
    return [(plane_at(plane, offset), core, zed) for offset in range(1, 4)]


class Wires:
    def __init__(self, sends, recvs):
        self.sends, self.recvs, self.out = sends, recvs, []

    def copy(self, source, target, slot, device):
        return pltpu.make_async_remote_copy(
            src_ref=source,
            dst_ref=target,
            send_sem=self.sends.at[slot],
            recv_sem=self.recvs.at[slot],
            device_id=device,
            device_id_type=MESH_IDS,
        )

    def put(self, source, target, slot, device):
        copy = self.copy(source, target, slot, device)
        copy.start()
        self.out.append((copy, None))

    def put_unless(self, own, source, target, slot, device):
        copy = self.copy(source, target, slot, device)

        @pl.when(own)
        def _here():
            pltpu.make_async_copy(source, target, self.recvs.at[slot]).start()

        @pl.when(jnp.logical_not(own))
        def _there():
            copy.start()

        self.out.append((copy, own))

    def put_if(self, valid, source, target, slot, device):
        copy = self.copy(source, target, slot, device)
        pl.when(valid)(copy.start)
        self.out.append((copy, jnp.logical_not(valid)))

    def got(self, target, slot, device):
        self.copy(target, target, slot, device).wait_recv()

    def got_if(self, valid, target, slot, device):
        pl.when(valid)(self.copy(target, target, slot, device).wait_recv)

    def wait_sent(self, puts):
        gone = [id(put) for put in puts]
        self.out = [put for put in self.out if id(put) not in gone]
        for copy, own in puts:
            if own is None:
                copy.wait_send()
            else:
                pl.when(jnp.logical_not(own))(copy.wait_send)

    def finish(self):
        self.wait_sent(list(self.out))


ANYWHERE = pl.BlockSpec(memory_space=pl.ANY)


def visible_to(seg_col, seg_row, block):
    keys = (block + 1) * QB
    lanes = seg_row[:, block * QB : keys]
    cols = seg_col[:keys, :]
    same = jnp.concatenate([cols, cols], 1) == lanes
    rows = lax.broadcasted_iota(jnp.int32, (keys, QB), 0)
    places = lax.broadcasted_iota(jnp.int32, (keys, QB), 1) + block * QB
    return same & (rows <= places)


def forward_pair(slots, qkv, keys_pre, values_pre, seg_row, seg_col, heads, logs):
    seq = qkv.shape[0]
    keys = qkv[:, 128:256]
    values_t = jnp.transpose(qkv[:, 256:384])
    values_pre_t = jnp.transpose(values_pre)
    pre_row = lax.broadcasted_iota(jnp.int32, (keys_pre.shape[0], QB), 0)
    for block in range(seq // QB):
        extent = (block + 1) * QB
        here = slice(block * QB, extent)
        visible = visible_to(seg_col, seg_row, block)
        queries = qkv[here, :128] * 0.125
        parts = []
        for head in range(2):
            rows = slice(head * HEAD_DIM, (head + 1) * HEAD_DIM)
            query = half_mask(queries, head)
            s_tok = jnp.where(visible, nt(keys[:extent], query), MASKED)
            s_pre = jnp.where(pre_row < slots, nt(keys_pre, query), MASKED)
            top = jnp.maximum(
                jnp.max(s_tok, 0, keepdims=True), jnp.max(s_pre, 0, keepdims=True)
            )
            p_tok, p_pre = jnp.exp(s_tok - top), jnp.exp(s_pre - top)
            total = jnp.sum(p_tok, 0, keepdims=True) + jnp.sum(p_pre, 0, keepdims=True)
            mixed = nn(values_t[rows, :extent], p_tok.astype(jnp.bfloat16)) + nn(
                values_pre_t[rows], p_pre.astype(jnp.bfloat16)
            )
            parts.append(mixed * (1.0 / total))
            logs[head : head + 1, here] = top + jnp.log(total)
        heads[here, :] = jnp.transpose(jnp.concatenate(parts, 0)).astype(jnp.bfloat16)


PAIRS = 6


def front_kernel(
    slots,
    normed_ref, qkv_ref, bias_ref, table_ref, ids_ref, own_ref,
    rows_out, weight_out, qkv_out, heads_out, feed_out, proj_out,
    log_out, tab_out, seg_out, live_out, bias_out,
    sends, recvs, local,
    rows_v, weight_v, qkv_v, heads_v, log_v, biases_v, tables_v, ids_v, other_v, col_v, feed_v,
):
    plane, core, zed = position()
    parity = lax.rem(zed, 2)
    mine = 2 * parity + core
    origin = lax.div(zed, 2)
    sibling = (plane, 1 - core, zed)
    share = normed_ref.shape[1]
    seq = 4 * share
    around = [(plane_at(plane, offset), core, zed) for offset in range(4)]
    ahead = [lax.rem(zed + step, 4) for step in range(4)]
    greet(column_partners() + plane_partners())
    wires = Wires(sends, recvs)
    slot_at = {}

    def slot(*name):
        return slot_at.setdefault(name, len(slot_at))

    width = qkv_ref.shape[0] // 4

    def strip(at):
        return pl.ds(pl.multiple_of(at * width, 32), width)

    def rolled(z_from, z_at):
        return lax.rem(z_from + 2 * lax.rem(z_at, 2), 4)

    def apart(z_of, z_at):
        return lax.rem(z_of - z_at + 4, 4)

    own_copies = [
        pltpu.make_async_copy(qkv_ref, weight_v.at[rolled(zed, zed)], local.at[0]),
        pltpu.make_async_copy(bias_ref, biases_v.at[zed], local.at[1]),
        pltpu.make_async_copy(table_ref, tables_v.at[plane, core, zed], local.at[2]),
        pltpu.make_async_copy(ids_ref, ids_v, local.at[3]),
    ]
    for copy in own_copies:
        copy.start()
    wires.put(ids_ref, other_v, slot("ids"), sibling)

    sides = (1, -1)
    hops = [(sign, hop) for hop in range(1, 4) for sign in sides]

    def owner(sign, hop):
        at = zed - sign * hop
        return lax.rem(at + 4, 4), jnp.logical_and(at >= 0, at <= 3)

    def next_along(sign):
        at = zed + sign
        return lax.rem(at + 4, 4), jnp.logical_and(at >= 0, at <= 3)

    def early_parts(z_of, z_at):
        return (
            weight_v.at[rolled(z_of, z_at), strip(plane)],
            biases_v.at[z_of],
            tables_v.at[plane, core, z_of],
        )

    def late_part(at, core_at, z_of, z_at):
        return feed_v.at[at, core_at, apart(z_of, z_at) - 1]

    total = own_ref.shape[0]
    part_rows = feed_out.shape[3] // 2
    halves = (pl.ds(0, total // 2), pl.ds(total // 2, total // 2))
    routes = ((1, 2), (2, 1))

    def half_strip(at, half):
        return pl.ds(pl.multiple_of(at * width + half * (width // 2), 16), width // 2)

    def send_early(sign, hop):
        z_of, there_is = owner(sign, hop - 1)
        z_to, can = next_along(sign)
        valid = jnp.logical_and(there_is, can)
        sources, targets = early_parts(z_of, zed), early_parts(z_of, z_to)
        for kind in range(3):
            wires.put_if(
                valid, sources[kind], targets[kind], slot("e", sign, hop, kind), (plane, core, z_to)
            )

    def send_late(sign, hop):
        z_of, there_is = owner(sign, hop - 1)
        z_to, can = next_along(sign)
        valid = jnp.logical_and(there_is, can)
        source = own_ref if hop == 1 else late_part(plane, core, z_of, zed)
        wires.put_if(
            valid, source, late_part(plane, core, z_of, z_to), slot("l", sign, hop), (plane, core, z_to)
        )

    def take_early(sign, hop):
        z_of, valid = owner(sign, hop)
        back = (plane, core, lax.rem(zed + 4 - sign, 4))
        for kind, part in enumerate(early_parts(z_of, zed)):
            wires.got_if(valid, part, slot("e", sign, hop, kind), back)
        if hop < 3:
            send_early(sign, hop + 1)
        for half in range(2):
            part = weight_v.at[rolled(z_of, zed), half_strip(plane, half)]
            for offset in routes[half]:
                wires.put_if(valid, part, part, slot("ep", sign, hop, half, offset), around[offset])

    def early_across(sign, hop):
        z_of, valid = owner(sign, hop)
        for half, (came, goes) in enumerate(routes):
            part = weight_v.at[rolled(z_of, zed), half_strip(plane_at(plane, came), half)]
            wires.got_if(valid, part, slot("ep", sign, hop, half, came), around[came])
            wires.put_if(valid, part, part, slot("ep", sign, hop, half, 3), around[goes])

    def early_end(sign, hop):
        z_of, valid = owner(sign, hop)
        for half, (came, goes) in enumerate(routes):
            for offset, over in ((goes, goes), (3, goes)):
                part = weight_v.at[rolled(z_of, zed), half_strip(plane_at(plane, offset), half)]
                wires.got_if(valid, part, slot("ep", sign, hop, half, offset), around[over])

    def take_late(sign, hop):
        z_of, valid = owner(sign, hop)
        part = late_part(plane, core, z_of, zed)
        wires.got_if(valid, part, slot("l", sign, hop), (plane, core, lax.rem(zed + 4 - sign, 4)))
        if hop < 3:
            send_late(sign, hop + 1)
        for half in range(2):
            piece = part.at[halves[half]]
            for offset in routes[half]:
                wires.put_if(
                    valid, piece, piece, slot("lp", sign, hop, half, offset), around[offset]
                )
        wires.put_if(valid, part, part, slot("ls", sign, hop, 0), sibling)

    def take_across(sign, hop):
        z_of, valid = owner(sign, hop)
        for half, (came, goes) in enumerate(routes):
            piece = late_part(plane_at(plane, came), core, z_of, zed).at[halves[half]]
            wires.got_if(valid, piece, slot("lp", sign, hop, half, came), around[came])
            wires.put_if(valid, piece, piece, slot("lp", sign, hop, half, 3), around[goes])
        for half, (_, other) in enumerate(routes):
            piece = late_part(plane_at(plane, other), core, z_of, zed).at[halves[half]]
            wires.got_if(valid, piece, slot("lp", sign, hop, half, other), around[other])
        for offset in (1, 2):
            part = late_part(plane_at(plane, offset), core, z_of, zed)
            wires.put_if(valid, part, part, slot("ls", sign, hop, offset), sibling)

    def take_far(sign, hop):
        z_of, valid = owner(sign, hop)
        part = late_part(plane_at(plane, 3), core, z_of, zed)
        for half, (_, goes) in enumerate(routes):
            wires.got_if(
                valid, part.at[halves[half]], slot("lp", sign, hop, half, 3), around[goes]
            )
        wires.put_if(valid, part, part, slot("ls", sign, hop, 3), sibling)

    def end_across(sign, hop):
        z_of, valid = owner(sign, hop)
        for offset in range(4):
            part = late_part(plane_at(plane, offset), 1 - core, z_of, zed)
            wires.got_if(valid, part, slot("ls", sign, hop, offset), sibling)

    for copy in own_copies:
        copy.wait()
    for sign in sides:
        send_early(sign, 1)
    first_far = slot("nb", 0)
    slot("nb", 1)
    first_row = slot("n", 0)
    for step in range(1, 4):
        slot("n", step)
    outside = lax.div(zed, 2) != core
    near_home = jnp.logical_or(zed == 1, zed == 2)
    far_z = zed + 1 - 2 * parity
    first_over = slot("f", 0)
    for step in range(1, 4):
        slot("f", step)

    def send_rows(kind):
        for half in range(2):
            k = 2 * half + kind
            z_to = 2 * core + half
            own = jnp.logical_and(core == kind, z_to == zed)
            source, target = normed_ref.at[1 if kind else k], rows_v.at[kind, zed]
            number = first_row + lax.rem(k + 4 - zed, 4)

            @pl.when(own)
            def _here():
                pltpu.make_async_copy(source, target, recvs.at[number]).start()

            goes = jnp.logical_not(own)
            if kind:
                far_to = jnp.logical_or(z_to == 0, z_to == 3)
                goes = jnp.logical_and(goes, jnp.logical_not(jnp.logical_and(outside, far_to)))
            wires.put_if(goes, source, target, number, (plane, kind, z_to))

    def pass_rows(kind):
        here = core == kind
        for step in range(4):
            z_from = lax.rem(2 * parity + kind + 4 - step, 4)
            block = rows_v.at[kind, z_from]
            if kind:
                from_outside = jnp.logical_and(here, lax.div(z_from, 2) != origin)
                via = jnp.logical_and(from_outside, jnp.logical_not(near_home))
                far_number = first_far + lax.rem(z_from, 2)
                wires.got_if(via, block, far_number, sibling)
                wires.got_if(
                    jnp.logical_and(here, jnp.logical_not(via)), block, first_row + step, sibling
                )
                wires.put_if(
                    jnp.logical_and(from_outside, near_home),
                    block,
                    block,
                    far_number,
                    (plane, core, far_z),
                )
            else:
                wires.got_if(here, block, first_row + step, sibling)
            wires.put_if(here, block, block, first_over + step, sibling)

    def rows_passed(kind):
        for step in range(4):
            z_from = lax.rem(2 * parity + kind + 4 - step, 4)
            wires.got_if(core != kind, rows_v.at[kind, z_from], first_over + step, sibling)

    send_rows(0)
    for sign in sides:
        send_late(sign, 1)
    for hop in range(1, 4):
        for sign in sides:
            take_early(sign, hop)
    for sign in sides:
        take_late(sign, 1)
    for sign, hop in hops:
        early_across(sign, hop)
    pass_rows(0)
    send_rows(1)
    for offset in range(1, 4):
        wires.put(
            tables_v.at[plane, core], tables_v.at[plane, core], slot("tp", offset), around[offset]
        )
    for offset in range(1, 4):
        wires.got(tables_v.at[plane_at(plane, offset), core], slot("tp", offset), around[offset])
    wires.put(tables_v.at[:, core], tables_v.at[:, core], slot("ts"), sibling)

    wires.got(other_v, slot("ids"), sibling)
    wires.got(tables_v.at[:, 1 - core], slot("ts"), sibling)
    for row in range(2):
        at = 1 if row else 2 * parity
        here = jnp.where(origin == core, ids_v[at], other_v[at])
        seg = here[:, :seq]
        length = jnp.concatenate([here[:, seq:]] * (seq // 128), 1)
        live = (lax.broadcasted_iota(jnp.int32, (1, seq), 1) < length).astype(jnp.int32)
        seg_out[row] = seg
        live_out[row] = live
        line = jnp.where(live > 0, seg, -1).astype(jnp.float32)
        col_v[row] = jnp.transpose(jnp.broadcast_to(line, (128, seq)))
    for at in range(8):
        for step in range(4):
            bias_out[at, step : step + 1] = biases_v[ahead[step], 2, at : at + 1]
    for at in range(4):
        z_at = rolled(at, zed)
        for s in range(2):
            tab_out[at, :, 128 * s : 128 * s + 128] = jnp.concatenate(
                [tables_v[2 * core + t, s, z_at][:, :HEAD_DIM] for t in range(2)], 1
            )

    for sign, hop in hops:
        early_end(sign, hop)
    rows_passed(0)
    keep = [
        pltpu.make_async_copy(weight_v, weight_out, local.at[5]),
        pltpu.make_async_copy(rows_v, rows_out, local.at[4]),
    ]
    keep[0].start()

    def heads_copy(pair, step):
        z_to = lax.rem(mine + 4 - step, 4)
        own = jnp.logical_and(origin == core, z_to == zed)
        tokens = pl.ds(pl.multiple_of(z_to * share, share), share)
        on_b = lax.div(pair, 4)
        row = on_b + (1 - on_b) * 2 * parity
        target = heads_out.at[row, apart(rolled(lax.rem(pair, 4), zed), z_to), core]
        return own, heads_v.at[pair, tokens], target, (plane, origin, z_to)

    first_heads = slot("h", 0)
    for number in range(1, 4 * PAIRS):
        slot("h", number)

    def attend(pair):
        row, at = lax.div(pair, 4), lax.rem(pair, 4)
        z_at = rolled(at, zed)
        bias = jnp.concatenate([biases_v[z_at, core, j : j + 1] for j in range(3)], 1)
        for quarter in range(4):
            part = nt(rows_v[row, quarter], weight_v[at]) + bias
            qkv_v[pair, quarter * share : (quarter + 1) * share] = part.astype(jnp.bfloat16)
        forward_pair(
            slots,
            qkv_v.at[pair],
            tab_out[at, :, :128],
            tab_out[at, :, 128:],
            seg_out[row].astype(jnp.float32),
            col_v.at[row],
            heads_v.at[pair],
            log_v.at[pair],
        )
        for step in range(4):
            own, source, target, there = heads_copy(pair, step)
            number = first_heads + 4 * pair + step
            copy = wires.copy(source, target, number, there)

            @pl.when(own)
            def _here():
                pltpu.make_async_copy(source, target, recvs.at[number]).start()

            @pl.when(jnp.logical_not(own))
            def _there():
                copy.start()

    pl.loop(0, 2)(attend)
    for sign in sides:
        take_late(sign, 2)
    for sign in sides:
        take_across(sign, 1)
    pass_rows(1)
    pl.loop(2, 4)(attend)
    for sign in sides:
        take_late(sign, 3)
    for sign in sides:
        take_across(sign, 2)
    for sign in sides:
        take_far(sign, 1)
    rows_passed(1)
    keep[1].start()
    pl.loop(4, PAIRS)(attend)
    for sign in sides:
        take_across(sign, 3)
    for sign in sides:
        take_far(sign, 2)
    keep.append(pltpu.make_async_copy(qkv_v, qkv_out, local.at[6]))
    keep[-1].start()
    log_out[...] = log_v[...]
    for sign in sides:
        take_far(sign, 3)
    for at in range(2):
        if at:
            for sign, hop in hops:
                end_across(sign, hop)
        side = core if at == 0 else 1 - core
        keep.append(
            pltpu.make_async_copy(
                feed_v.at[:, side, :, : 2 * part_rows], feed_out.at[:, side], local.at[7 + at]
            )
        )
        keep[-1].start()
        for quarter in range(4):
            keep.append(
                pltpu.make_async_copy(
                    feed_v.at[quarter, side, :, 2 * part_rows :],
                    proj_out.at[:, side, quarter],
                    local.at[9 + 4 * at + quarter],
                )
            )
            keep[-1].start()
    for pair in range(PAIRS):
        for k in range(4):
            half, c = k // 2, k % 2
            step = lax.rem(k + 4 - zed, 4)
            row = 1 if pair >= 4 else 2 * half
            target = heads_out.at[row, apart((pair % 4 + 2 * half) % 4, zed), c]
            wires.got(target, first_heads + 4 * pair + step, (plane, c, 2 * core + half))
        for step in range(4):
            own, source, target, there = heads_copy(pair, step)
            copy = wires.copy(source, target, first_heads + 4 * pair + step, there)
            pl.when(jnp.logical_not(own))(copy.wait_send)
    for copy in keep:
        copy.wait()
    wires.finish()
    assert len(slot_at) == FRONT_COPIES, len(slot_at)


FRONT_COPIES = 159


def front(slots, normed, qkv, bias, table, ids, own):
    bf16, f32 = jnp.bfloat16, jnp.float32
    _, share, width = normed.shape
    seq = 4 * share
    vmem = pl.BlockSpec(memory_space=pltpu.VMEM)
    shaped = jax.ShapeDtypeStruct
    return pl.pallas_call(
        functools.partial(front_kernel, slots),
        in_specs=[ANYWHERE] * 6,
        out_specs=[ANYWHERE] * 6 + [vmem] * 5,
        out_shape=[
            shaped((2, 4, share, width), bf16),
            shaped((4, 384, width), bf16),
            shaped((PAIRS, seq, 384), bf16),
            shaped((3, 4, 2, share, 128), bf16),
            shaped((4, 2, 3, 256, width), bf16),
            shaped((3, 2, 4, 32, width), bf16),
            shaped((PAIRS, 2, seq), f32),
            shaped((4, 16, 256), bf16),
            shaped((2, 1, seq), jnp.int32),
            shaped((2, 1, seq), jnp.int32),
            shaped((8, 4, 128), f32),
        ],
        scratch_shapes=[
            pltpu.SemaphoreType.DMA((FRONT_COPIES,)),
            pltpu.SemaphoreType.DMA((FRONT_COPIES,)),
            pltpu.SemaphoreType.DMA((17,)),
            pltpu.VMEM((2, 4, share, width), bf16),
            pltpu.VMEM((4, 384, width), bf16),
            pltpu.VMEM((PAIRS, seq, 384), bf16),
            pltpu.VMEM((PAIRS, seq, 128), bf16),
            pltpu.VMEM((PAIRS, 2, seq), f32),
            pltpu.VMEM((4, 3, 8, 128), f32),
            pltpu.VMEM((4, 2, 4, 16, 128), bf16),
            pltpu.VMEM(ids.shape, jnp.int32),
            pltpu.VMEM(ids.shape, jnp.int32),
            pltpu.VMEM((2, seq, 128), f32),
            pltpu.VMEM((4, 2, 3, own.shape[0], width), bf16),
        ],
        compiler_params=pltpu.CompilerParams(
            collective_id=0, has_side_effects=True, vmem_limit_bytes=48 << 20
        ),
        cost_estimate=pl.CostEstimate(
            flops=40_000_000_000, bytes_accessed=60 << 20, transcendentals=8_000_000
        ),
        name="front",
    )(normed, qkv, bias, table, ids, own)


def backward_pair(
    slots, qkv, keys_pre, values_pre, seg_row, seg_col, grads_in, logs, dtab, dbias, dk_acc, dv_acc
):
    seq = qkv.shape[0]
    keys, values = qkv[:, 128:256], qkv[:, 256:384]
    keys_t = jnp.transpose(keys)
    keys_pre_t = jnp.transpose(keys_pre)
    pre_row = lax.broadcasted_iota(jnp.int32, (keys_pre.shape[0], QB), 0)
    zero = jnp.zeros((keys_pre.shape[0], 128), jnp.float32)
    dtab_k, dtab_v, dq_sum = zero, zero, jnp.zeros((1, 128), jnp.float32)
    for block in reversed(range(seq // QB)):
        extent = (block + 1) * QB
        here = slice(block * QB, extent)
        visible = visible_to(seg_col, seg_row, block)
        queries = qkv[here, :128] * 0.125
        grads = grads_in[here, :]
        weights, dscores, weights_pre, dscores_pre, query_halves, grad_halves, dq_parts = (
            [], [], [], [], [], [], [],
        )
        for head in range(2):
            rows = slice(head * HEAD_DIM, (head + 1) * HEAD_DIM)
            query, grad = half_mask(queries, head), half_mask(grads, head)
            log_total = logs[head : head + 1, here]
            s_tok = jnp.where(visible, nt(keys[:extent], query), MASKED)
            s_pre = jnp.where(pre_row < slots, nt(keys_pre, query), MASKED)
            w_tok, w_pre = jnp.exp(s_tok - log_total), jnp.exp(s_pre - log_total)
            dp_tok, dp_pre = nt(values[:extent], grad), nt(values_pre, grad)
            delta = jnp.sum(w_tok * dp_tok, 0, keepdims=True) + jnp.sum(
                w_pre * dp_pre, 0, keepdims=True
            )
            ds_tok = (w_tok * (dp_tok - delta)).astype(jnp.bfloat16)
            ds_pre = (w_pre * (dp_pre - delta)).astype(jnp.bfloat16)
            dq_parts.append(nn(keys_t[rows, :extent], ds_tok) + nn(keys_pre_t[rows], ds_pre))
            weights.append(w_tok.astype(jnp.bfloat16))
            weights_pre.append(w_pre.astype(jnp.bfloat16))
            dscores.append(ds_tok)
            dscores_pre.append(ds_pre)
            query_halves.append(query)
            grad_halves.append(grad)
        query_both = jnp.concatenate(query_halves, 0)
        grad_both = jnp.concatenate(grad_halves, 0)
        dv = nn(jnp.concatenate(weights, 1), grad_both)
        dk = nn(jnp.concatenate(dscores, 1), query_both)
        if block == seq // QB - 1:
            dv_acc[...] = dv
            dk_acc[...] = dk
        else:
            dv_acc[:extent] += dv
            dk_acc[:extent] += dk
        dtab_v = dtab_v + nn(jnp.concatenate(weights_pre, 1), grad_both)
        dtab_k = dtab_k + nn(jnp.concatenate(dscores_pre, 1), query_both)
        dq = jnp.transpose(jnp.concatenate(dq_parts, 0)) * 0.125
        dq_sum = dq_sum + jnp.sum(dq, 0, keepdims=True)
        qkv[here, :128] = dq.astype(jnp.bfloat16)
    dk, dv = dk_acc[...], dv_acc[...]
    qkv[:, 128:256] = dk.astype(jnp.bfloat16)
    qkv[:, 256:384] = dv.astype(jnp.bfloat16)
    dbias[...] = jnp.concatenate(
        [dq_sum, jnp.sum(dk, 0, keepdims=True), jnp.sum(dv, 0, keepdims=True)], 1
    )
    dtab[:, :128] = dtab_k
    dtab[:, 128:] = dtab_v


def add_up(rows, target, *sources):
    chunk = 96 if rows % 96 == 0 else 64

    @pl.loop(0, rows // chunk)
    def _add(at):
        span = pl.ds(pl.multiple_of(at * chunk, 32), chunk)
        if len(sources) == 2:
            target[span] = sources[0][span] + sources[1][span]
            return
        value = sources[0][span].astype(jnp.float32)
        for source in sources[1:]:
            value = value + source[span].astype(jnp.float32)
        target[span] = value.astype(jnp.bfloat16)


def back_kernel(
    slots,
    heads_ref, feed_ref, proj_ref, qkv_ref, rows_ref, weight_ref,
    log_ref, tab_ref, seg_ref, live_ref, upb_ref, norms_ref, tokens_ref, rout_ref,
    full_out, back_out, first_out, second_out,
    sends, recvs, local,
    dh_v, sib_v, own_v, plane_v, sum_v, z_v, gq_v, plane_q, sum_q, z_q, done_v,
    qkv_v, weight_v, df_v, dfs_v, col_v, dk_acc, dv_acc,
    dtab_v, dbias_v, back_v, first_v, first_in, second_v, second_in, dfm_v,
):
    plane, core, zed = position()
    parity = lax.rem(zed, 2)
    mine = 2 * parity + core
    origin = lax.div(zed, 2)
    sibling = (plane, 1 - core, zed)
    share = heads_ref.shape[3]
    seq = 4 * share
    feed_rows, proj_rows = feed_ref.shape[3], proj_ref.shape[3]
    both = feed_rows + proj_rows
    q_rows = gq_v.shape[2]
    around = [(plane_at(plane, offset), core, zed) for offset in range(4)]
    ahead = [lax.rem(zed + step, 4) for step in range(4)]
    greet(column_partners() + plane_partners())
    wires = Wires(sends, recvs)
    slot_at = {}

    def slot(*name):
        return slot_at.setdefault(name, len(slot_at))

    tokens = pl.ds(pl.multiple_of(zed * share, share), share)
    first_heads = slot("h", 0)
    for number in range(1, 4 * PAIRS):
        slot("h", number)
    for pair in range(PAIRS):
        for step in range(4):
            k = ahead[step]
            half, c = lax.div(k, 2), lax.rem(k, 2)
            z_to = 2 * core + half
            own = jnp.logical_and(c == core, z_to == zed)
            row = 1 if pair >= 4 else 2 * half
            wires.put_unless(
                own,
                heads_ref.at[row, lax.rem(pair % 4 + 2 * half + 4 - zed, 4), c],
                dh_v.at[pair, tokens],
                first_heads + 4 * pair + step,
                (plane, c, z_to),
            )
    turns = [lax.rem(zed + 1 + turn, 4) for turn in range(4)]
    own_copies = []
    for turn in range(4):
        z_at = (turn + 1) % 4
        wires.put(
            feed_ref.at[:, 1 - core, z_at], sib_v.at[turn, :, :feed_rows], slot("s", turn), sibling
        )
        wires.put(
            proj_ref.at[z_at, 1 - core], sib_v.at[turn, :, feed_rows:], slot("sp", turn), sibling
        )
        own_copies.append(
            [
                pltpu.make_async_copy(
                    feed_ref.at[:, core, z_at],
                    own_v.at[turn % 2, :, :feed_rows],
                    local.at[2 * (turn % 2)],
                ),
                pltpu.make_async_copy(
                    proj_ref.at[z_at, core],
                    own_v.at[turn % 2, :, feed_rows:],
                    local.at[2 * (turn % 2) + 1],
                ),
            ]
        )
    later = [
        pltpu.make_async_copy(qkv_ref, qkv_v, local.at[4]),
        pltpu.make_async_copy(weight_ref, weight_v, local.at[5]),
    ]
    for copy in own_copies[0] + own_copies[1] + later:
        copy.start()
    for row in range(2):
        line = jnp.where(live_ref[row] > 0, seg_ref[row], -1).astype(jnp.float32)
        col_v[row] = jnp.transpose(jnp.broadcast_to(line, (128, seq)))

    def chip_sum(turn):
        for copy in own_copies[turn]:
            copy.wait()
        wires.got(sib_v.at[turn, :, :feed_rows], slot("s", turn), sibling)
        wires.got(sib_v.at[turn, :, feed_rows:], slot("sp", turn), sibling)
        for at in range(4):
            add_up(both, sib_v.at[turn, at], sib_v.at[turn, at], own_v.at[turn % 2, at])
        if turn < 2:
            for copy in own_copies[turn + 2]:
                copy.start()
        first, _ = axes(turn)
        for kind, offset in enumerate((3, first)):
            wires.put(
                sib_v.at[turn, plane_at(plane, offset)],
                plane_v.at[kind, turn],
                slot("p", turn, kind),
                around[first],
            )

    def axes(turn):
        return (1, 2) if turn % 2 else (2, 1)

    def merge(turn):
        first, other = axes(turn)
        wires.got(plane_v.at[0, turn], slot("p", turn, 0), around[first])
        target = sib_v.at[turn, plane_at(plane, other)]
        add_up(both, target, target, plane_v.at[0, turn])
        wires.put(target, plane_v.at[2, turn], slot("p", turn, 2), around[other])

    chip_sum(0)
    chip_sum(1)
    for copy in later:
        copy.wait()

    def heads_here(pairs):
        for pair in pairs:
            for step in range(4):
                z_from = lax.rem(mine + 4 - step, 4)
                there = pl.ds(pl.multiple_of(z_from * share, share), share)
                wires.got(dh_v.at[pair, there], first_heads + 4 * pair + step, sibling)

    def attend(pair):
        row, at = lax.div(pair, 4), lax.rem(pair, 4)
        backward_pair(
            slots,
            qkv_v.at[pair],
            tab_ref[at, :, :128],
            tab_ref[at, :, 128:],
            seg_ref[row].astype(jnp.float32),
            col_v.at[row],
            dh_v.at[pair],
            log_ref.at[pair],
            dtab_v.at[pair],
            dbias_v.at[pair],
            dk_acc,
            dv_acc,
        )

    def plane_sum(turn):
        for kind, offset in zip((1, 2), axes(turn)):
            wires.got(plane_v.at[kind, turn], slot("p", turn, kind), around[offset])
        add_up(
            both, sum_v.at[turn], sib_v.at[turn, plane], *[plane_v.at[j, turn] for j in (1, 2)]
        )
        if turn < 3:
            wires.put(
                sum_v.at[turn], z_v.at[turn], slot("z", turn), (plane, core, turns[turn])
            )

    low = lax.rem(zed, 2)
    partners = [
        sibling, around[1], around[2],
        (plane, core, zed + 1 - 2 * low), (plane, core, ahead[2]),
    ]

    def small_send(name, values, arrived, step):
        source = arrived.at[step - 1] if step else values.at[0]
        wires.put(source, arrived.at[step], slot(name, step), partners[step])

    def small_take(name, values, arrived, step):
        wires.got(arrived.at[step], slot(name, step), partners[step])
        arrived[step] = arrived[step] + (arrived[step - 1] if step else values[0])
        if step < 4:
            small_send(name, values, arrived, step + 1)

    def first_sums():
        first_v[0] = jnp.zeros(first_v.shape[1:], jnp.float32)
        for at in range(8):
            for step in range(4):
                line = upb_ref[at, :, 128 * step : 128 * step + 128]
                first_v[0, pl.ds(4 * at + ahead[step], 1)] = line
        for at in range(4):
            for j in range(8):
                line = norms_ref[at : at + 1, 128 * j : 128 * j + 128]
                first_v[0, 32 + 8 * at + j : 33 + 8 * at + j] = line
        for at in range(4):
            entry = core * 4 + lax.rem(at + 2 * parity, 4)
            table, bias = dtab_v[at], dbias_v[at]
            if at < 2:
                table, bias = table + dtab_v[4 + at], bias + dbias_v[4 + at]
            base = pl.multiple_of(64 + 32 * entry, 8)
            first_v[0, pl.ds(base, 16)] = table[:, :128]
            first_v[0, pl.ds(base + 16, 16)] = table[:, 128:]
            base = pl.multiple_of(320 + 8 * entry, 8)
            first_v[0, pl.ds(base, 8)] = jnp.concatenate(
                [bias[:, :128], bias[:, 128:256], bias[:, 256:], jnp.zeros((5, 128), jnp.float32)], 0
            )
        small_send("a", first_v, first_in, 0)

    def tanh_part():
        entry = lax.div(plane, 2) * 4 + zed
        base = pl.multiple_of(64 + 32 * entry + 16 * core, 8)
        table = first_in[4, pl.ds(base, 16)]
        table = jnp.where(lax.rem(plane, 2) == 0, table[:, :HEAD_DIM], table[:, HEAD_DIM:])
        part = lax.dot_general(
            table,
            rout_ref[...].astype(jnp.float32),
            (((1,), (1,)), ((), ())),
            preferred_element_type=jnp.float32,
            precision=HIGHEST,
        )
        for j in range(4):
            second_v[0, 16 * j : 16 * j + 16] = part[:, 128 * j : 128 * j + 128]

    def norm_sums():
        span_rows = 64

        def body(at, sums):
            row, part = lax.div(at, share // span_rows), lax.rem(at, share // span_rows)
            span = pl.ds(pl.multiple_of(part * span_rows, span_rows), span_rows)
            grad = back_v[row, span].astype(jnp.float32)
            extra = back_v[3, span].astype(jnp.float32)
            grad = grad + jnp.where(row == 1, extra, 0.0)
            hat, _ = normalize(tokens_ref[row, span].astype(jnp.float32))
            return (
                sums[0] + jnp.sum(grad * hat, 0, keepdims=True),
                sums[1] + jnp.sum(grad, 0, keepdims=True),
            )

        zero = jnp.zeros((1, back_v.shape[2]), jnp.float32)
        sums = lax.fori_loop(0, 3 * (share // span_rows), body, (zero, zero))
        for kind in range(2):
            for j in range(8):
                at = 64 + 8 * kind + j
                second_v[0, at : at + 1] = sums[kind][:, 128 * j : 128 * j + 128]
        small_send("b", second_v, second_in, 0)

    first_row = slot("r", 0)
    for number in range(1, 4):
        slot("r", number)

    far_home = jnp.logical_or(zed == 0, zed == 3)
    other_home = zed + 1 - 2 * parity
    outside = lax.div(zed, 2) != core
    far_place = 1 + 2 * core

    @pl.when(outside)
    def _nothing():
        back_v[far_place] = jnp.zeros(back_v.shape[1:], jnp.bfloat16)

    def row_grads(kind):
        for quarter in range(4):
            span = slice(quarter * share, (quarter + 1) * share)
            parts = [
                nn(qkv_v[4 * kind + at, span], weight_v[at]) for at in range(2 if kind else 4)
            ]
            total = parts[0] + parts[1]
            for part in parts[2:]:
                total = total + part
            df_v[kind, quarter] = total.astype(jnp.bfloat16)
            wires.put_if(
                core != kind, df_v.at[kind, quarter], dfs_v.at[quarter], slot("df", quarter, kind),
                sibling,
            )

    def send_rows(kind):
        here = core == kind
        for quarter in range(4):
            wires.got_if(here, dfs_v.at[quarter], slot("df", quarter, kind), sibling)

            @pl.when(here)
            def _sum():
                add_up(share, dfs_v.at[quarter], dfs_v.at[quarter], df_v.at[kind, quarter])

        if kind:
            for j in range(2):
                z_out = 2 - 2 * origin + j
                wires.put_if(
                    jnp.logical_and(here, far_home), dfs_v.at[z_out], dfm_v.at[j], slot("m", j),
                    (plane, core, other_home),
                )
                joins = jnp.logical_and(here, jnp.logical_not(far_home))
                wires.got_if(joins, dfm_v.at[j], slot("m", j), (plane, core, other_home))

                @pl.when(joins)
                def _join():
                    add_up(share, dfs_v.at[z_out], dfs_v.at[z_out], dfm_v.at[j])

        for step in range(4):
            z_to = lax.rem(2 * parity + kind + 4 - step, 4)
            own = jnp.logical_and(origin == core, z_to == zed)
            goes = here
            if kind:
                beyond = jnp.logical_and(far_home, lax.div(z_to, 2) != origin)
                goes = jnp.logical_and(here, jnp.logical_not(beyond))
            source, target = dfs_v.at[z_to], back_v.at[2 * parity + kind]

            @pl.when(jnp.logical_and(here, own))
            def _here():
                pltpu.make_async_copy(source, target, recvs.at[first_row + step]).start()

            wires.put_if(
                jnp.logical_and(goes, jnp.logical_not(own)),
                source,
                target,
                first_row + step,
                (plane, origin, z_to),
            )

    heads_here((0, 1))
    pl.loop(0, 2)(attend)
    chip_sum(2)
    merge(0)
    heads_here((2, 3))
    pl.loop(2, 4)(attend)
    chip_sum(3)
    merge(1)
    rows_v = own_v
    row_copy = pltpu.make_async_copy(rows_ref, rows_v.at[:, :, :share], local.at[0])
    row_copy.start()
    plane_sum(0)
    row_grads(0)
    merge(2)
    heads_here((4, 5))
    pl.loop(4, PAIRS)(attend)
    merge(3)
    plane_sum(1)
    first_sums()
    send_rows(0)
    row_grads(1)
    plane_sum(2)
    small_take("a", first_v, first_in, 0)
    row_copy.wait()
    rows_a = jnp.concatenate([rows_v[0, j, :share] for j in range(4)], 0)
    for at in range(4):
        grad = outer_sum(qkv_v[at], rows_a)
        if at < 2:
            grad = grad + outer_sum(
                qkv_v[4 + at], jnp.concatenate([rows_v[1, j, :share] for j in range(4)], 0)
            )
        grad = grad.astype(jnp.bfloat16)
        for j in range(4):
            gq_v[at, j] = grad[j * q_rows : (j + 1) * q_rows]
        if at % 2:
            sub = at // 2
            slots_here = slice(at - 1, at + 1)
            first, _ = axes(sub)
            for kind, offset in enumerate((3, first)):
                wires.put(
                    gq_v.at[slots_here, plane_at(plane, offset)],
                    plane_q.at[kind, slots_here],
                    slot("pq", sub, kind),
                    around[first],
                )
    small_take("a", first_v, first_in, 1)
    send_rows(1)
    plane_sum(3)
    small_take("a", first_v, first_in, 2)
    for sub in range(2):
        first, other = axes(sub)
        slots_here = slice(2 * sub, 2 * sub + 2)
        wires.got(plane_q.at[0, slots_here], slot("pq", sub, 0), around[first])
        at_other = plane_at(plane, other)
        for at in (2 * sub, 2 * sub + 1):
            target = gq_v.at[at, at_other]
            add_up(q_rows, target, target, plane_q.at[0, at])
        wires.put(
            gq_v.at[slots_here, at_other], plane_q.at[2, slots_here], slot("pq", sub, 2), around[other]
        )
    small_take("a", first_v, first_in, 3)

    def spread(name, span_of):
        copy = pltpu.make_async_copy(
            done_v.at[span_of(2)],
            full_out.at[plane, core, span_of(2)],
            local.at[6 if name == "f" else 7],
        )
        copy.start()
        for half in range(2):
            for offset in (1, 2) if half == 0 else (2, 1):
                wires.put(
                    done_v.at[span_of(half)],
                    full_out.at[plane, core, span_of(half)],
                    slot(name, half, offset),
                    around[offset],
                )
        wires.put(
            done_v.at[span_of(2)], full_out.at[plane, core, span_of(2)], slot(name, 2, 0), sibling
        )
        return copy

    def spread_on(name, span_of):
        for half in range(2):
            came, goes = (1, 2) if half == 0 else (2, 1)
            piece = full_out.at[plane_at(plane, came), core, span_of(half)]
            wires.got(piece, slot(name, half, came), around[came])
            wires.put(piece, piece, slot(name, half, 3), around[goes])
        for half in range(2):
            came = 2 if half == 0 else 1
            piece = full_out.at[plane_at(plane, came), core, span_of(half)]
            wires.got(piece, slot(name, half, came), around[came])
        for offset in (1, 2):
            piece = full_out.at[plane_at(plane, offset), core, span_of(2)]
            wires.put(piece, piece, slot(name, 2, offset), sibling)

    def spread_far(name, span_of):
        for half in range(2):
            piece = full_out.at[plane_at(plane, 3), core, span_of(half)]
            wires.got(piece, slot(name, half, 3), around[2 if half == 0 else 1])
        piece = full_out.at[plane_at(plane, 3), core, span_of(2)]
        wires.put(piece, piece, slot(name, 2, 3), sibling)

    def spread_end(name, span_of):
        for offset in range(4):
            wires.got(
                full_out.at[plane_at(plane, offset), 1 - core, span_of(2)],
                slot(name, 2, offset),
                sibling,
            )

    def feed_span(half):
        return (pl.ds(0, both // 2), pl.ds(both // 2, both // 2), pl.ds(0, both))[half]

    def q_span(half):
        return (
            pl.ds(both, q_rows // 2), pl.ds(both + q_rows // 2, q_rows // 2), pl.ds(both, q_rows)
        )[half]

    for turn in range(3):
        wires.got(z_v.at[turn], slot("z", turn), (plane, core, lax.rem(zed + 3 - turn, 4)))
    add_up(both, done_v.at[feed_span(2)], sum_v.at[3], *[z_v.at[j] for j in range(3)])
    last = [spread("f", feed_span)]
    small_take("a", first_v, first_in, 4)
    tanh_part()
    for sub in range(2):
        slots_here = slice(2 * sub, 2 * sub + 2)
        for kind, offset in zip((1, 2), axes(sub)):
            wires.got(plane_q.at[kind, slots_here], slot("pq", sub, kind), around[offset])
        for at in (2 * sub, 2 * sub + 1):
            add_up(q_rows, sum_q.at[at], gq_v.at[at, plane], *[plane_q.at[j, at] for j in (1, 2)])
    for turn in range(3):
        wires.put(
            sum_q.at[lax.rem(turns[turn] + 2 * parity, 4)],
            z_q.at[turn],
            slot("zq", turn),
            (plane, core, turns[turn]),
        )
    spread_on("f", feed_span)
    for k in range(4):
        wires.got_if(
            jnp.logical_not(jnp.logical_and(outside, far_place == k)),
            back_v.at[k],
            first_row + lax.rem(k + 4 - zed, 4),
            (plane, k % 2, 2 * core + k // 2),
        )
    last.append(pltpu.make_async_copy(back_v, back_out, local.at[8]))
    last[-1].start()
    norm_sums()
    for turn in range(3):
        wires.got(z_q.at[turn], slot("zq", turn), (plane, core, lax.rem(zed + 3 - turn, 4)))
    add_up(
        q_rows,
        done_v.at[q_span(2)],
        sum_q.at[lax.rem(zed + 2 * parity, 4)],
        *[z_q.at[j] for j in range(3)],
    )
    last.append(spread("q", q_span))
    small_take("b", second_v, second_in, 0)
    spread_far("f", feed_span)
    small_take("b", second_v, second_in, 1)
    spread_on("q", q_span)
    small_take("b", second_v, second_in, 2)
    spread_far("q", q_span)
    small_take("b", second_v, second_in, 3)
    small_take("b", second_v, second_in, 4)
    first_out[...] = first_in[4]
    second_out[...] = second_in[4]
    spread_end("f", feed_span)
    spread_end("q", q_span)
    for copy in last:
        copy.wait()
    wires.finish()
    assert len(slot_at) == BACK_COPIES, len(slot_at)


BACK_COPIES = 100


def back(
    slots, d_heads, grad_feed, grad_out, qkv, rows, weights, logs, tab, seg, live, upb, norms, tokens, rout
):
    bf16, f32 = jnp.bfloat16, jnp.float32
    share, width = rows.shape[2:]
    seq = 4 * share
    vmem = pl.BlockSpec(memory_space=pltpu.VMEM)
    shaped, held = jax.ShapeDtypeStruct, pltpu.VMEM
    both, q_rows = grad_feed.shape[3] + grad_out.shape[3], 96
    return pl.pallas_call(
        functools.partial(back_kernel, slots),
        in_specs=[ANYWHERE] * 6 + [vmem] * 8,
        out_specs=[ANYWHERE] * 2 + [vmem] * 2,
        out_shape=[
            shaped((4, 2, both + q_rows, width), bf16),
            shaped((4, share, width), bf16),
            shaped((384, 128), f32),
            shaped((80, 128), f32),
        ],
        scratch_shapes=[
            pltpu.SemaphoreType.DMA((BACK_COPIES,)),
            pltpu.SemaphoreType.DMA((BACK_COPIES,)),
            pltpu.SemaphoreType.DMA((9,)),
            held((PAIRS, seq, 128), bf16),
            held((4, 4, both, width), bf16),
            held((2, 4, both, width), bf16),
            held((3, 4, both, width), bf16),
            held((4, both, width), bf16),
            held((3, both, width), bf16),
            held((4, 4, q_rows, width), bf16),
            held((3, 4, q_rows, width), bf16),
            held((4, q_rows, width), bf16),
            held((3, q_rows, width), bf16),
            held((both + q_rows, width), bf16),
            held((PAIRS, seq, 384), bf16),
            held((4, 384, width), bf16),
            held((2, 4, share, width), bf16),
            held((4, share, width), bf16),
            held((2, seq, 128), f32),
            held((seq, 128), f32),
            held((seq, 128), f32),
            held((PAIRS, 16, 256), f32),
            held((PAIRS, 1, 384), f32),
            held((4, share, width), bf16),
            held((1, 384, 128), f32),
            held((5, 384, 128), f32),
            held((1, 80, 128), f32),
            held((5, 80, 128), f32),
            held((2, share, width), bf16),
        ],
        compiler_params=pltpu.CompilerParams(
            collective_id=2, has_side_effects=True, vmem_limit_bytes=62 << 20
        ),
        cost_estimate=pl.CostEstimate(
            flops=80_000_000_000, bytes_accessed=60 << 20, transcendentals=8_000_000
        ),
        name="back",
    )(
        d_heads, grad_feed, grad_out, qkv, rows, weights, logs, tab, seg, live, upb, norms, tokens, rout
    )


def write_feed_kernel(piece_ref, up_ref, down_ref):
    for c in range(2):
        span = slice(128 * c, 128 * c + 128)
        up_ref[:, span] = jnp.transpose(piece_ref[0, c, :128].astype(jnp.float32))
        down_ref[span] = piece_ref[0, c, 128:].astype(jnp.float32)


def write_rest_kernel(piece_ref, grad_ref, out_ref):
    for at in range(4):
        out_ref[32 * at : 32 * at + 32] = piece_ref[at, 0, :32].astype(jnp.float32)
    turned = [jnp.transpose(piece_ref[at, 0, 32:].astype(jnp.float32)) for at in range(4)]
    turned = jnp.concatenate(turned, 1)
    order = [(kind, head) for head in range(2) for kind in range(3)]
    grad_ref[...] = jnp.concatenate(
        [turned[:, 128 * kind + 64 * head : 128 * kind + 64 * head + 64] for kind, head in order], 1
    )


def last_kernel(came_ref, tokens_ref, resid_ref, gain_ref, grad_ref):
    row = pl.program_id(0)
    grad = came_ref[row].astype(jnp.float32) + jnp.where(
        row == 1, came_ref[3].astype(jnp.float32), 0.0
    )
    hat, inverse = normalize(tokens_ref[0].astype(jnp.float32))
    grad_ref[0] = resid_ref[0] + norm_back(grad, hat, inverse, gain_ref[...])


def last_norm(came, tokens, d_resid, gain):
    rows = pl.BlockSpec((1, *tokens.shape[1:]), lambda m: (m, 0, 0))
    return pl.pallas_call(
        last_kernel,
        grid=(tokens.shape[0],),
        in_specs=[
            pl.BlockSpec(came.shape, lambda m: (0, 0, 0)),
            rows,
            rows,
            pl.BlockSpec((1, tokens.shape[2]), lambda m: (0, 0)),
        ],
        out_specs=rows,
        out_shape=jax.ShapeDtypeStruct(tokens.shape, jnp.float32),
        compiler_params=pltpu.CompilerParams(vmem_limit_bytes=32 << 20),
        name="last_norm",
    )(came, tokens, d_resid, gain)


def write_grads(full):
    f32 = jnp.float32
    width = full.shape[3]
    up, down = pl.pallas_call(
        write_feed_kernel,
        grid=(4,),
        in_specs=[pl.BlockSpec((1, 2, 256, width), lambda p: (p, 0, 0, 0))],
        out_specs=[
            pl.BlockSpec((width, 256), lambda p: (0, p)),
            pl.BlockSpec((256, width), lambda p: (p, 0)),
        ],
        out_shape=[
            jax.ShapeDtypeStruct((width, 1024), f32),
            jax.ShapeDtypeStruct((1024, width), f32),
        ],
        name="write_feed",
    )(full)
    qkv, out = pl.pallas_call(
        write_rest_kernel,
        grid=(2,),
        in_specs=[pl.BlockSpec((4, 1, 128, width), lambda c: (0, c, 2, 0))],
        out_specs=[
            pl.BlockSpec((width, 384), lambda c: (0, c)),
            pl.BlockSpec((128, width), lambda c: (c, 0)),
        ],
        out_shape=[
            jax.ShapeDtypeStruct((width, 768), f32),
            jax.ShapeDtypeStruct((256, width), f32),
        ],
        compiler_params=pltpu.CompilerParams(vmem_limit_bytes=40 << 20),
        name="write_rest",
    )(full)
    return up, down, out, qkv


def per_device_fast(
    tokens,
    segment_ids,
    row_lengths,
    ln1_gain,
    ln1_bias,
    qkv_weight,
    qkv_bias,
    out_weight,
    out_bias,
    ln2_gain,
    ln2_bias,
    up_weight,
    up_bias,
    down_weight,
    down_bias,
    prefix_embed,
    reparam_in,
    reparam_in_bias,
    reparam_out,
    reparam_out_bias,
    cotangent,
):
    bf16, f32 = jnp.bfloat16, jnp.float32
    plane, core, zed = lax.axis_index("pl"), lax.axis_index("core"), lax.axis_index("mp")
    micro, share, width = tokens.shape
    seq = segment_ids.shape[1]
    slots = prefix_embed.shape[0]

    def pick(stack, index):
        return lax.dynamic_index_in_dim(stack, index, 0, keepdims=False)

    pre_act = nn(prefix_embed, reparam_in) + reparam_in_bias
    tanh_hidden = jnp.tanh(pre_act)
    tanh_low = tanh_hidden.astype(bf16)
    table_part = (nn(tanh_low, reparam_out) + reparam_out_bias).astype(bf16)
    table_part = jnp.pad(table_part, ((0, 16 - slots), (0, 128 - HEAD_DIM)))
    packed_ids = jnp.concatenate(
        [segment_ids, jnp.broadcast_to(row_lengths[:, :1], (micro, 128))], 1
    )
    packed_ids = jnp.pad(packed_ids, ((0, 8 - micro), (0, 0)))[:, None]
    packed_bias = jnp.concatenate(
        [
            jnp.pad(
                qkv_bias.reshape(2, 2, 3, HEAD_DIM).transpose(0, 2, 1, 3).reshape(2, 3, 128),
                ((0, 0), (0, 5), (0, 0)),
            ),
            up_bias.reshape(1, 8, 128),
        ]
    )
    x_share = tokens.astype(f32)
    hat_first, inverse_first = normalize(x_share)
    normed_first = (hat_first * ln1_gain + ln1_bias).astype(bf16)
    qkv_half = lax.dynamic_index_in_dim(
        qkv_weight.reshape(width, 2, 2, 3, HEAD_DIM), core, 1, keepdims=False
    )
    qkv_half = qkv_half.transpose(2, 1, 3, 0).reshape(384, width)
    down_own = down_weight.reshape(8, 128, width)
    (
        normed_home, qkv_full, qkv, heads_rows, feed_full, out_full, logs, tab, seg, live, biases
    ) = front(
        slots,
        normed_first,
        qkv_half,
        packed_bias,
        table_part,
        packed_ids,
        jnp.concatenate(
            [
                lax.dynamic_slice_in_dim(up_weight, (2 * plane + core) * 128, 128, 1).T,
                pick(down_own, 2 * plane + core),
                lax.dynamic_slice_in_dim(out_weight, core * 128 + plane * 32, 32, 0),
            ]
        ),
    )
    up_bias_all = biases.reshape(8, 1, 512)
    block_out, d_resid, d_heads, grad_out, sums, grad_feed, grad_up_bias = feed_forward(
        heads_rows,
        tokens.reshape(3 * share, width),
        cotangent.reshape(3 * share, width),
        out_weight,
        out_full.reshape(3 * 256, width),
        [vector.reshape(1, width) for vector in (out_bias, ln2_gain, ln2_bias, down_bias)],
        up_weight,
        down_own,
        feed_full.reshape(8, 3, 256, width),
        up_bias_all,
    )
    block_out = block_out.reshape(tokens.shape)
    grad_feed = grad_feed.reshape(4, 2, 4, 256, width)
    grad_out = grad_out.reshape(4, 2, 4, 32, width)
    full, came, first, second = back(
        slots,
        d_heads,
        grad_feed,
        grad_out,
        qkv,
        normed_home,
        qkv_full,
        logs,
        tab,
        seg,
        live,
        grad_up_bias,
        sums,
        tokens,
        reparam_out,
    )
    input_grad = last_norm(
        came, tokens, d_resid.reshape(tokens.shape), ln1_gain.reshape(1, width)
    )
    grad_up, grad_down, grad_out, grad_qkv = write_grads(full)
    grad_up_bias = pick(first[:32].reshape(8, 4, 128).transpose(1, 0, 2).reshape(4, 1024), zed)
    ln2_gain_grad, ln2_bias_grad, out_bias_grad, down_bias_grad = first[32:64].reshape(4, width)
    table_own = first[64:320].reshape(2, 4, 2, 16, 2, HEAD_DIM)
    table_own = table_own[plane // 2, zed, core, :slots, plane % 2]
    grad_qkv_bias = pick(
        first[320:].reshape(2, 4, 8, 2, HEAD_DIM).transpose(1, 0, 3, 2, 4)[..., :3, :], zed
    ).reshape(768)
    grad_rout = jnp.dot(tanh_low.astype(f32).T, table_own, precision=HIGHEST)
    grad_rout_bias = jnp.sum(table_own, 0)
    tanh_sum = second[:64].reshape(4, 16, 128).transpose(1, 0, 2).reshape(16, 512)[:slots]
    ln1_gain_grad, ln1_bias_grad = second[64:].reshape(2, width)
    d_pre = tanh_sum * (1.0 - tanh_hidden * tanh_hidden)
    grad_rin = jnp.dot(prefix_embed.astype(f32).T, d_pre, precision=HIGHEST)
    grad_rin_bias = jnp.sum(d_pre, 0)
    grad_embed = jnp.dot(d_pre, reparam_in.astype(f32).T, precision=HIGHEST)
    return (
        block_out,
        input_grad,
        ln1_gain_grad,
        ln1_bias_grad,
        grad_qkv,
        grad_qkv_bias,
        grad_out,
        out_bias_grad,
        ln2_gain_grad,
        ln2_bias_grad,
        grad_up,
        grad_up_bias,
        grad_down,
        down_bias_grad,
        grad_embed,
        grad_rin,
        grad_rin_bias,
        grad_rout,
        grad_rout_bias,
    )


def specs(dp, mp):
    rows = P(None, dp + mp, None)
    ins = (
        rows, P(None, dp), P(None, dp), P(), P(), P(None, mp), P(mp), P(mp, None), P(), P(), P(),
        P(None, mp), P(mp), P(mp, None), P(), P(), P(), P(), P(None, mp + dp), P(mp + dp), rows,
    )
    outs = (
        rows, rows, P(), P(), P(None, mp), P(mp), P(mp, None), P(), P(), P(), P(None, mp), P(mp),
        P(mp, None), P(), P(), P(), P(), P(None, mp + dp), P(mp + dp),
    )
    return ins, outs


def solution(mesh):
    if mesh.shape["dp"] == 8 and mesh.shape["mp"] == 4:
        body = per_device_fast
        grid = jax.sharding.Mesh(mesh.devices.reshape(4, 2, 4), ALL)
        ins, outs = specs(("pl", "core"), ("mp",))
    else:
        body = per_device
        grid = mesh
        ins, outs = specs(("dp",), ("mp",))
    return jax.shard_map(body, mesh=grid, in_specs=ins, out_specs=outs, check_vma=False)
```

```python
import functools
import math

import jax
import jax.numpy as jnp
from jax import lax
from jax.experimental import pallas as pl
from jax.experimental.pallas import tpu as pltpu
from jax.sharding import PartitionSpec as P

HEAD_DIM = 64


EPSILON = 1e-05
MASKED = -1e30
HIGHEST = lax.Precision.HIGHEST


def normalize(inputs):
    average = jnp.mean(inputs, -1, keepdims=True)
    centered = inputs - average
    variance = jnp.mean(centered * centered, -1, keepdims=True)
    inverse = lax.rsqrt(variance + EPSILON)
    return (centered * inverse, inverse)


def norm_back(grad_norm, normed_hat, inverse, norm_gain):
    scaled = grad_norm * norm_gain
    return inverse * (
        scaled
        - jnp.mean(scaled, -1, keepdims=True)
        - normed_hat * jnp.mean(scaled * normed_hat, -1, keepdims=True)
    )


def product_transposed(rows_in, matrix):
    return lax.dot_general(
        rows_in, matrix, (((1,), (1,)), ((), ())), preferred_element_type=jnp.float32
    )


def outer_sum(left, right):
    return lax.dot_general(
        left, right, (((0,), (0,)), ((), ())), preferred_element_type=jnp.float32
    )


def gelu_tanh(values_in):
    return jax.nn.gelu(values_in, approximate=True)


def attention_scores(queries, keys_tok, keys_pre, visible, log_total):
    score_scale = 1.0 / math.sqrt(queries.shape[-1])
    scores_tok = (
        jnp.einsum("hqd,hkd->hqk", queries, keys_tok, preferred_element_type=jnp.float32)
        * score_scale
    )
    scores_tok = jnp.where(visible[None], scores_tok, MASKED)
    scores_pre = (
        jnp.einsum("hqd,hkd->hqk", queries, keys_pre, preferred_element_type=jnp.float32)
        * score_scale
    )
    if log_total is None:
        highest = jnp.maximum(
            jnp.max(scores_tok, -1, keepdims=True), jnp.max(scores_pre, -1, keepdims=True)
        )
        totals = jnp.sum(jnp.exp(scores_tok - highest), -1, keepdims=True) + jnp.sum(
            jnp.exp(scores_pre - highest), -1, keepdims=True
        )
        log_total = highest + jnp.log(totals)
    return (jnp.exp(scores_tok - log_total), jnp.exp(scores_pre - log_total), log_total)


def per_device(
    tokens,
    segment_ids,
    row_lengths,
    ln1_gain,
    ln1_bias,
    qkv_weight,
    qkv_bias,
    out_weight,
    out_bias,
    ln2_gain,
    ln2_bias,
    up_weight,
    up_bias,
    down_weight,
    down_bias,
    prefix_embed,
    reparam_in,
    reparam_in_bias,
    reparam_out,
    reparam_out_bias,
    cotangent,
):
    width_head = out_weight.shape[0]
    heads_local = width_head // HEAD_DIM
    prefix_slots = prefix_embed.shape[0]
    pre_act = (
        jnp.dot(prefix_embed, reparam_in, preferred_element_type=jnp.float32) + reparam_in_bias
    )
    tanh_hidden = jnp.tanh(pre_act)
    tanh_low = tanh_hidden.astype(jnp.bfloat16)
    table_part = (
        jnp.dot(tanh_low, reparam_out, preferred_element_type=jnp.float32) + reparam_out_bias
    ).astype(jnp.bfloat16)

    def micro_step(carried, inputs):
        big_sums, small_sums, table_grad = carried
        tokens_mb, segments_mb, length_mb, cotangent_mb = inputs
        table_full = lax.all_gather(table_part, "dp", axis=1, tiled=True)
        seq_len = segments_mb.shape[0]
        table_heads = table_full.reshape(prefix_slots, heads_local, 2, HEAD_DIM).transpose(
            2, 1, 0, 3
        )
        positions = jnp.arange(seq_len)
        visible = (
            (segments_mb[:, None] == segments_mb[None, :])
            & (positions[None, :] <= positions[:, None])
            & (positions[None, :] < length_mb)
        )
        x_share = tokens_mb.astype(jnp.float32)
        hat_first, inverse_first = normalize(x_share)
        normed_first = lax.all_gather(
            (hat_first * ln1_gain + ln1_bias).astype(jnp.bfloat16), "mp", axis=0, tiled=True
        )
        qkv_low = (
            jnp.dot(normed_first, qkv_weight, preferred_element_type=jnp.float32) + qkv_bias
        ).astype(jnp.bfloat16)
        packed = qkv_low.reshape(seq_len, heads_local, 3, HEAD_DIM).transpose(2, 1, 0, 3)
        weights_tok, weights_pre, log_total = attention_scores(
            packed[0], packed[1], table_heads[0], visible, None
        )
        heads_out = (
            jnp.einsum(
                "hqk,hkd->hqd",
                weights_tok.astype(jnp.bfloat16),
                packed[2],
                preferred_element_type=jnp.float32,
            )
            + jnp.einsum(
                "hqk,hkd->hqd",
                weights_pre.astype(jnp.bfloat16),
                table_heads[1],
                preferred_element_type=jnp.float32,
            )
        ).astype(jnp.bfloat16)
        head_rows = heads_out.transpose(1, 0, 2).reshape(seq_len, width_head)
        resid = (
            x_share
            + lax.psum_scatter(
                jnp.dot(head_rows, out_weight, preferred_element_type=jnp.float32).astype(
                    jnp.bfloat16
                ),
                "mp",
                scatter_dimension=0,
                tiled=True,
            ).astype(jnp.float32)
            + out_bias
        )
        hat_second, inverse_second = normalize(resid)
        normed_second = lax.all_gather(
            (hat_second * ln2_gain + ln2_bias).astype(jnp.bfloat16), "mp", axis=0, tiled=True
        )
        up_act = jnp.dot(normed_second, up_weight, preferred_element_type=jnp.float32) + up_bias
        gelu_out, gelu_back = jax.vjp(gelu_tanh, up_act)
        hidden_low = gelu_out.astype(jnp.bfloat16)
        block_share = (
            resid
            + lax.psum_scatter(
                jnp.dot(hidden_low, down_weight, preferred_element_type=jnp.float32).astype(
                    jnp.bfloat16
                ),
                "mp",
                scatter_dimension=0,
                tiled=True,
            ).astype(jnp.float32)
            + down_bias
        ).astype(jnp.bfloat16)
        cot_full = lax.all_gather(cotangent_mb, "mp", axis=0, tiled=True)
        d_up = gelu_back(product_transposed(cot_full, down_weight))[0].astype(jnp.bfloat16)
        grad_down = outer_sum(hidden_low, cot_full)
        grad_up = outer_sum(normed_second, d_up)
        grad_up_bias = jnp.sum(d_up.astype(jnp.float32), 0)
        d_second = lax.psum_scatter(
            product_transposed(d_up, up_weight).astype(jnp.bfloat16),
            "mp",
            scatter_dimension=0,
            tiled=True,
        ).astype(jnp.float32)
        cot_share = cotangent_mb.astype(jnp.float32)
        d_resid = cot_share + norm_back(d_second, hat_second, inverse_second, ln2_gain)
        d_attn = lax.all_gather(d_resid.astype(jnp.bfloat16), "mp", axis=0, tiled=True)
        grad_out = outer_sum(head_rows, d_attn)
        d_heads = (
            product_transposed(d_attn, out_weight)
            .astype(jnp.bfloat16)
            .reshape(seq_len, heads_local, HEAD_DIM)
            .transpose(1, 0, 2)
        )
        weights_tok, weights_pre, unused_total = attention_scores(
            packed[0], packed[1], table_heads[0], visible, log_total
        )
        score_scale = 1.0 / math.sqrt(HEAD_DIM)
        d_vtok = jnp.einsum(
            "hqk,hqd->hkd",
            weights_tok.astype(jnp.bfloat16),
            d_heads,
            preferred_element_type=jnp.float32,
        )
        d_vpre = jnp.einsum(
            "hqk,hqd->hkd",
            weights_pre.astype(jnp.bfloat16),
            d_heads,
            preferred_element_type=jnp.float32,
        )
        dprob_tok = jnp.einsum(
            "hqd,hkd->hqk", d_heads, packed[2], preferred_element_type=jnp.float32
        )
        dprob_pre = jnp.einsum(
            "hqd,hkd->hqk", d_heads, table_heads[1], preferred_element_type=jnp.float32
        )
        delta = jnp.sum(weights_tok * dprob_tok, -1, keepdims=True) + jnp.sum(
            weights_pre * dprob_pre, -1, keepdims=True
        )
        dscore_tok = (weights_tok * (dprob_tok - delta)).astype(jnp.bfloat16)
        dscore_pre = (weights_pre * (dprob_pre - delta)).astype(jnp.bfloat16)
        d_queries = (
            jnp.einsum("hqk,hkd->hqd", dscore_tok, packed[1], preferred_element_type=jnp.float32)
            + jnp.einsum(
                "hqk,hkd->hqd", dscore_pre, table_heads[0], preferred_element_type=jnp.float32
            )
        ) * score_scale
        d_ktok = (
            jnp.einsum("hqk,hqd->hkd", dscore_tok, packed[0], preferred_element_type=jnp.float32)
            * score_scale
        )
        d_kpre = (
            jnp.einsum("hqk,hqd->hkd", dscore_pre, packed[0], preferred_element_type=jnp.float32)
            * score_scale
        )
        prefix_add = (
            jnp.stack([d_kpre, d_vpre], 0)
            .transpose(2, 1, 0, 3)
            .reshape(prefix_slots, 2 * width_head)
        )
        d_qkv = (
            jnp.stack([d_queries, d_ktok, d_vtok], 0)
            .transpose(2, 1, 0, 3)
            .reshape(seq_len, 3 * width_head)
            .astype(jnp.bfloat16)
        )
        grad_qkv = outer_sum(normed_first, d_qkv)
        grad_qkv_bias = jnp.sum(d_qkv.astype(jnp.float32), 0)
        d_first = lax.psum_scatter(
            product_transposed(d_qkv, qkv_weight).astype(jnp.bfloat16),
            "mp",
            scatter_dimension=0,
            tiled=True,
        ).astype(jnp.float32)
        input_grad = d_resid + norm_back(d_first, hat_first, inverse_first, ln1_gain)
        small_add = (
            jnp.sum(d_first * hat_first, 0),
            jnp.sum(d_first, 0),
            jnp.sum(d_second * hat_second, 0),
            jnp.sum(d_second, 0),
            jnp.sum(d_resid, 0),
            jnp.sum(cot_share, 0),
        )
        big_add = (
            lax.psum(grad_qkv.astype(jnp.bfloat16), "dp").astype(jnp.float32),
            lax.psum(grad_qkv_bias.astype(jnp.bfloat16), "dp").astype(jnp.float32),
            lax.psum(grad_out.astype(jnp.bfloat16), "dp").astype(jnp.float32),
            lax.psum(grad_up.astype(jnp.bfloat16), "dp").astype(jnp.float32),
            lax.psum(grad_up_bias.astype(jnp.bfloat16), "dp").astype(jnp.float32),
            lax.psum(grad_down.astype(jnp.bfloat16), "dp").astype(jnp.float32),
        )
        big_sums = jax.tree.map(jnp.add, big_sums, tuple(big_add))
        small_sums = jax.tree.map(jnp.add, small_sums, small_add)
        return ((big_sums, small_sums, table_grad + prefix_add), (block_share, input_grad))

    big_zero = tuple(
        (
            jnp.zeros(member.shape, jnp.float32)
            for member in (qkv_weight, qkv_bias, out_weight, up_weight, up_bias, down_weight)
        )
    )
    small_zero = tuple((jnp.zeros(ln1_gain.shape, jnp.float32) for member in range(6)))
    table_zero = jnp.zeros((prefix_slots, 2 * width_head), jnp.float32)
    carried, stacked = lax.scan(
        micro_step,
        (big_zero, small_zero, table_zero),
        (tokens, segment_ids, row_lengths[:, 0], cotangent),
    )
    big_sums, small_sums, table_grad = carried
    block_out, input_grad = stacked
    table_own = lax.psum_scatter(table_grad, "dp", scatter_dimension=1, tiled=True)
    grad_rout = jnp.dot(tanh_low.astype(jnp.float32).T, table_own, precision=HIGHEST)
    grad_rout_bias = jnp.sum(table_own, 0)
    tanh_part = jnp.dot(table_own, reparam_out.astype(jnp.float32).T, precision=HIGHEST)
    shared = lax.psum(
        (
            tanh_part,
            small_sums[0],
            small_sums[1],
            small_sums[2],
            small_sums[3],
            small_sums[4],
            small_sums[5],
        ),
        ("dp", "mp"),
    )
    d_pre = shared[0] * (1.0 - tanh_hidden * tanh_hidden)
    grad_rin = jnp.dot(prefix_embed.astype(jnp.float32).T, d_pre, precision=HIGHEST)
    grad_rin_bias = jnp.sum(d_pre, 0)
    grad_embed = jnp.dot(d_pre, reparam_in.astype(jnp.float32).T, precision=HIGHEST)
    return (
        block_out,
        input_grad,
        shared[1],
        shared[2],
        big_sums[0],
        big_sums[1],
        big_sums[2],
        shared[5],
        shared[3],
        shared[4],
        big_sums[3],
        big_sums[4],
        big_sums[5],
        shared[6],
        grad_embed,
        grad_rin,
        grad_rin_bias,
        grad_rout,
        grad_rout_bias,
    )


ALL = ("pl", "core", "mp")
QB = 256
MICRO = 3


def nt(left, right):
    return lax.dot_general(
        left, right, (((1,), (1,)), ((), ())), preferred_element_type=jnp.float32
    )


def nn(left, right):
    return jnp.dot(left, right, preferred_element_type=jnp.float32)


def half_mask(value, head):
    lane = lax.broadcasted_iota(jnp.int32, value.shape, 1)
    keep = (lane < HEAD_DIM) if head == 0 else (lane >= HEAD_DIM)
    return jnp.where(keep, value, jnp.zeros_like(value))


GELU_A = math.sqrt(2.0 / math.pi)
GELU_B = 0.044715


def feed_kernel(
    heads_ref, tokens_ref, cot_ref, out_own_ref, out_ref, obias_ref, gain_ref, offset_ref, dbias_ref,
    own_up_ref, own_down_ref, weight_ref, bias_ref,
    block_ref, resid_ref, dheads_ref, gout_ref, sums_ref, grad_ref, gbias_ref,
    heads_s, normed_s, resid_s, mlp_s, dn_s,
):
    step = pl.program_id(0)
    blocks, near, cores, share, lanes = heads_ref.shape
    own_rows = out_own_ref.shape[0]
    out_bias, gain, offset, down_bias = obias_ref[...], gain_ref[...], offset_ref[...], dbias_ref[...]

    @pl.when(step == 0)
    def _before():
        for m in range(blocks):
            rows = slice(m * share, (m + 1) * share)
            heads = jnp.concatenate(
                [heads_ref[m, r, c] for r in range(near) for c in range(cores)], 1
            )
            heads_s[rows] = heads
            resid = (
                tokens_ref[rows].astype(jnp.float32)
                + nn(heads[:, :own_rows], out_own_ref[...])
                + nn(heads[:, own_rows:], out_ref[...])
                + out_bias
            )
            resid_s[rows] = resid
            hat, _ = normalize(resid)
            normed_s[rows] = (hat * gain + offset).astype(jnp.bfloat16)

    normed, cot = normed_s[...], cot_ref[...]
    groups, depth, width = grad_ref.shape[1:]
    half_rows = depth // 2
    units = (groups - 1) * half_rows
    up = jnp.concatenate(
        [jnp.transpose(own_up_ref[...]), weight_ref[0, :, :half_rows].reshape(units, width)], 0
    )
    down = jnp.concatenate(
        [own_down_ref[0], weight_ref[0, :, half_rows:].reshape(units, width)], 0
    )
    act = nt(normed, up) + bias_ref[0]
    square = act * act
    curve = jnp.tanh(GELU_A * act * (1.0 + GELU_B * square))
    half = 0.5 * (1.0 + curve)
    hidden = (act * half).astype(jnp.bfloat16)
    slope = half + 0.5 * act * (1.0 - curve * curve) * (
        GELU_A * (1.0 + (3.0 * GELU_B) * square)
    )
    d_act = nt(cot, down) * slope
    gbias_ref[0] = jnp.sum(d_act, 0, keepdims=True)
    d_low = d_act.astype(jnp.bfloat16)
    gup = outer_sum(d_low, normed).astype(jnp.bfloat16)
    gdown = outer_sum(hidden, cot).astype(jnp.bfloat16)
    grad_ref[0, :, :half_rows] = gup.reshape(groups, half_rows, width)
    grad_ref[0, :, half_rows:] = gdown.reshape(groups, half_rows, width)
    mlp, dn = nn(hidden, down), nn(d_low, up)

    @pl.when(step == 0)
    def _first():
        mlp_s[...] = mlp
        dn_s[...] = dn

    @pl.when(step > 0)
    def _later():
        mlp_s[...] += mlp
        dn_s[...] += dn

    @pl.when(step == pl.num_programs(0) - 1)
    def _after():
        sums = [jnp.zeros((1, width), jnp.float32) for _ in range(4)]
        for m in range(blocks):
            rows = slice(m * share, (m + 1) * share)
            resid, d_second = resid_s[rows], dn_s[rows]
            block_ref[rows] = (resid + mlp_s[rows] + down_bias).astype(jnp.bfloat16)
            hat, inverse = normalize(resid)
            cot_wide = cot_ref[rows].astype(jnp.float32)
            d_resid = cot_wide + norm_back(d_second, hat, inverse, gain)
            resid_ref[rows] = d_resid
            for j, value in enumerate((d_second * hat, d_second, d_resid, cot_wide)):
                sums[j] = sums[j] + jnp.sum(value, 0, keepdims=True)
            d_attn = d_resid.astype(jnp.bfloat16)
            normed_s[rows] = d_attn
            d_own = nt(d_attn, out_own_ref[...]).astype(jnp.bfloat16)
            d_rest = nt(d_attn, out_ref[...]).astype(jnp.bfloat16)
            for r in range(near):
                for c in range(cores):
                    source = d_rest if r else d_own
                    at = (2 * r + c) * lanes - (own_rows if r else 0)
                    dheads_ref[m, r, c] = source[:, at : at + lanes]
        for j in range(4):
            sums_ref[j : j + 1] = sums[j]
        for j in range(near):
            columns = slice(j * own_rows, (j + 1) * own_rows)
            gout_ref[columns] = outer_sum(heads_s[:, columns], normed_s[...]).astype(jnp.bfloat16)


def feed_forward(heads, tokens, cot, out_own, out, vectors, own_up, own_down, weights, bias):
    rows, width = tokens.shape
    tiles, others, depth, _ = weights.shape
    groups = others + 1
    units = groups * depth // 2
    once = pl.Buffered(1)

    def whole(shape):
        return pl.BlockSpec(shape, lambda i: (0,) * len(shape), pipeline_mode=once)

    shaped, bf16, f32 = jax.ShapeDtypeStruct, jnp.bfloat16, jnp.float32
    line = pl.BlockSpec((1, 1, units), lambda i: (i, 0, 0))
    square = (rows, width)
    return pl.pallas_call(
        feed_kernel,
        grid=(tiles,),
        in_specs=[
            whole(heads.shape),
            whole(square),
            whole(square),
            whole(out_own.shape),
            whole(out.shape),
            *[whole((1, width))] * 4,
            pl.BlockSpec((width, depth // 2), lambda i: (0, i)),
            pl.BlockSpec((1, depth // 2, width), lambda i: (i, 0, 0)),
            pl.BlockSpec((1, others, depth, width), lambda i: (i, 0, 0, 0)),
            line,
        ],
        out_specs=[
            whole(square),
            whole(square),
            whole(heads.shape),
            whole((width, width)),
            whole((4, width)),
            pl.BlockSpec((1, groups, depth, width), lambda i: (i, 0, 0, 0)),
            line,
        ],
        out_shape=[
            shaped(square, bf16),
            shaped(square, f32),
            shaped(heads.shape, bf16),
            shaped((width, width), bf16),
            shaped((4, width), f32),
            shaped((tiles, groups, depth, width), bf16),
            shaped((tiles, 1, units), f32),
        ],
        scratch_shapes=[
            pltpu.VMEM(square, bf16),
            pltpu.VMEM(square, bf16),
            pltpu.VMEM(square, f32),
            pltpu.VMEM(square, f32),
            pltpu.VMEM(square, f32),
        ],
        compiler_params=pltpu.CompilerParams(vmem_limit_bytes=62 << 20),
        cost_estimate=pl.CostEstimate(
            flops=12 * rows * width * tiles * units, bytes_accessed=60_000_000,
            transcendentals=rows * tiles * units,
        ),
        name="feed_forward",
    )(heads, tokens, cot, out_own, out, *vectors, own_up, own_down, weights, bias)


MESH_IDS = pl.DeviceIdType.MESH


def position():
    return lax.axis_index("pl"), lax.axis_index("core"), lax.axis_index("mp")


def plane_at(plane, offset):
    across, down = lax.rem(plane, 2), lax.div(plane, 2)
    if offset & 1:
        across = 1 - across
    if offset & 2:
        down = 1 - down
    return 2 * down + across


def greet(partners):
    barrier = pltpu.get_barrier_semaphore()
    for partner in partners:
        pl.semaphore_signal(barrier, inc=1, device_id=partner, device_id_type=MESH_IDS)
    pl.semaphore_wait(barrier, len(partners))


def column_partners():
    plane, core, zed = position()
    found = [(plane, core, lax.rem(zed + step, 4)) for step in range(1, 4)]
    return found + [(plane, 1 - core, lax.rem(zed + step, 4)) for step in range(4)]


def plane_partners():
    plane, core, zed = position()
    return [(plane_at(plane, offset), core, zed) for offset in range(1, 4)]


class Wires:
    def __init__(self, sends, recvs):
        self.sends, self.recvs, self.out = sends, recvs, []

    def copy(self, source, target, slot, device):
        return pltpu.make_async_remote_copy(
            src_ref=source,
            dst_ref=target,
            send_sem=self.sends.at[slot],
            recv_sem=self.recvs.at[slot],
            device_id=device,
            device_id_type=MESH_IDS,
        )

    def put(self, source, target, slot, device):
        copy = self.copy(source, target, slot, device)
        copy.start()
        self.out.append((copy, None))

    def put_unless(self, own, source, target, slot, device):
        copy = self.copy(source, target, slot, device)

        @pl.when(own)
        def _here():
            pltpu.make_async_copy(source, target, self.recvs.at[slot]).start()

        @pl.when(jnp.logical_not(own))
        def _there():
            copy.start()

        self.out.append((copy, own))

    def put_if(self, valid, source, target, slot, device):
        copy = self.copy(source, target, slot, device)
        pl.when(valid)(copy.start)
        self.out.append((copy, jnp.logical_not(valid)))

    def got(self, target, slot, device):
        self.copy(target, target, slot, device).wait_recv()

    def got_if(self, valid, target, slot, device):
        pl.when(valid)(self.copy(target, target, slot, device).wait_recv)

    def wait_sent(self, puts):
        gone = [id(put) for put in puts]
        self.out = [put for put in self.out if id(put) not in gone]
        for copy, own in puts:
            if own is None:
                copy.wait_send()
            else:
                pl.when(jnp.logical_not(own))(copy.wait_send)

    def finish(self):
        self.wait_sent(list(self.out))


ANYWHERE = pl.BlockSpec(memory_space=pl.ANY)


def visible_to(seg_col, seg_row, block):
    keys = (block + 1) * QB
    lanes = seg_row[:, block * QB : keys]
    cols = seg_col[:keys, :]
    same = jnp.concatenate([cols, cols], 1) == lanes
    rows = lax.broadcasted_iota(jnp.int32, (keys, QB), 0)
    places = lax.broadcasted_iota(jnp.int32, (keys, QB), 1) + block * QB
    return same & (rows <= places)


def forward_pair(slots, qkv, keys_pre, values_pre, seg_row, seg_col, heads, logs):
    seq = qkv.shape[0]
    keys = qkv[:, 128:256]
    values_t = jnp.transpose(qkv[:, 256:384])
    values_pre_t = jnp.transpose(values_pre)
    pre_row = lax.broadcasted_iota(jnp.int32, (keys_pre.shape[0], QB), 0)
    for block in range(seq // QB):
        extent = (block + 1) * QB
        here = slice(block * QB, extent)
        visible = visible_to(seg_col, seg_row, block)
        queries = qkv[here, :128] * 0.125
        parts = []
        for head in range(2):
            rows = slice(head * HEAD_DIM, (head + 1) * HEAD_DIM)
            query = half_mask(queries, head)
            s_tok = jnp.where(visible, nt(keys[:extent], query), MASKED)
            s_pre = jnp.where(pre_row < slots, nt(keys_pre, query), MASKED)
            top = jnp.maximum(
                jnp.max(s_tok, 0, keepdims=True), jnp.max(s_pre, 0, keepdims=True)
            )
            p_tok, p_pre = jnp.exp(s_tok - top), jnp.exp(s_pre - top)
            total = jnp.sum(p_tok, 0, keepdims=True) + jnp.sum(p_pre, 0, keepdims=True)
            mixed = nn(values_t[rows, :extent], p_tok.astype(jnp.bfloat16)) + nn(
                values_pre_t[rows], p_pre.astype(jnp.bfloat16)
            )
            parts.append(mixed * (1.0 / total))
            logs[head : head + 1, here] = top + jnp.log(total)
        heads[here, :] = jnp.transpose(jnp.concatenate(parts, 0)).astype(jnp.bfloat16)


PAIRS = 6


def front_kernel(
    slots,
    normed_ref, qkv_ref, bias_ref, table_ref, ids_ref, own_ref,
    rows_out, weight_out, qkv_out, heads_out, feed_out, proj_out,
    log_out, tab_out, seg_out, live_out, bias_out,
    sends, recvs, local,
    rows_v, weight_v, qkv_v, heads_v, log_v, biases_v, tables_v, ids_v, other_v, col_v, feed_v,
):
    plane, core, zed = position()
    parity = lax.rem(zed, 2)
    mine = 2 * parity + core
    origin = lax.div(zed, 2)
    sibling = (plane, 1 - core, zed)
    share = normed_ref.shape[1]
    seq = 4 * share
    around = [(plane_at(plane, offset), core, zed) for offset in range(4)]
    ahead = [lax.rem(zed + step, 4) for step in range(4)]
    greet(column_partners() + plane_partners())
    wires = Wires(sends, recvs)
    slot_at = {}

    def slot(*name):
        return slot_at.setdefault(name, len(slot_at))

    width = qkv_ref.shape[0] // 4

    def strip(at):
        return pl.ds(pl.multiple_of(at * width, 32), width)

    def rolled(z_from, z_at):
        return lax.rem(z_from + 2 * lax.rem(z_at, 2), 4)

    def apart(z_of, z_at):
        return lax.rem(z_of - z_at + 4, 4)

    own_copies = [
        pltpu.make_async_copy(qkv_ref, weight_v.at[rolled(zed, zed)], local.at[0]),
        pltpu.make_async_copy(bias_ref, biases_v.at[zed], local.at[1]),
        pltpu.make_async_copy(table_ref, tables_v.at[plane, core, zed], local.at[2]),
        pltpu.make_async_copy(ids_ref, ids_v, local.at[3]),
    ]
    for copy in own_copies:
        copy.start()
    wires.put(ids_ref, other_v, slot("ids"), sibling)

    sides = (1, -1)
    hops = [(sign, hop) for hop in range(1, 4) for sign in sides]

    def owner(sign, hop):
        at = zed - sign * hop
        return lax.rem(at + 4, 4), jnp.logical_and(at >= 0, at <= 3)

    def next_along(sign):
        at = zed + sign
        return lax.rem(at + 4, 4), jnp.logical_and(at >= 0, at <= 3)

    def early_parts(z_of, z_at):
        return (
            weight_v.at[rolled(z_of, z_at), strip(plane)],
            biases_v.at[z_of],
            tables_v.at[plane, core, z_of],
        )

    def late_part(at, core_at, z_of, z_at):
        return feed_v.at[at, core_at, apart(z_of, z_at) - 1]

    total = own_ref.shape[0]
    part_rows = feed_out.shape[3] // 2
    halves = (pl.ds(0, total // 2), pl.ds(total // 2, total // 2))
    routes = ((1, 2), (2, 1))

    def half_strip(at, half):
        return pl.ds(pl.multiple_of(at * width + half * (width // 2), 16), width // 2)

    def send_early(sign, hop):
        z_of, there_is = owner(sign, hop - 1)
        z_to, can = next_along(sign)
        valid = jnp.logical_and(there_is, can)
        sources, targets = early_parts(z_of, zed), early_parts(z_of, z_to)
        for kind in range(3):
            wires.put_if(
                valid, sources[kind], targets[kind], slot("e", sign, hop, kind), (plane, core, z_to)
            )

    def send_late(sign, hop):
        z_of, there_is = owner(sign, hop - 1)
        z_to, can = next_along(sign)
        valid = jnp.logical_and(there_is, can)
        source = own_ref if hop == 1 else late_part(plane, core, z_of, zed)
        wires.put_if(
            valid, source, late_part(plane, core, z_of, z_to), slot("l", sign, hop), (plane, core, z_to)
        )

    def take_early(sign, hop):
        z_of, valid = owner(sign, hop)
        back = (plane, core, lax.rem(zed + 4 - sign, 4))
        for kind, part in enumerate(early_parts(z_of, zed)):
            wires.got_if(valid, part, slot("e", sign, hop, kind), back)
        if hop < 3:
            send_early(sign, hop + 1)
        for half in range(2):
            part = weight_v.at[rolled(z_of, zed), half_strip(plane, half)]
            for offset in routes[half]:
                wires.put_if(valid, part, part, slot("ep", sign, hop, half, offset), around[offset])

    def early_across(sign, hop):
        z_of, valid = owner(sign, hop)
        for half, (came, goes) in enumerate(routes):
            part = weight_v.at[rolled(z_of, zed), half_strip(plane_at(plane, came), half)]
            wires.got_if(valid, part, slot("ep", sign, hop, half, came), around[came])
            wires.put_if(valid, part, part, slot("ep", sign, hop, half, 3), around[goes])

    def early_end(sign, hop):
        z_of, valid = owner(sign, hop)
        for half, (came, goes) in enumerate(routes):
            for offset, over in ((goes, goes), (3, goes)):
                part = weight_v.at[rolled(z_of, zed), half_strip(plane_at(plane, offset), half)]
                wires.got_if(valid, part, slot("ep", sign, hop, half, offset), around[over])

    def take_late(sign, hop):
        z_of, valid = owner(sign, hop)
        part = late_part(plane, core, z_of, zed)
        wires.got_if(valid, part, slot("l", sign, hop), (plane, core, lax.rem(zed + 4 - sign, 4)))
        if hop < 3:
            send_late(sign, hop + 1)
        for half in range(2):
            piece = part.at[halves[half]]
            for offset in routes[half]:
                wires.put_if(
                    valid, piece, piece, slot("lp", sign, hop, half, offset), around[offset]
                )
        wires.put_if(valid, part, part, slot("ls", sign, hop, 0), sibling)

    def take_across(sign, hop):
        z_of, valid = owner(sign, hop)
        for half, (came, goes) in enumerate(routes):
            piece = late_part(plane_at(plane, came), core, z_of, zed).at[halves[half]]
            wires.got_if(valid, piece, slot("lp", sign, hop, half, came), around[came])
            wires.put_if(valid, piece, piece, slot("lp", sign, hop, half, 3), around[goes])
        for half, (_, other) in enumerate(routes):
            piece = late_part(plane_at(plane, other), core, z_of, zed).at[halves[half]]
            wires.got_if(valid, piece, slot("lp", sign, hop, half, other), around[other])
        for offset in (1, 2):
            part = late_part(plane_at(plane, offset), core, z_of, zed)
            wires.put_if(valid, part, part, slot("ls", sign, hop, offset), sibling)

    def take_far(sign, hop):
        z_of, valid = owner(sign, hop)
        part = late_part(plane_at(plane, 3), core, z_of, zed)
        for half, (_, goes) in enumerate(routes):
            wires.got_if(
                valid, part.at[halves[half]], slot("lp", sign, hop, half, 3), around[goes]
            )
        wires.put_if(valid, part, part, slot("ls", sign, hop, 3), sibling)

    def end_across(sign, hop):
        z_of, valid = owner(sign, hop)
        for offset in range(4):
            part = late_part(plane_at(plane, offset), 1 - core, z_of, zed)
            wires.got_if(valid, part, slot("ls", sign, hop, offset), sibling)

    for copy in own_copies:
        copy.wait()
    for sign in sides:
        send_early(sign, 1)
    first_far = slot("nb", 0)
    slot("nb", 1)
    first_row = slot("n", 0)
    for step in range(1, 4):
        slot("n", step)
    outside = lax.div(zed, 2) != core
    near_home = jnp.logical_or(zed == 1, zed == 2)
    far_z = zed + 1 - 2 * parity
    first_over = slot("f", 0)
    for step in range(1, 4):
        slot("f", step)

    def send_rows(kind):
        for half in range(2):
            k = 2 * half + kind
            z_to = 2 * core + half
            own = jnp.logical_and(core == kind, z_to == zed)
            source, target = normed_ref.at[1 if kind else k], rows_v.at[kind, zed]
            number = first_row + lax.rem(k + 4 - zed, 4)

            @pl.when(own)
            def _here():
                pltpu.make_async_copy(source, target, recvs.at[number]).start()

            goes = jnp.logical_not(own)
            if kind:
                far_to = jnp.logical_or(z_to == 0, z_to == 3)
                goes = jnp.logical_and(goes, jnp.logical_not(jnp.logical_and(outside, far_to)))
            wires.put_if(goes, source, target, number, (plane, kind, z_to))

    def pass_rows(kind):
        here = core == kind
        for step in range(4):
            z_from = lax.rem(2 * parity + kind + 4 - step, 4)
            block = rows_v.at[kind, z_from]
            if kind:
                from_outside = jnp.logical_and(here, lax.div(z_from, 2) != origin)
                via = jnp.logical_and(from_outside, jnp.logical_not(near_home))
                far_number = first_far + lax.rem(z_from, 2)
                wires.got_if(via, block, far_number, sibling)
                wires.got_if(
                    jnp.logical_and(here, jnp.logical_not(via)), block, first_row + step, sibling
                )
                wires.put_if(
                    jnp.logical_and(from_outside, near_home),
                    block,
                    block,
                    far_number,
                    (plane, core, far_z),
                )
            else:
                wires.got_if(here, block, first_row + step, sibling)
            wires.put_if(here, block, block, first_over + step, sibling)

    def rows_passed(kind):
        for step in range(4):
            z_from = lax.rem(2 * parity + kind + 4 - step, 4)
            wires.got_if(core != kind, rows_v.at[kind, z_from], first_over + step, sibling)

    send_rows(0)
    for sign in sides:
        send_late(sign, 1)
    for hop in range(1, 4):
        for sign in sides:
            take_early(sign, hop)
    for sign in sides:
        take_late(sign, 1)
    for sign, hop in hops:
        early_across(sign, hop)
    pass_rows(0)
    send_rows(1)
    for offset in range(1, 4):
        wires.put(
            tables_v.at[plane, core], tables_v.at[plane, core], slot("tp", offset), around[offset]
        )
    for offset in range(1, 4):
        wires.got(tables_v.at[plane_at(plane, offset), core], slot("tp", offset), around[offset])
    wires.put(tables_v.at[:, core], tables_v.at[:, core], slot("ts"), sibling)

    wires.got(other_v, slot("ids"), sibling)
    wires.got(tables_v.at[:, 1 - core], slot("ts"), sibling)
    for row in range(2):
        at = 1 if row else 2 * parity
        here = jnp.where(origin == core, ids_v[at], other_v[at])
        seg = here[:, :seq]
        length = jnp.concatenate([here[:, seq:]] * (seq // 128), 1)
        live = (lax.broadcasted_iota(jnp.int32, (1, seq), 1) < length).astype(jnp.int32)
        seg_out[row] = seg
        live_out[row] = live
        line = jnp.where(live > 0, seg, -1).astype(jnp.float32)
        col_v[row] = jnp.transpose(jnp.broadcast_to(line, (128, seq)))
    for at in range(8):
        for step in range(4):
            bias_out[at, step : step + 1] = biases_v[ahead[step], 2, at : at + 1]
    for at in range(4):
        z_at = rolled(at, zed)
        for s in range(2):
            tab_out[at, :, 128 * s : 128 * s + 128] = jnp.concatenate(
                [tables_v[2 * core + t, s, z_at][:, :HEAD_DIM] for t in range(2)], 1
            )

    for sign, hop in hops:
        early_end(sign, hop)
    rows_passed(0)
    keep = [
        pltpu.make_async_copy(weight_v, weight_out, local.at[5]),
        pltpu.make_async_copy(rows_v, rows_out, local.at[4]),
    ]
    keep[0].start()

    def heads_copy(pair, step):
        z_to = lax.rem(mine + 4 - step, 4)
        own = jnp.logical_and(origin == core, z_to == zed)
        tokens = pl.ds(pl.multiple_of(z_to * share, share), share)
        on_b = lax.div(pair, 4)
        row = on_b + (1 - on_b) * 2 * parity
        target = heads_out.at[row, apart(rolled(lax.rem(pair, 4), zed), z_to), core]
        return own, heads_v.at[pair, tokens], target, (plane, origin, z_to)

    first_heads = slot("h", 0)
    for number in range(1, 4 * PAIRS):
        slot("h", number)

    def attend(pair):
        row, at = lax.div(pair, 4), lax.rem(pair, 4)
        z_at = rolled(at, zed)
        bias = jnp.concatenate([biases_v[z_at, core, j : j + 1] for j in range(3)], 1)
        for quarter in range(4):
            part = nt(rows_v[row, quarter], weight_v[at]) + bias
            qkv_v[pair, quarter * share : (quarter + 1) * share] = part.astype(jnp.bfloat16)
        forward_pair(
            slots,
            qkv_v.at[pair],
            tab_out[at, :, :128],
            tab_out[at, :, 128:],
            seg_out[row].astype(jnp.float32),
            col_v.at[row],
            heads_v.at[pair],
            log_v.at[pair],
        )
        for step in range(4):
            own, source, target, there = heads_copy(pair, step)
            number = first_heads + 4 * pair + step
            copy = wires.copy(source, target, number, there)

            @pl.when(own)
            def _here():
                pltpu.make_async_copy(source, target, recvs.at[number]).start()

            @pl.when(jnp.logical_not(own))
            def _there():
                copy.start()

    pl.loop(0, 2)(attend)
    for sign in sides:
        take_late(sign, 2)
    for sign in sides:
        take_across(sign, 1)
    pass_rows(1)
    pl.loop(2, 4)(attend)
    for sign in sides:
        take_late(sign, 3)
    for sign in sides:
        take_across(sign, 2)
    for sign in sides:
        take_far(sign, 1)
    rows_passed(1)
    keep[1].start()
    pl.loop(4, PAIRS)(attend)
    for sign in sides:
        take_across(sign, 3)
    for sign in sides:
        take_far(sign, 2)
    keep.append(pltpu.make_async_copy(qkv_v, qkv_out, local.at[6]))
    keep[-1].start()
    log_out[...] = log_v[...]
    for sign in sides:
        take_far(sign, 3)
    for at in range(2):
        if at:
            for sign, hop in hops:
                end_across(sign, hop)
        side = core if at == 0 else 1 - core
        keep.append(
            pltpu.make_async_copy(
                feed_v.at[:, side, :, : 2 * part_rows], feed_out.at[:, side], local.at[7 + at]
            )
        )
        keep[-1].start()
        for quarter in range(4):
            keep.append(
                pltpu.make_async_copy(
                    feed_v.at[quarter, side, :, 2 * part_rows :],
                    proj_out.at[:, side, quarter],
                    local.at[9 + 4 * at + quarter],
                )
            )
            keep[-1].start()
    for pair in range(PAIRS):
        for k in range(4):
            half, c = k // 2, k % 2
            step = lax.rem(k + 4 - zed, 4)
            row = 1 if pair >= 4 else 2 * half
            target = heads_out.at[row, apart((pair % 4 + 2 * half) % 4, zed), c]
            wires.got(target, first_heads + 4 * pair + step, (plane, c, 2 * core + half))
        for step in range(4):
            own, source, target, there = heads_copy(pair, step)
            copy = wires.copy(source, target, first_heads + 4 * pair + step, there)
            pl.when(jnp.logical_not(own))(copy.wait_send)
    for copy in keep:
        copy.wait()
    wires.finish()
    assert len(slot_at) == FRONT_COPIES, len(slot_at)


FRONT_COPIES = 159


def front(slots, normed, qkv, bias, table, ids, own):
    bf16, f32 = jnp.bfloat16, jnp.float32
    _, share, width = normed.shape
    seq = 4 * share
    vmem = pl.BlockSpec(memory_space=pltpu.VMEM)
    shaped = jax.ShapeDtypeStruct
    return pl.pallas_call(
        functools.partial(front_kernel, slots),
        in_specs=[ANYWHERE] * 6,
        out_specs=[ANYWHERE] * 6 + [vmem] * 5,
        out_shape=[
            shaped((2, 4, share, width), bf16),
            shaped((4, 384, width), bf16),
            shaped((PAIRS, seq, 384), bf16),
            shaped((3, 4, 2, share, 128), bf16),
            shaped((4, 2, 3, 256, width), bf16),
            shaped((3, 2, 4, 32, width), bf16),
            shaped((PAIRS, 2, seq), f32),
            shaped((4, 16, 256), bf16),
            shaped((2, 1, seq), jnp.int32),
            shaped((2, 1, seq), jnp.int32),
            shaped((8, 4, 128), f32),
        ],
        scratch_shapes=[
            pltpu.SemaphoreType.DMA((FRONT_COPIES,)),
            pltpu.SemaphoreType.DMA((FRONT_COPIES,)),
            pltpu.SemaphoreType.DMA((17,)),
            pltpu.VMEM((2, 4, share, width), bf16),
            pltpu.VMEM((4, 384, width), bf16),
            pltpu.VMEM((PAIRS, seq, 384), bf16),
            pltpu.VMEM((PAIRS, seq, 128), bf16),
            pltpu.VMEM((PAIRS, 2, seq), f32),
            pltpu.VMEM((4, 3, 8, 128), f32),
            pltpu.VMEM((4, 2, 4, 16, 128), bf16),
            pltpu.VMEM(ids.shape, jnp.int32),
            pltpu.VMEM(ids.shape, jnp.int32),
            pltpu.VMEM((2, seq, 128), f32),
            pltpu.VMEM((4, 2, 3, own.shape[0], width), bf16),
        ],
        compiler_params=pltpu.CompilerParams(
            collective_id=0, has_side_effects=True, vmem_limit_bytes=48 << 20
        ),
        cost_estimate=pl.CostEstimate(
            flops=40_000_000_000, bytes_accessed=60 << 20, transcendentals=8_000_000
        ),
        name="front",
    )(normed, qkv, bias, table, ids, own)


def backward_pair(
    slots, qkv, keys_pre, values_pre, seg_row, seg_col, grads_in, logs, dtab, dbias, dk_acc, dv_acc
):
    seq = qkv.shape[0]
    keys, values = qkv[:, 128:256], qkv[:, 256:384]
    keys_t = jnp.transpose(keys)
    keys_pre_t = jnp.transpose(keys_pre)
    pre_row = lax.broadcasted_iota(jnp.int32, (keys_pre.shape[0], QB), 0)
    zero = jnp.zeros((keys_pre.shape[0], 128), jnp.float32)
    dtab_k, dtab_v, dq_sum = zero, zero, jnp.zeros((1, 128), jnp.float32)
    for block in reversed(range(seq // QB)):
        extent = (block + 1) * QB
        here = slice(block * QB, extent)
        visible = visible_to(seg_col, seg_row, block)
        queries = qkv[here, :128] * 0.125
        grads = grads_in[here, :]
        weights, dscores, weights_pre, dscores_pre, query_halves, grad_halves, dq_parts = (
            [], [], [], [], [], [], [],
        )
        for head in range(2):
            rows = slice(head * HEAD_DIM, (head + 1) * HEAD_DIM)
            query, grad = half_mask(queries, head), half_mask(grads, head)
            log_total = logs[head : head + 1, here]
            s_tok = jnp.where(visible, nt(keys[:extent], query), MASKED)
            s_pre = jnp.where(pre_row < slots, nt(keys_pre, query), MASKED)
            w_tok, w_pre = jnp.exp(s_tok - log_total), jnp.exp(s_pre - log_total)
            dp_tok, dp_pre = nt(values[:extent], grad), nt(values_pre, grad)
            delta = jnp.sum(w_tok * dp_tok, 0, keepdims=True) + jnp.sum(
                w_pre * dp_pre, 0, keepdims=True
            )
            ds_tok = (w_tok * (dp_tok - delta)).astype(jnp.bfloat16)
            ds_pre = (w_pre * (dp_pre - delta)).astype(jnp.bfloat16)
            dq_parts.append(nn(keys_t[rows, :extent], ds_tok) + nn(keys_pre_t[rows], ds_pre))
            weights.append(w_tok.astype(jnp.bfloat16))
            weights_pre.append(w_pre.astype(jnp.bfloat16))
            dscores.append(ds_tok)
            dscores_pre.append(ds_pre)
            query_halves.append(query)
            grad_halves.append(grad)
        query_both = jnp.concatenate(query_halves, 0)
        grad_both = jnp.concatenate(grad_halves, 0)
        dv = nn(jnp.concatenate(weights, 1), grad_both)
        dk = nn(jnp.concatenate(dscores, 1), query_both)
        if block == seq // QB - 1:
            dv_acc[...] = dv
            dk_acc[...] = dk
        else:
            dv_acc[:extent] += dv
            dk_acc[:extent] += dk
        dtab_v = dtab_v + nn(jnp.concatenate(weights_pre, 1), grad_both)
        dtab_k = dtab_k + nn(jnp.concatenate(dscores_pre, 1), query_both)
        dq = jnp.transpose(jnp.concatenate(dq_parts, 0)) * 0.125
        dq_sum = dq_sum + jnp.sum(dq, 0, keepdims=True)
        qkv[here, :128] = dq.astype(jnp.bfloat16)
    dk, dv = dk_acc[...], dv_acc[...]
    qkv[:, 128:256] = dk.astype(jnp.bfloat16)
    qkv[:, 256:384] = dv.astype(jnp.bfloat16)
    dbias[...] = jnp.concatenate(
        [dq_sum, jnp.sum(dk, 0, keepdims=True), jnp.sum(dv, 0, keepdims=True)], 1
    )
    dtab[:, :128] = dtab_k
    dtab[:, 128:] = dtab_v


def add_up(rows, target, *sources):
    chunk = 96 if rows % 96 == 0 else 64

    @pl.loop(0, rows // chunk)
    def _add(at):
        span = pl.ds(pl.multiple_of(at * chunk, 32), chunk)
        if len(sources) == 2:
            target[span] = sources[0][span] + sources[1][span]
            return
        value = sources[0][span].astype(jnp.float32)
        for source in sources[1:]:
            value = value + source[span].astype(jnp.float32)
        target[span] = value.astype(jnp.bfloat16)


def back_kernel(
    slots,
    heads_ref, feed_ref, proj_ref, qkv_ref, rows_ref, weight_ref,
    log_ref, tab_ref, seg_ref, live_ref, upb_ref, norms_ref, tokens_ref, rout_ref,
    full_out, back_out, first_out, second_out,
    sends, recvs, local,
    dh_v, sib_v, own_v, plane_v, sum_v, z_v, gq_v, plane_q, sum_q, z_q, done_v,
    qkv_v, weight_v, df_v, dfs_v, col_v, dk_acc, dv_acc,
    dtab_v, dbias_v, back_v, first_v, first_in, second_v, second_in, dfm_v,
):
    plane, core, zed = position()
    parity = lax.rem(zed, 2)
    mine = 2 * parity + core
    origin = lax.div(zed, 2)
    sibling = (plane, 1 - core, zed)
    share = heads_ref.shape[3]
    seq = 4 * share
    feed_rows, proj_rows = feed_ref.shape[3], proj_ref.shape[3]
    both = feed_rows + proj_rows
    q_rows = gq_v.shape[2]
    around = [(plane_at(plane, offset), core, zed) for offset in range(4)]
    ahead = [lax.rem(zed + step, 4) for step in range(4)]
    greet(column_partners() + plane_partners())
    wires = Wires(sends, recvs)
    slot_at = {}

    def slot(*name):
        return slot_at.setdefault(name, len(slot_at))

    tokens = pl.ds(pl.multiple_of(zed * share, share), share)
    first_heads = slot("h", 0)
    for number in range(1, 4 * PAIRS):
        slot("h", number)
    for pair in range(PAIRS):
        for step in range(4):
            k = ahead[step]
            half, c = lax.div(k, 2), lax.rem(k, 2)
            z_to = 2 * core + half
            own = jnp.logical_and(c == core, z_to == zed)
            row = 1 if pair >= 4 else 2 * half
            wires.put_unless(
                own,
                heads_ref.at[row, lax.rem(pair % 4 + 2 * half + 4 - zed, 4), c],
                dh_v.at[pair, tokens],
                first_heads + 4 * pair + step,
                (plane, c, z_to),
            )
    turns = [lax.rem(zed + 1 + turn, 4) for turn in range(4)]
    own_copies = []
    for turn in range(4):
        z_at = (turn + 1) % 4
        wires.put(
            feed_ref.at[:, 1 - core, z_at], sib_v.at[turn, :, :feed_rows], slot("s", turn), sibling
        )
        wires.put(
            proj_ref.at[z_at, 1 - core], sib_v.at[turn, :, feed_rows:], slot("sp", turn), sibling
        )
        own_copies.append(
            [
                pltpu.make_async_copy(
                    feed_ref.at[:, core, z_at],
                    own_v.at[turn % 2, :, :feed_rows],
                    local.at[2 * (turn % 2)],
                ),
                pltpu.make_async_copy(
                    proj_ref.at[z_at, core],
                    own_v.at[turn % 2, :, feed_rows:],
                    local.at[2 * (turn % 2) + 1],
                ),
            ]
        )
    later = [
        pltpu.make_async_copy(qkv_ref, qkv_v, local.at[4]),
        pltpu.make_async_copy(weight_ref, weight_v, local.at[5]),
    ]
    for copy in own_copies[0] + own_copies[1] + later:
        copy.start()
    for row in range(2):
        line = jnp.where(live_ref[row] > 0, seg_ref[row], -1).astype(jnp.float32)
        col_v[row] = jnp.transpose(jnp.broadcast_to(line, (128, seq)))

    def chip_sum(turn):
        for copy in own_copies[turn]:
            copy.wait()
        wires.got(sib_v.at[turn, :, :feed_rows], slot("s", turn), sibling)
        wires.got(sib_v.at[turn, :, feed_rows:], slot("sp", turn), sibling)
        for at in range(4):
            add_up(both, sib_v.at[turn, at], sib_v.at[turn, at], own_v.at[turn % 2, at])
        if turn < 2:
            for copy in own_copies[turn + 2]:
                copy.start()
        first, _ = axes(turn)
        for kind, offset in enumerate((3, first)):
            wires.put(
                sib_v.at[turn, plane_at(plane, offset)],
                plane_v.at[kind, turn],
                slot("p", turn, kind),
                around[first],
            )

    def axes(turn):
        return (1, 2) if turn % 2 else (2, 1)

    def merge(turn):
        first, other = axes(turn)
        wires.got(plane_v.at[0, turn], slot("p", turn, 0), around[first])
        target = sib_v.at[turn, plane_at(plane, other)]
        add_up(both, target, target, plane_v.at[0, turn])
        wires.put(target, plane_v.at[2, turn], slot("p", turn, 2), around[other])

    chip_sum(0)
    chip_sum(1)
    for copy in later:
        copy.wait()

    def heads_here(pairs):
        for pair in pairs:
            for step in range(4):
                z_from = lax.rem(mine + 4 - step, 4)
                there = pl.ds(pl.multiple_of(z_from * share, share), share)
                wires.got(dh_v.at[pair, there], first_heads + 4 * pair + step, sibling)

    def attend(pair):
        row, at = lax.div(pair, 4), lax.rem(pair, 4)
        backward_pair(
            slots,
            qkv_v.at[pair],
            tab_ref[at, :, :128],
            tab_ref[at, :, 128:],
            seg_ref[row].astype(jnp.float32),
            col_v.at[row],
            dh_v.at[pair],
            log_ref.at[pair],
            dtab_v.at[pair],
            dbias_v.at[pair],
            dk_acc,
            dv_acc,
        )

    def plane_sum(turn):
        for kind, offset in zip((1, 2), axes(turn)):
            wires.got(plane_v.at[kind, turn], slot("p", turn, kind), around[offset])
        add_up(
            both, sum_v.at[turn], sib_v.at[turn, plane], *[plane_v.at[j, turn] for j in (1, 2)]
        )
        if turn < 3:
            wires.put(
                sum_v.at[turn], z_v.at[turn], slot("z", turn), (plane, core, turns[turn])
            )

    low = lax.rem(zed, 2)
    partners = [
        sibling, around[1], around[2],
        (plane, core, zed + 1 - 2 * low), (plane, core, ahead[2]),
    ]

    def small_send(name, values, arrived, step):
        source = arrived.at[step - 1] if step else values.at[0]
        wires.put(source, arrived.at[step], slot(name, step), partners[step])

    def small_take(name, values, arrived, step):
        wires.got(arrived.at[step], slot(name, step), partners[step])
        arrived[step] = arrived[step] + (arrived[step - 1] if step else values[0])
        if step < 4:
            small_send(name, values, arrived, step + 1)

    half_rows = first_v.shape[1] // 2
    mine_rows = pl.ds(pl.multiple_of(core * half_rows, 8), half_rows)
    other_rows = pl.ds(pl.multiple_of((1 - core) * half_rows, 8), half_rows)

    def first_take(step):
        if step == 5:
            wires.got(first_in.at[4, other_rows], slot("a", 5), sibling)
            return
        here = first_in.at[step, mine_rows]
        wires.got(here, slot("a", step), partners[step])
        before = first_in[step - 1, mine_rows] if step else first_v[0, mine_rows]
        first_in[step, mine_rows] = first_in[step, mine_rows] + before
        at, there = (step + 1, partners[step + 1]) if step < 4 else (4, sibling)
        wires.put(here, first_in.at[at, mine_rows], slot("a", step + 1), there)

    def first_sums():
        first_v[0] = jnp.zeros(first_v.shape[1:], jnp.float32)
        for at in range(8):
            for step in range(4):
                line = upb_ref[at, :, 128 * step : 128 * step + 128]
                first_v[0, pl.ds(4 * at + ahead[step], 1)] = line
        for at in range(4):
            for j in range(8):
                line = norms_ref[at : at + 1, 128 * j : 128 * j + 128]
                first_v[0, 32 + 8 * at + j : 33 + 8 * at + j] = line
        for at in range(4):
            entry = core * 4 + lax.rem(at + 2 * parity, 4)
            table, bias = dtab_v[at], dbias_v[at]
            if at < 2:
                table, bias = table + dtab_v[4 + at], bias + dbias_v[4 + at]
            base = pl.multiple_of(64 + 32 * entry, 8)
            first_v[0, pl.ds(base, 16)] = table[:, :128]
            first_v[0, pl.ds(base + 16, 16)] = table[:, 128:]
            base = pl.multiple_of(320 + 8 * entry, 8)
            first_v[0, pl.ds(base, 8)] = jnp.concatenate(
                [bias[:, :128], bias[:, 128:256], bias[:, 256:], jnp.zeros((5, 128), jnp.float32)], 0
            )
        wires.put(first_v.at[0, other_rows], first_in.at[0, other_rows], slot("a", 0), sibling)

    def tanh_part():
        entry = lax.div(plane, 2) * 4 + zed
        base = pl.multiple_of(64 + 32 * entry + 16 * core, 8)
        table = first_in[4, pl.ds(base, 16)]
        table = jnp.where(lax.rem(plane, 2) == 0, table[:, :HEAD_DIM], table[:, HEAD_DIM:])
        part = lax.dot_general(
            table,
            rout_ref[...].astype(jnp.float32),
            (((1,), (1,)), ((), ())),
            preferred_element_type=jnp.float32,
            precision=HIGHEST,
        )
        for j in range(4):
            second_v[0, 16 * j : 16 * j + 16] = part[:, 128 * j : 128 * j + 128]

    def norm_sums():
        span_rows = 64

        def body(at, sums):
            row, part = lax.div(at, share // span_rows), lax.rem(at, share // span_rows)
            span = pl.ds(pl.multiple_of(part * span_rows, span_rows), span_rows)
            grad = back_v[row, span].astype(jnp.float32)
            extra = back_v[3, span].astype(jnp.float32)
            grad = grad + jnp.where(row == 1, extra, 0.0)
            hat, _ = normalize(tokens_ref[row, span].astype(jnp.float32))
            return (
                sums[0] + jnp.sum(grad * hat, 0, keepdims=True),
                sums[1] + jnp.sum(grad, 0, keepdims=True),
            )

        zero = jnp.zeros((1, back_v.shape[2]), jnp.float32)
        sums = lax.fori_loop(0, 3 * (share // span_rows), body, (zero, zero))
        for kind in range(2):
            for j in range(8):
                at = 64 + 8 * kind + j
                second_v[0, at : at + 1] = sums[kind][:, 128 * j : 128 * j + 128]
        small_send("b", second_v, second_in, 0)

    first_row = slot("r", 0)
    for number in range(1, 4):
        slot("r", number)

    far_home = jnp.logical_or(zed == 0, zed == 3)
    other_home = zed + 1 - 2 * parity
    outside = lax.div(zed, 2) != core
    far_place = 1 + 2 * core

    @pl.when(outside)
    def _nothing():
        back_v[far_place] = jnp.zeros(back_v.shape[1:], jnp.bfloat16)

    def row_grads(kind):
        for quarter in range(4):
            span = slice(quarter * share, (quarter + 1) * share)
            parts = [
                nn(qkv_v[4 * kind + at, span], weight_v[at]) for at in range(2 if kind else 4)
            ]
            total = parts[0] + parts[1]
            for part in parts[2:]:
                total = total + part
            df_v[kind, quarter] = total.astype(jnp.bfloat16)
            wires.put_if(
                core != kind, df_v.at[kind, quarter], dfs_v.at[quarter], slot("df", quarter, kind),
                sibling,
            )

    def send_rows(kind):
        here = core == kind
        for quarter in range(4):
            wires.got_if(here, dfs_v.at[quarter], slot("df", quarter, kind), sibling)

            @pl.when(here)
            def _sum():
                add_up(share, dfs_v.at[quarter], dfs_v.at[quarter], df_v.at[kind, quarter])

        if kind:
            for j in range(2):
                z_out = 2 - 2 * origin + j
                wires.put_if(
                    jnp.logical_and(here, far_home), dfs_v.at[z_out], dfm_v.at[j], slot("m", j),
                    (plane, core, other_home),
                )
                joins = jnp.logical_and(here, jnp.logical_not(far_home))
                wires.got_if(joins, dfm_v.at[j], slot("m", j), (plane, core, other_home))

                @pl.when(joins)
                def _join():
                    add_up(share, dfs_v.at[z_out], dfs_v.at[z_out], dfm_v.at[j])

        for step in range(4):
            z_to = lax.rem(2 * parity + kind + 4 - step, 4)
            own = jnp.logical_and(origin == core, z_to == zed)
            goes = here
            if kind:
                beyond = jnp.logical_and(far_home, lax.div(z_to, 2) != origin)
                goes = jnp.logical_and(here, jnp.logical_not(beyond))
            source, target = dfs_v.at[z_to], back_v.at[2 * parity + kind]

            @pl.when(jnp.logical_and(here, own))
            def _here():
                pltpu.make_async_copy(source, target, recvs.at[first_row + step]).start()

            wires.put_if(
                jnp.logical_and(goes, jnp.logical_not(own)),
                source,
                target,
                first_row + step,
                (plane, origin, z_to),
            )

    heads_here((0, 1))
    pl.loop(0, 2)(attend)
    chip_sum(2)
    merge(0)
    heads_here((2, 3))
    pl.loop(2, 4)(attend)
    chip_sum(3)
    merge(1)
    rows_v = own_v
    row_copy = pltpu.make_async_copy(rows_ref, rows_v.at[:, :, :share], local.at[0])
    row_copy.start()
    plane_sum(0)
    row_grads(0)
    merge(2)
    heads_here((4, 5))
    pl.loop(4, PAIRS)(attend)
    merge(3)
    plane_sum(1)
    first_sums()
    send_rows(0)
    row_grads(1)
    plane_sum(2)
    first_take(0)
    row_copy.wait()
    rows_a = jnp.concatenate([rows_v[0, j, :share] for j in range(4)], 0)
    for at in range(4):
        grad = outer_sum(qkv_v[at], rows_a)
        if at < 2:
            grad = grad + outer_sum(
                qkv_v[4 + at], jnp.concatenate([rows_v[1, j, :share] for j in range(4)], 0)
            )
        grad = grad.astype(jnp.bfloat16)
        for j in range(4):
            gq_v[at, j] = grad[j * q_rows : (j + 1) * q_rows]
        if at % 2:
            sub = at // 2
            slots_here = slice(at - 1, at + 1)
            first, _ = axes(sub)
            for kind, offset in enumerate((3, first)):
                wires.put(
                    gq_v.at[slots_here, plane_at(plane, offset)],
                    plane_q.at[kind, slots_here],
                    slot("pq", sub, kind),
                    around[first],
                )
    first_take(1)
    send_rows(1)
    plane_sum(3)
    first_take(2)
    for sub in range(2):
        first, other = axes(sub)
        slots_here = slice(2 * sub, 2 * sub + 2)
        wires.got(plane_q.at[0, slots_here], slot("pq", sub, 0), around[first])
        at_other = plane_at(plane, other)
        for at in (2 * sub, 2 * sub + 1):
            target = gq_v.at[at, at_other]
            add_up(q_rows, target, target, plane_q.at[0, at])
        wires.put(
            gq_v.at[slots_here, at_other], plane_q.at[2, slots_here], slot("pq", sub, 2), around[other]
        )
    first_take(3)

    def spread(name, span_of):
        copy = pltpu.make_async_copy(
            done_v.at[span_of(2)],
            full_out.at[plane, core, span_of(2)],
            local.at[6 if name == "f" else 7],
        )
        copy.start()
        for half in range(2):
            for offset in (1, 2) if half == 0 else (2, 1):
                wires.put(
                    done_v.at[span_of(half)],
                    full_out.at[plane, core, span_of(half)],
                    slot(name, half, offset),
                    around[offset],
                )
        wires.put(
            done_v.at[span_of(2)], full_out.at[plane, core, span_of(2)], slot(name, 2, 0), sibling
        )
        return copy

    def spread_on(name, span_of):
        for half in range(2):
            came, goes = (1, 2) if half == 0 else (2, 1)
            piece = full_out.at[plane_at(plane, came), core, span_of(half)]
            wires.got(piece, slot(name, half, came), around[came])
            wires.put(piece, piece, slot(name, half, 3), around[goes])
        for half in range(2):
            came = 2 if half == 0 else 1
            piece = full_out.at[plane_at(plane, came), core, span_of(half)]
            wires.got(piece, slot(name, half, came), around[came])
        for offset in (1, 2):
            piece = full_out.at[plane_at(plane, offset), core, span_of(2)]
            wires.put(piece, piece, slot(name, 2, offset), sibling)

    def spread_far(name, span_of):
        for half in range(2):
            piece = full_out.at[plane_at(plane, 3), core, span_of(half)]
            wires.got(piece, slot(name, half, 3), around[2 if half == 0 else 1])
        piece = full_out.at[plane_at(plane, 3), core, span_of(2)]
        wires.put(piece, piece, slot(name, 2, 3), sibling)

    def spread_end(name, span_of):
        for offset in range(4):
            wires.got(
                full_out.at[plane_at(plane, offset), 1 - core, span_of(2)],
                slot(name, 2, offset),
                sibling,
            )

    def feed_span(half):
        return (pl.ds(0, both // 2), pl.ds(both // 2, both // 2), pl.ds(0, both))[half]

    def q_span(half):
        return (
            pl.ds(both, q_rows // 2), pl.ds(both + q_rows // 2, q_rows // 2), pl.ds(both, q_rows)
        )[half]

    for turn in range(3):
        wires.got(z_v.at[turn], slot("z", turn), (plane, core, lax.rem(zed + 3 - turn, 4)))
    add_up(both, done_v.at[feed_span(2)], sum_v.at[3], *[z_v.at[j] for j in range(3)])
    last = [spread("f", feed_span)]
    first_take(4)
    for sub in range(2):
        slots_here = slice(2 * sub, 2 * sub + 2)
        for kind, offset in zip((1, 2), axes(sub)):
            wires.got(plane_q.at[kind, slots_here], slot("pq", sub, kind), around[offset])
        for at in (2 * sub, 2 * sub + 1):
            add_up(q_rows, sum_q.at[at], gq_v.at[at, plane], *[plane_q.at[j, at] for j in (1, 2)])
    for turn in range(3):
        wires.put(
            sum_q.at[lax.rem(turns[turn] + 2 * parity, 4)],
            z_q.at[turn],
            slot("zq", turn),
            (plane, core, turns[turn]),
        )
    first_take(5)
    tanh_part()
    spread_on("f", feed_span)
    for k in range(4):
        wires.got_if(
            jnp.logical_not(jnp.logical_and(outside, far_place == k)),
            back_v.at[k],
            first_row + lax.rem(k + 4 - zed, 4),
            (plane, k % 2, 2 * core + k // 2),
        )
    last.append(pltpu.make_async_copy(back_v, back_out, local.at[8]))
    last[-1].start()
    norm_sums()
    for turn in range(3):
        wires.got(z_q.at[turn], slot("zq", turn), (plane, core, lax.rem(zed + 3 - turn, 4)))
    add_up(
        q_rows,
        done_v.at[q_span(2)],
        sum_q.at[lax.rem(zed + 2 * parity, 4)],
        *[z_q.at[j] for j in range(3)],
    )
    last.append(spread("q", q_span))
    small_take("b", second_v, second_in, 0)
    spread_far("f", feed_span)
    small_take("b", second_v, second_in, 1)
    spread_on("q", q_span)
    small_take("b", second_v, second_in, 2)
    spread_far("q", q_span)
    small_take("b", second_v, second_in, 3)
    small_take("b", second_v, second_in, 4)
    first_out[...] = first_in[4]
    second_out[...] = second_in[4]
    spread_end("f", feed_span)
    spread_end("q", q_span)
    for copy in last:
        copy.wait()
    wires.finish()
    assert len(slot_at) == BACK_COPIES, len(slot_at)


BACK_COPIES = 101


def back(
    slots, d_heads, grad_feed, grad_out, qkv, rows, weights, logs, tab, seg, live, upb, norms, tokens, rout
):
    bf16, f32 = jnp.bfloat16, jnp.float32
    share, width = rows.shape[2:]
    seq = 4 * share
    vmem = pl.BlockSpec(memory_space=pltpu.VMEM)
    shaped, held = jax.ShapeDtypeStruct, pltpu.VMEM
    both, q_rows = grad_feed.shape[3] + grad_out.shape[3], 96
    return pl.pallas_call(
        functools.partial(back_kernel, slots),
        in_specs=[ANYWHERE] * 6 + [vmem] * 8,
        out_specs=[ANYWHERE] * 2 + [vmem] * 2,
        out_shape=[
            shaped((4, 2, both + q_rows, width), bf16),
            shaped((4, share, width), bf16),
            shaped((384, 128), f32),
            shaped((80, 128), f32),
        ],
        scratch_shapes=[
            pltpu.SemaphoreType.DMA((BACK_COPIES,)),
            pltpu.SemaphoreType.DMA((BACK_COPIES,)),
            pltpu.SemaphoreType.DMA((9,)),
            held((PAIRS, seq, 128), bf16),
            held((4, 4, both, width), bf16),
            held((2, 4, both, width), bf16),
            held((3, 4, both, width), bf16),
            held((4, both, width), bf16),
            held((3, both, width), bf16),
            held((4, 4, q_rows, width), bf16),
            held((3, 4, q_rows, width), bf16),
            held((4, q_rows, width), bf16),
            held((3, q_rows, width), bf16),
            held((both + q_rows, width), bf16),
            held((PAIRS, seq, 384), bf16),
            held((4, 384, width), bf16),
            held((2, 4, share, width), bf16),
            held((4, share, width), bf16),
            held((2, seq, 128), f32),
            held((seq, 128), f32),
            held((seq, 128), f32),
            held((PAIRS, 16, 256), f32),
            held((PAIRS, 1, 384), f32),
            held((4, share, width), bf16),
            held((1, 384, 128), f32),
            held((5, 384, 128), f32),
            held((1, 80, 128), f32),
            held((5, 80, 128), f32),
            held((2, share, width), bf16),
        ],
        compiler_params=pltpu.CompilerParams(
            collective_id=2, has_side_effects=True, vmem_limit_bytes=62 << 20
        ),
        cost_estimate=pl.CostEstimate(
            flops=80_000_000_000, bytes_accessed=60 << 20, transcendentals=8_000_000
        ),
        name="back",
    )(
        d_heads, grad_feed, grad_out, qkv, rows, weights, logs, tab, seg, live, upb, norms, tokens, rout
    )


def write_feed_kernel(piece_ref, up_ref, down_ref):
    for c in range(2):
        span = slice(128 * c, 128 * c + 128)
        up_ref[:, span] = jnp.transpose(piece_ref[0, c, :128].astype(jnp.float32))
        down_ref[span] = piece_ref[0, c, 128:].astype(jnp.float32)


def write_rest_kernel(piece_ref, grad_ref, out_ref):
    for at in range(4):
        out_ref[32 * at : 32 * at + 32] = piece_ref[at, 0, :32].astype(jnp.float32)
    turned = [jnp.transpose(piece_ref[at, 0, 32:].astype(jnp.float32)) for at in range(4)]
    turned = jnp.concatenate(turned, 1)
    order = [(kind, head) for head in range(2) for kind in range(3)]
    grad_ref[...] = jnp.concatenate(
        [turned[:, 128 * kind + 64 * head : 128 * kind + 64 * head + 64] for kind, head in order], 1
    )


def last_kernel(came_ref, tokens_ref, resid_ref, gain_ref, grad_ref):
    row = pl.program_id(0)
    grad = came_ref[row].astype(jnp.float32) + jnp.where(
        row == 1, came_ref[3].astype(jnp.float32), 0.0
    )
    hat, inverse = normalize(tokens_ref[0].astype(jnp.float32))
    grad_ref[0] = resid_ref[0] + norm_back(grad, hat, inverse, gain_ref[...])


def last_norm(came, tokens, d_resid, gain):
    rows = pl.BlockSpec((1, *tokens.shape[1:]), lambda m: (m, 0, 0))
    return pl.pallas_call(
        last_kernel,
        grid=(tokens.shape[0],),
        in_specs=[
            pl.BlockSpec(came.shape, lambda m: (0, 0, 0)),
            rows,
            rows,
            pl.BlockSpec((1, tokens.shape[2]), lambda m: (0, 0)),
        ],
        out_specs=rows,
        out_shape=jax.ShapeDtypeStruct(tokens.shape, jnp.float32),
        compiler_params=pltpu.CompilerParams(vmem_limit_bytes=32 << 20),
        name="last_norm",
    )(came, tokens, d_resid, gain)


def write_grads(full):
    f32 = jnp.float32
    width = full.shape[3]
    up, down = pl.pallas_call(
        write_feed_kernel,
        grid=(4,),
        in_specs=[pl.BlockSpec((1, 2, 256, width), lambda p: (p, 0, 0, 0))],
        out_specs=[
            pl.BlockSpec((width, 256), lambda p: (0, p)),
            pl.BlockSpec((256, width), lambda p: (p, 0)),
        ],
        out_shape=[
            jax.ShapeDtypeStruct((width, 1024), f32),
            jax.ShapeDtypeStruct((1024, width), f32),
        ],
        name="write_feed",
    )(full)
    qkv, out = pl.pallas_call(
        write_rest_kernel,
        grid=(2,),
        in_specs=[pl.BlockSpec((4, 1, 128, width), lambda c: (0, c, 2, 0))],
        out_specs=[
            pl.BlockSpec((width, 384), lambda c: (0, c)),
            pl.BlockSpec((128, width), lambda c: (c, 0)),
        ],
        out_shape=[
            jax.ShapeDtypeStruct((width, 768), f32),
            jax.ShapeDtypeStruct((256, width), f32),
        ],
        compiler_params=pltpu.CompilerParams(vmem_limit_bytes=40 << 20),
        name="write_rest",
    )(full)
    return up, down, out, qkv


def per_device_fast(
    tokens,
    segment_ids,
    row_lengths,
    ln1_gain,
    ln1_bias,
    qkv_weight,
    qkv_bias,
    out_weight,
    out_bias,
    ln2_gain,
    ln2_bias,
    up_weight,
    up_bias,
    down_weight,
    down_bias,
    prefix_embed,
    reparam_in,
    reparam_in_bias,
    reparam_out,
    reparam_out_bias,
    cotangent,
):
    bf16, f32 = jnp.bfloat16, jnp.float32
    plane, core, zed = lax.axis_index("pl"), lax.axis_index("core"), lax.axis_index("mp")
    micro, share, width = tokens.shape
    seq = segment_ids.shape[1]
    slots = prefix_embed.shape[0]

    def pick(stack, index):
        return lax.dynamic_index_in_dim(stack, index, 0, keepdims=False)

    pre_act = nn(prefix_embed, reparam_in) + reparam_in_bias
    tanh_hidden = jnp.tanh(pre_act)
    tanh_low = tanh_hidden.astype(bf16)
    table_part = (nn(tanh_low, reparam_out) + reparam_out_bias).astype(bf16)
    table_part = jnp.pad(table_part, ((0, 16 - slots), (0, 128 - HEAD_DIM)))
    packed_ids = jnp.concatenate(
        [segment_ids, jnp.broadcast_to(row_lengths[:, :1], (micro, 128))], 1
    )
    packed_ids = jnp.pad(packed_ids, ((0, 8 - micro), (0, 0)))[:, None]
    packed_bias = jnp.concatenate(
        [
            jnp.pad(
                qkv_bias.reshape(2, 2, 3, HEAD_DIM).transpose(0, 2, 1, 3).reshape(2, 3, 128),
                ((0, 0), (0, 5), (0, 0)),
            ),
            up_bias.reshape(1, 8, 128),
        ]
    )
    x_share = tokens.astype(f32)
    hat_first, inverse_first = normalize(x_share)
    normed_first = (hat_first * ln1_gain + ln1_bias).astype(bf16)
    qkv_half = lax.dynamic_index_in_dim(
        qkv_weight.reshape(width, 2, 2, 3, HEAD_DIM), core, 1, keepdims=False
    )
    qkv_half = qkv_half.transpose(2, 1, 3, 0).reshape(384, width)
    down_own = down_weight.reshape(8, 128, width)
    (
        normed_home, qkv_full, qkv, heads_rows, feed_full, out_full, logs, tab, seg, live, biases
    ) = front(
        slots,
        normed_first,
        qkv_half,
        packed_bias,
        table_part,
        packed_ids,
        jnp.concatenate(
            [
                lax.dynamic_slice_in_dim(up_weight, (2 * plane + core) * 128, 128, 1).T,
                pick(down_own, 2 * plane + core),
                lax.dynamic_slice_in_dim(out_weight, core * 128 + plane * 32, 32, 0),
            ]
        ),
    )
    up_bias_all = biases.reshape(8, 1, 512)
    block_out, d_resid, d_heads, grad_out, sums, grad_feed, grad_up_bias = feed_forward(
        heads_rows,
        tokens.reshape(3 * share, width),
        cotangent.reshape(3 * share, width),
        out_weight,
        out_full.reshape(3 * 256, width),
        [vector.reshape(1, width) for vector in (out_bias, ln2_gain, ln2_bias, down_bias)],
        up_weight,
        down_own,
        feed_full.reshape(8, 3, 256, width),
        up_bias_all,
    )
    block_out = block_out.reshape(tokens.shape)
    grad_feed = grad_feed.reshape(4, 2, 4, 256, width)
    grad_out = grad_out.reshape(4, 2, 4, 32, width)
    full, came, first, second = back(
        slots,
        d_heads,
        grad_feed,
        grad_out,
        qkv,
        normed_home,
        qkv_full,
        logs,
        tab,
        seg,
        live,
        grad_up_bias,
        sums,
        tokens,
        reparam_out,
    )
    input_grad = last_norm(
        came, tokens, d_resid.reshape(tokens.shape), ln1_gain.reshape(1, width)
    )
    grad_up, grad_down, grad_out, grad_qkv = write_grads(full)
    grad_up_bias = pick(first[:32].reshape(8, 4, 128).transpose(1, 0, 2).reshape(4, 1024), zed)
    ln2_gain_grad, ln2_bias_grad, out_bias_grad, down_bias_grad = first[32:64].reshape(4, width)
    table_own = first[64:320].reshape(2, 4, 2, 16, 2, HEAD_DIM)
    table_own = table_own[plane // 2, zed, core, :slots, plane % 2]
    grad_qkv_bias = pick(
        first[320:].reshape(2, 4, 8, 2, HEAD_DIM).transpose(1, 0, 3, 2, 4)[..., :3, :], zed
    ).reshape(768)
    grad_rout = jnp.dot(tanh_low.astype(f32).T, table_own, precision=HIGHEST)
    grad_rout_bias = jnp.sum(table_own, 0)
    tanh_sum = second[:64].reshape(4, 16, 128).transpose(1, 0, 2).reshape(16, 512)[:slots]
    ln1_gain_grad, ln1_bias_grad = second[64:].reshape(2, width)
    d_pre = tanh_sum * (1.0 - tanh_hidden * tanh_hidden)
    grad_rin = jnp.dot(prefix_embed.astype(f32).T, d_pre, precision=HIGHEST)
    grad_rin_bias = jnp.sum(d_pre, 0)
    grad_embed = jnp.dot(d_pre, reparam_in.astype(f32).T, precision=HIGHEST)
    return (
        block_out,
        input_grad,
        ln1_gain_grad,
        ln1_bias_grad,
        grad_qkv,
        grad_qkv_bias,
        grad_out,
        out_bias_grad,
        ln2_gain_grad,
        ln2_bias_grad,
        grad_up,
        grad_up_bias,
        grad_down,
        down_bias_grad,
        grad_embed,
        grad_rin,
        grad_rin_bias,
        grad_rout,
        grad_rout_bias,
    )


def specs(dp, mp):
    rows = P(None, dp + mp, None)
    ins = (
        rows, P(None, dp), P(None, dp), P(), P(), P(None, mp), P(mp), P(mp, None), P(), P(), P(),
        P(None, mp), P(mp), P(mp, None), P(), P(), P(), P(), P(None, mp + dp), P(mp + dp), rows,
    )
    outs = (
        rows, rows, P(), P(), P(None, mp), P(mp), P(mp, None), P(), P(), P(), P(None, mp), P(mp),
        P(mp, None), P(), P(), P(), P(), P(None, mp + dp), P(mp + dp),
    )
    return ins, outs


def solution(mesh):
    if mesh.shape["dp"] == 8 and mesh.shape["mp"] == 4:
        body = per_device_fast
        grid = jax.sharding.Mesh(mesh.devices.reshape(4, 2, 4), ALL)
        ins, outs = specs(("pl", "core"), ("mp",))
    else:
        body = per_device
        grid = mesh
        ins, outs = specs(("dp",), ("mp",))
    return jax.shard_map(body, mesh=grid, in_specs=ins, out_specs=outs, check_vma=False)
```
